512 devices in a mesh: fsdp: 32 (over x, y, z_hi), head: 16 (over z_lo, core).
Axes of the slice: x: 4, y: 4, z: 16 (z_hi: 2, z_lo: 8; z = z_hi * 8 + z_lo), core: 2. Of those that a mesh axis runs over, the one named last changes fastest.
Arguments:
- query_latent: bfloat16 [512, 1536], P('fsdp'), may hold values from -6 to 6
- query_rope: bfloat16 [512, 128, 64], P('fsdp', 'head')
- lengths: int32 [512], replicated, may hold values from 256 to 2048, as said below
- kv_cache: bfloat16 [16384, 576], P('fsdp')
- w_uq: bfloat16 [128, 1536, 128], P('head', 'fsdp'), may hold values from -0.15625 to 0.15625
- w_uk: bfloat16 [128, 512, 128], P('head', 'fsdp'), may hold values from -0.5 to 0.5
- w_uv: bfloat16 [128, 512, 128], P('head', 'fsdp'), may hold values from -0.25 to 0.25
- w_out: bfloat16 [128, 128, 7168], P('head', 'fsdp'), may hold values from -0.5 to 0.5
Outputs:
- attended: bfloat16 [512, 7168], P('fsdp', 'head')
The draws below stay inside these ranges and needn't reach their ends.
Inputs may be any that keep to these rules, and one draw needn't show every extreme that they name: `lengths`: every sequence has a row that sees its whole cache and a row that sees only 256 tokens.
All inputs are finite; a program needn't handle non-finite values.
Results may differ from the reference program's by a relative error of at most 0.025.
Values may be sent and summed in bfloat16 or wider, within the bound.
No kernel may reach another device: no remote copies, remote signals or barrier semaphores. Data moves between devices by JAX's collectives and lax.ppermute only.
A program may use at most 64 MiB of HBM per device.

```python
import math
import jax
import jax.numpy as jnp
from jax import lax

D = 7168
HEADS = 128
QRANK = 1536
LATENT = 512
ROPE = 64
NOPE = 128
VDIM = 128
QROWS = 64
CLEN = 2048
SEQS = 8
ROWS = 512


def rope_keys(key):
    return jax.random.normal(key, (SEQS * CLEN, ROPE), jnp.float32)


def draw_kv_cache(key, part):
    keys_rope = rope_keys(key)
    key = jax.random.fold_in(key, 11)
    latent = jax.random.normal(key, (SEQS * CLEN, LATENT), jnp.float32)
    return jnp.concatenate([latent, keys_rope], axis=1).astype(jnp.bfloat16)


def draw_query_rope(key, part):
    key = jax.random.fold_in(key, 12)
    values = jax.random.normal(key, (ROWS, HEADS, ROPE), jnp.float32)
    return values.astype(jnp.bfloat16)


def draw_lengths(key, part):
    key = jax.random.fold_in(key, 13)
    drawn = jax.random.randint(key, (SEQS, QROWS), CLEN // 8, CLEN + 1)
    drawn = drawn.at[:, 0].set(CLEN).at[:, 1].set(CLEN // 8)
    return drawn.reshape(-1).astype(jnp.int32)


def level_of(rng, dims, cuts, least, largest):
    loudness = 1.0
    for position, shards_of in cuts:
        draws = jax.random.uniform(jax.random.fold_in(jax.random.fold_in(rng, 6), position), (shards_of,), jnp.float32, least / len(cuts), largest / len(cuts))
        loudness = loudness * jnp.repeat(jnp.exp(draws), dims[position] // shards_of).reshape((-1,) + (1,) * (len(dims) - 1 - position))
    return loudness


def normal_values(stream_key, extent, deviation, most, pieces=(), held_as=jnp.bfloat16):
    values = deviation * jax.random.normal(stream_key, extent, jnp.float32)
    if pieces:
        values = values * level_of(stream_key, extent, pieces, -0.22, 0.18)
    return jnp.clip(values, -most, most).astype(held_as)


def setup_inputs(seed: int = 0) -> dict:
    splits = jax.random.split(jax.random.key(seed), 9)
    return {
        "query_latent": normal_values(splits[0], (ROWS, QRANK), 1.0, 6.0, ((0, 32),)),
        "query_rope": draw_query_rope(jax.random.fold_in(splits[8], 71), 0),
        "lengths": draw_lengths(jax.random.fold_in(splits[8], 71), 0),
        "kv_cache": draw_kv_cache(jax.random.fold_in(splits[8], 71), 0),
        "w_uq": normal_values(splits[4], (HEADS, QRANK, NOPE), QRANK ** -0.5, 0.15625, ((0, 16), (1, 32))),
        "w_uk": normal_values(splits[5], (HEADS, LATENT, NOPE), NOPE ** -0.5, 0.5, ((0, 16), (1, 32))),
        "w_uv": normal_values(splits[6], (HEADS, LATENT, VDIM), LATENT ** -0.5, 0.25, ((0, 16), (1, 32))),
        "w_out": normal_values(splits[7], (HEADS, VDIM, D), VDIM ** -0.5, 0.5, ((0, 16), (1, 32))),
    }


def reference(query_latent, query_rope, lengths, kv_cache, w_uq, w_uk, w_uv, w_out):
    temper = 1.0 / math.sqrt(NOPE + ROPE)
    caches = kv_cache.reshape(SEQS, CLEN, LATENT + ROPE).astype(jnp.float32)
    visible = jnp.arange(CLEN)[None, None, :] < lengths.reshape(SEQS, QROWS)[:, :, None]
    rope_heads = jnp.transpose(query_rope, (1, 0, 2))

    def one_head(total, items):
        up_query, up_key, up_value, out_proj, rope_part = items
        query_absorb = jnp.dot(up_query, up_key.T, preferred_element_type=jnp.float32).astype(jnp.bfloat16)
        out_absorb = jnp.dot(up_value, out_proj, preferred_element_type=jnp.float32).astype(jnp.bfloat16)
        query_lat = jnp.dot(query_latent, query_absorb, preferred_element_type=jnp.float32).astype(jnp.bfloat16)
        query_full = jnp.concatenate([query_lat, rope_part], axis=1)
        query_full = query_full.reshape(SEQS, QROWS, LATENT + ROPE).astype(jnp.float32)
        scores = jnp.einsum('srk,stk->srt', query_full, caches) * temper
        scores = jnp.where(visible, scores, -1e+30)
        weights_soft = jax.nn.softmax(scores, axis=-1).astype(jnp.bfloat16)
        context = jnp.einsum('srt,stc->src', weights_soft.astype(jnp.float32), caches[:, :, :LATENT])
        context = context.astype(jnp.bfloat16).reshape(ROWS, LATENT)
        return (total + jnp.dot(context, out_absorb, preferred_element_type=jnp.float32), None)
    start = jnp.zeros((ROWS, D), jnp.float32)
    total = lax.scan(one_head, start, (w_uq, w_uk, w_uv, w_out, rope_heads))[0]
    return total.astype(jnp.bfloat16)
```

```python
import math

import jax
import jax.numpy as jnp
from jax import lax
from jax.experimental import pallas as pl
from jax.experimental.pallas import tpu as pltpu
from jax.sharding import Mesh, PartitionSpec as P

AXES = ("x", "yh", "yl", "zh", "zlh", "zll", "c")
SIZES = (4, 2, 2, 2, 4, 2, 2)
FSDP = ("x", "yh", "yl", "zh")
HEAD = ("zlh", "zll", "c")
PLANE = ("x", "yh", "yl")
COLUMN = ("zlh", "zll", "zh")
BF16 = jnp.bfloat16
F32 = jnp.float32
VMEM_LIMIT = 40 * 1024 * 1024


def swap(block, axis):
    return lax.ppermute(block, axis, [(0, 1), (1, 0)])


def pair(block, axis):
    theirs = swap(block, axis)
    upper = lax.axis_index(axis) == 1
    return jnp.where(
        upper,
        jnp.concatenate([theirs, block], axis=0),
        jnp.concatenate([block, theirs], axis=0),
    )


def exchange(blocks, axes):
    return lax.all_to_all(blocks, axes, 0, 0, tiled=True)


def dot(a, b):
    return jnp.dot(a, b, preferred_element_type=F32)


def dot_nt(a, b):
    return lax.dot_general(a, b, (((1,), (1,)), ((), ())), preferred_element_type=F32)


def attend_kernel(
    starts, latent, weights, rope, lengths, kv0, kv1, kv2, kv3, value_out, scores, *, sizes, temper
):
    rows, heads, n_uq, n_uk, n_uv, width = sizes
    caches = (kv0, kv1, kv2, kv3)
    per_block = kv0.shape[0]
    chunk = per_block * len(caches) // starts.shape[0]
    query = latent[...]
    limit = lengths[...]
    lanes = lax.broadcasted_iota(jnp.int32, (rows, chunk), 1)
    for h in range(heads):
        w_uq = weights[:, h, :, 0:n_uq, :].reshape(-1, weights.shape[-1])
        w_uk = weights[:, h, :, n_uq : n_uq + n_uk, :].reshape(-1, weights.shape[-1])
        q_nope = dot(query, w_uq).astype(BF16)
        q_lat = dot_nt(q_nope, w_uk).astype(BF16)
        rope_width = kv0.shape[1] - width
        q_rope = rope[:, h * rope_width : (h + 1) * rope_width]
        top = jnp.full((rows, 1), -1e30, F32)
        for b, cache in enumerate(caches):
            s = dot_nt(q_lat, cache[:, :width]) + dot_nt(q_rope, cache[:, width:])
            s = s * temper
            for i in range(per_block // chunk):
                k = b * (per_block // chunk) + i
                piece = s[:, i * chunk : (i + 1) * chunk]
                piece = jnp.where(lanes + starts[k] < limit, piece, -1e30)
                top = jnp.maximum(top, jnp.max(piece, axis=1, keepdims=True))
                scores[:, k * chunk : (k + 1) * chunk] = piece
        total = jnp.zeros((rows, 1), F32)
        context = jnp.zeros((rows, width), F32)
        for b, cache in enumerate(caches):
            p = jnp.exp(scores[:, b * per_block : (b + 1) * per_block] - top)
            total = total + jnp.sum(p, axis=1, keepdims=True)
            context = context + dot(p.astype(BF16), cache[:, :width])
        context = (context / total).astype(BF16)
        w_uv = weights[:, h, :, n_uq + n_uk :, :].reshape(-1, weights.shape[-1])
        vdim = w_uv.shape[1]
        value_out[:, h * vdim : (h + 1) * vdim] = dot(context, w_uv).astype(BF16)


def project_kernel(values, weights, out):
    total = None
    half = values.shape[3]
    for y in range(values.shape[1]):
        rows = values[:, y].reshape(-1, half)
        part = dot(rows, weights[y * half : (y + 1) * half, :])
        total = part if total is None else total + part
    out[...] = total.astype(BF16)


def local(query_latent, query_rope, lengths, kv_cache, w_uq, w_uk, w_uv, w_out):
    yl, zh, zll, core = (lax.axis_index(a) for a in ("yl", "zh", "zll", "c"))
    plane = 16
    tokens, kv_width = kv_cache.shape
    latent_width = w_uk.shape[1] * 32
    rope_width = kv_width - latent_width
    temper = 1.0 / math.sqrt(w_uq.shape[2] + rope_width)
    n_uq, n_uk, n_uv = w_uq.shape[1], w_uk.shape[1], w_uv.shape[1]

    stacked = jnp.concatenate([w_uq, w_uk, w_uv], axis=1)
    stacked = lax.all_to_all(stacked, "zh", 0, 1, tiled=True)
    quarter = tokens // 4
    piece = lax.dynamic_slice_in_dim(kv_cache, (core * 2 + zll) * quarter, quarter, 0)
    piece = swap(piece, "zh")
    near = swap(kv_cache, "yl")
    latent_rows = pair(query_latent, "zh")
    rope_rows = query_rope.reshape(query_rope.shape[0], -1)
    rope_rows = lax.all_to_all(rope_rows, "zh", 1, 0, tiled=True)

    heads = stacked.shape[0] // 2
    weights = jnp.broadcast_to(
        stacked.reshape((1, 2, heads) + stacked.shape[1:]),
        (plane // 2, 2, heads) + stacked.shape[1:],
    ).reshape((plane * heads,) + stacked.shape[1:])
    weights = exchange(weights, PLANE).reshape(plane, heads, 2, n_uq + n_uk + n_uv, -1)

    latent_rows = pair(latent_rows, "yl")
    rope_rows = lax.all_to_all(rope_rows, "yl", 1, 0, tiled=True)

    piece = jnp.concatenate([piece, swap(piece, "yl")], axis=0)
    piece = jnp.concatenate([piece, swap(piece, "zll")], axis=0)
    far = swap(piece, "c")
    starts = []
    for ylo in (yl, 1 - yl):
        for i in range(4):
            starts.append((ylo * 2 + zh) * tokens + i * quarter)
    for co in (core, 1 - core):
        for zo in (zll, 1 - zll):
            for ylo in (yl, 1 - yl):
                starts.append((ylo * 2 + 1 - zh) * tokens + (co * 2 + zo) * quarter)
    starts = jnp.stack(starts).astype(jnp.int32)

    rows = latent_rows.shape[0]
    sequence = lax.axis_index("x") * 2 + lax.axis_index("yh")
    row_lengths = lax.dynamic_slice_in_dim(lengths, sequence * rows, rows, 0)[:, None]
    vdim = w_uv.shape[2]
    vmem = pl.BlockSpec(memory_space=pltpu.VMEM)
    values = pl.pallas_call(
        lambda *refs: attend_kernel(
            *refs, sizes=(rows, heads, n_uq, n_uk, n_uv, latent_width), temper=temper
        ),
        out_shape=jax.ShapeDtypeStruct((rows, heads * vdim), BF16),
        in_specs=[pl.BlockSpec(memory_space=pltpu.SMEM)] + [vmem] * 8,
        out_specs=vmem,
        scratch_shapes=[pltpu.VMEM((rows, 4 * tokens), F32)],
        compiler_params=pltpu.CompilerParams(vmem_limit_bytes=VMEM_LIMIT),
        cost_estimate=pl.CostEstimate(flops=10**9, bytes_accessed=5 * 10**6, transcendentals=0),
        name="attend",
    )(starts, latent_rows, weights, rope_rows, row_lengths, kv_cache, near, piece, far)

    w_out, _ = lax.optimization_barrier((w_out, stacked))
    out_proj = lax.all_to_all(w_out, "zh", 0, 1, tiled=True)
    four, vpart, width = out_proj.shape
    columns = width // plane
    out_proj = out_proj.reshape(four, vpart, plane, columns)
    out_proj = exchange(jnp.transpose(out_proj, (2, 0, 1, 3)), PLANE)
    out_proj = jnp.transpose(out_proj, (1, 0, 2, 3)).reshape(four * plane * vpart, columns)

    gathered = exchange(
        jnp.broadcast_to(values[None], (plane,) + values.shape).reshape(-1, values.shape[1]), PLANE
    ).reshape(plane // 2, 2, rows, heads * vdim)
    all_rows = plane // 2 * rows
    partial_out = pl.pallas_call(
        project_kernel,
        out_shape=jax.ShapeDtypeStruct((all_rows, columns), BF16),
        in_specs=[vmem, vmem],
        out_specs=vmem,
        compiler_params=pltpu.CompilerParams(vmem_limit_bytes=VMEM_LIMIT),
        cost_estimate=pl.CostEstimate(flops=2 * 10**8, bytes_accessed=2 * 10**6, transcendentals=0),
        name="project",
    )(gathered, out_proj)

    total = exchange(partial_out, "c").reshape(2, all_rows // 2, columns)
    total = jnp.sum(total.astype(F32), axis=0).astype(BF16)
    total = exchange(total, COLUMN).reshape(16, all_rows // 32, columns)
    total = jnp.sum(total.astype(F32), axis=0).astype(BF16)
    route = []
    for xy in range(16):
        for z_hi in range(2):
            for z_lo in range(8):
                for c in range(2):
                    source = ((xy * 2 + z_hi) * 8 + z_lo) * 2 + c
                    route.append((source, (c * 16 + z_lo * 2 + z_hi) * 16 + xy))
    return lax.ppermute(total, AXES, route)


def solution(mesh):
    fine = Mesh(mesh.devices.reshape(SIZES), AXES)
    placed = (
        P(FSDP, None),
        P(FSDP, HEAD, None),
        P(),
        P(FSDP, None),
        P(HEAD, FSDP, None),
        P(HEAD, FSDP, None),
        P(HEAD, FSDP, None),
        P(HEAD, FSDP, None),
    )
    return jax.shard_map(
        local, mesh=fine, in_specs=placed, out_specs=P(FSDP, HEAD), check_vma=False
    )
```

```python
import math

import jax
import jax.numpy as jnp
from jax import lax
from jax.experimental import pallas as pl
from jax.experimental.pallas import tpu as pltpu
from jax.sharding import Mesh, PartitionSpec as P

AXES = ("x", "yh", "yl", "zh", "zlh", "zll", "c")
SIZES = (4, 2, 2, 2, 4, 2, 2)
FSDP = ("x", "yh", "yl", "zh")
HEAD = ("zlh", "zll", "c")
PLANE = ("x", "yh", "yl")
COLUMN = ("zlh", "zll", "zh")
BF16 = jnp.bfloat16
F32 = jnp.float32
VMEM_LIMIT = 40 * 1024 * 1024


def swap(block, axis):
    return lax.ppermute(block, axis, [(0, 1), (1, 0)])


def ordered(ours, theirs, position, dim):
    return jnp.where(
        position == 1,
        jnp.concatenate([theirs, ours], axis=dim),
        jnp.concatenate([ours, theirs], axis=dim),
    )


def pack(blocks):
    return jnp.concatenate([block.reshape(-1, block.shape[-1]) for block in blocks], axis=0)


def unpack(packed, shapes):
    blocks, at = [], 0
    for shape in shapes:
        count = math.prod(shape[:-1])
        blocks.append(packed[at : at + count].reshape(shape))
        at += count
    return blocks


def exchange(blocks, axes):
    return lax.all_to_all(blocks, axes, 0, 0, tiled=True)


def dot(a, b):
    return jnp.dot(a, b, preferred_element_type=F32)


def dot_nt(a, b):
    return lax.dot_general(a, b, (((1,), (1,)), ((), ())), preferred_element_type=F32)


def attend_kernel(
    starts, latent, weights, rope, lengths, kv0, kv1, kv2, kv3, value_out, scores, *, sizes, temper
):
    rows, heads, n_uq, n_uk, n_uv, width = sizes
    caches = (kv0, kv1, kv2, kv3)
    per_block = kv0.shape[1]
    chunk = per_block * len(caches) // starts.shape[0]
    query = jnp.concatenate([latent[i] for i in range(latent.shape[0])], axis=1)
    limit = lengths[...]
    lanes = lax.broadcasted_iota(jnp.int32, (rows, chunk), 1)
    for h in range(heads):
        w_uq = weights[:, h, :, 0:n_uq, :].reshape(-1, weights.shape[-1])
        w_uk = weights[:, h, :, n_uq : n_uq + n_uk, :].reshape(-1, weights.shape[-1])
        q_nope = dot(query, w_uq).astype(BF16)
        q_lat = dot_nt(q_nope, w_uk).astype(BF16)
        rope_width = kv0.shape[0] - width
        q_rope = rope[:, h * rope_width : (h + 1) * rope_width]
        top = jnp.full((rows, 1), -1e30, F32)
        for b, cache in enumerate(caches):
            s = dot(q_lat, cache[:width, :]) + dot(q_rope, cache[width:, :])
            s = s * temper
            for i in range(per_block // chunk):
                k = b * (per_block // chunk) + i
                piece = s[:, i * chunk : (i + 1) * chunk]
                piece = jnp.where(lanes + starts[k] < limit, piece, -1e30)
                top = jnp.maximum(top, jnp.max(piece, axis=1, keepdims=True))
                scores[:, k * chunk : (k + 1) * chunk] = piece
        total = jnp.zeros((rows, 1), F32)
        context = jnp.zeros((rows, width), F32)
        for b, cache in enumerate(caches):
            p = jnp.exp(scores[:, b * per_block : (b + 1) * per_block] - top)
            total = total + jnp.sum(p, axis=1, keepdims=True)
            context = context + dot_nt(p.astype(BF16), cache[:width, :])
        context = (context / total).astype(BF16)
        w_uv = weights[:, h, :, n_uq + n_uk :, :].reshape(-1, weights.shape[-1])
        vdim = w_uv.shape[1]
        value_out[:, h * vdim : (h + 1) * vdim] = dot(context, w_uv).astype(BF16)


def project_kernel(values, weights, out):
    total = None
    half = values.shape[3]
    for y in range(values.shape[1]):
        rows = values[:, y].reshape(-1, half)
        part = dot(rows, weights[y * half : (y + 1) * half, :])
        total = part if total is None else total + part
    out[...] = total.astype(BF16)


def local(query_latent, query_rope, lengths, kv_cache, w_uq, w_uk, w_uv, w_out):
    yl, zh, zll, core = (lax.axis_index(a) for a in ("yl", "zh", "zll", "c"))
    plane = 16
    cache = kv_cache.T
    kv_width, tokens = cache.shape
    latent_width = w_uk.shape[1] * 32
    rope_width = kv_width - latent_width
    lanes = w_uq.shape[2]
    temper = 1.0 / math.sqrt(lanes + rope_width)
    n_uq, n_uk, n_uv = w_uq.shape[1], w_uk.shape[1], w_uv.shape[1]
    n_all = n_uq + n_uk + n_uv
    own_rows = query_latent.shape[0]
    heads_in = w_uq.shape[0]
    four, heads = heads_in // 2, heads_in // 4

    quarter = tokens // 4
    piece = lax.dynamic_slice_in_dim(cache, (core * 2 + zll) * quarter, quarter, 1)
    stacked = jnp.concatenate([w_uq, w_uk, w_uv], axis=1)
    kept = lax.dynamic_slice_in_dim(stacked, zh * four, four, 0)
    given = lax.dynamic_slice_in_dim(stacked, (1 - zh) * four, four, 0)
    latent = jnp.transpose(query_latent.reshape(own_rows, -1, lanes), (1, 0, 2))
    rope = jnp.transpose(query_rope.reshape(own_rows, -1, lanes), (1, 0, 2))
    rope_kept = lax.dynamic_slice_in_dim(rope, zh * 2, 2, 0)
    rope_given = lax.dynamic_slice_in_dim(rope, (1 - zh) * 2, 2, 0)
    sent = [piece, given, latent, rope_given]
    packed = pack(sent)
    near = swap(cache, "yl")
    far_piece, taken, latent_far, rope_far = unpack(
        swap(packed, "zh"), [block.shape for block in sent]
    )

    vpart, width = w_out.shape[1:]
    columns = width // plane
    out_proj = w_out.reshape(heads_in * vpart, plane, columns)
    out_proj = exchange(jnp.transpose(out_proj, (1, 0, 2)), PLANE)
    out_proj = out_proj.reshape(plane, heads_in, vpart, columns)

    far_piece, taken, latent_far, rope_far, near, out_proj = lax.optimization_barrier(
        (far_piece, taken, latent_far, rope_far, near, out_proj)
    )

    proj_kept = lax.dynamic_slice_in_dim(out_proj, zh * four, four, 1)
    proj_given = lax.dynamic_slice_in_dim(out_proj, (1 - zh) * four, four, 1)
    proj_far = [swap(proj_given[a:b], "zh") for a, b in ((0, 4), (4, 8), (8, 16))]

    stacked = ordered(kept, taken, zh, 1)
    weights = jnp.broadcast_to(
        stacked.reshape((1, 2, heads, 2 * n_all, lanes)), (plane // 2, 2, heads, 2 * n_all, lanes)
    ).reshape(plane * heads, 2 * n_all, lanes)
    weights = exchange(weights, PLANE).reshape(plane, heads, 2, n_all, lanes)

    latent = ordered(latent, latent_far, zh, 1)
    rope = ordered(rope_kept, rope_far, zh, 1)
    rope_kept = lax.dynamic_slice_in_dim(rope, yl, 1, 0)
    rope_given = lax.dynamic_slice_in_dim(rope, 1 - yl, 1, 0)
    sent = [far_piece, latent, rope_given]
    piece_y, latent_y, rope_y = unpack(swap(pack(sent), "yl"), [block.shape for block in sent])
    piece_z = swap(far_piece, "zll")
    piece_yz = lax.ppermute(far_piece, ("yl", "zll"), [(0, 3), (1, 2), (2, 1), (3, 0)])
    far = jnp.concatenate([far_piece, piece_y, piece_z, piece_yz], axis=1)
    far, proj_far[0] = lax.optimization_barrier((far, proj_far[0]))
    far_other = swap(far, "c")
    latent = ordered(latent, latent_y, yl, 1)
    rope = ordered(rope_kept[0], rope_y[0], yl, 0)

    starts = []
    for ylo in (yl, 1 - yl):
        for i in range(4):
            starts.append((ylo * 2 + zh) * tokens + i * quarter)
    for co in (core, 1 - core):
        for zo in (zll, 1 - zll):
            for ylo in (yl, 1 - yl):
                starts.append((ylo * 2 + 1 - zh) * tokens + (co * 2 + zo) * quarter)
    starts = jnp.stack(starts).astype(jnp.int32)

    weights, proj_far[1] = lax.optimization_barrier((weights, proj_far[1]))
    rows = latent.shape[1]
    sequence = lax.axis_index("x") * 2 + lax.axis_index("yh")
    row_lengths = lax.dynamic_slice_in_dim(lengths, sequence * rows, rows, 0)[:, None]
    vmem = pl.BlockSpec(memory_space=pltpu.VMEM)
    values = pl.pallas_call(
        lambda *refs: attend_kernel(
            *refs, sizes=(rows, heads, n_uq, n_uk, n_uv, latent_width), temper=temper
        ),
        out_shape=jax.ShapeDtypeStruct((rows, heads * lanes), BF16),
        in_specs=[pl.BlockSpec(memory_space=pltpu.SMEM)] + [vmem] * 8,
        out_specs=vmem,
        scratch_shapes=[pltpu.VMEM((rows, 4 * tokens), F32)],
        compiler_params=pltpu.CompilerParams(vmem_limit_bytes=VMEM_LIMIT),
        cost_estimate=pl.CostEstimate(flops=10**9, bytes_accessed=5 * 10**6, transcendentals=0),
        name="attend",
    )(starts, latent, weights, rope, row_lengths, cache, near, far, far_other)

    values, proj_far[2] = lax.optimization_barrier((values, proj_far[2]))
    out_proj = ordered(proj_kept, jnp.concatenate(proj_far, axis=0), zh, 2)
    out_proj = jnp.transpose(out_proj, (1, 0, 2, 3)).reshape(-1, columns)
    gathered = exchange(
        jnp.broadcast_to(values[None], (plane,) + values.shape).reshape(-1, values.shape[1]), PLANE
    ).reshape(plane // 2, 2, rows, heads * lanes)
    all_rows = plane // 2 * rows
    partial_out = pl.pallas_call(
        project_kernel,
        out_shape=jax.ShapeDtypeStruct((all_rows, columns), BF16),
        in_specs=[vmem, vmem],
        out_specs=vmem,
        compiler_params=pltpu.CompilerParams(vmem_limit_bytes=VMEM_LIMIT),
        cost_estimate=pl.CostEstimate(flops=2 * 10**8, bytes_accessed=2 * 10**6, transcendentals=0),
        name="project",
    )(gathered, out_proj)

    total = exchange(partial_out, "c").reshape(2, all_rows // 2, columns)
    total = jnp.sum(total.astype(F32), axis=0).astype(BF16)
    total = exchange(total, COLUMN).reshape(16, all_rows // 32, columns)
    total = jnp.sum(total.astype(F32), axis=0).astype(BF16)
    route = []
    for xy in range(16):
        for z_hi in range(2):
            for z_lo in range(8):
                for c in range(2):
                    source = ((xy * 2 + z_hi) * 8 + z_lo) * 2 + c
                    route.append((source, (c * 16 + z_lo * 2 + z_hi) * 16 + xy))
    return lax.ppermute(total, AXES, route)


def solution(mesh):
    fine = Mesh(mesh.devices.reshape(SIZES), AXES)
    placed = (
        P(FSDP, None),
        P(FSDP, HEAD, None),
        P(),
        P(FSDP, None),
        P(HEAD, FSDP, None),
        P(HEAD, FSDP, None),
        P(HEAD, FSDP, None),
        P(HEAD, FSDP, None),
    )
    return jax.shard_map(
        local, mesh=fine, in_specs=placed, out_specs=P(FSDP, HEAD), check_vma=False
    )
```

```python
import math

import jax
import jax.numpy as jnp
from jax import lax
from jax.experimental import pallas as pl
from jax.experimental.pallas import tpu as pltpu
from jax.sharding import Mesh, PartitionSpec as P

AXES = ("x", "yh", "yl", "zh", "zlh", "zll", "c")
SIZES = (4, 2, 2, 2, 4, 2, 2)
FSDP = ("x", "yh", "yl", "zh")
HEAD = ("zlh", "zll", "c")
PLANE = ("x", "yh", "yl")
COLUMN = ("zlh", "zll", "zh")
BF16 = jnp.bfloat16
F32 = jnp.float32
VMEM_LIMIT = 40 * 1024 * 1024
UNPACK_FLOPS = 2 * 10**10


def swap(block, axis):
    return lax.ppermute(block, axis, [(0, 1), (1, 0)])


def ordered(ours, theirs, position, dim):
    return jnp.where(
        position == 1,
        jnp.concatenate([theirs, ours], axis=dim),
        jnp.concatenate([ours, theirs], axis=dim),
    )


def pack(blocks):
    return jnp.concatenate([block.reshape(-1, block.shape[-1]) for block in blocks], axis=0)


def unpack(packed, shapes):
    blocks, at = [], 0
    for shape in shapes:
        count = math.prod(shape[:-1])
        blocks.append(packed[at : at + count].reshape(shape))
        at += count
    return blocks


def exchange(blocks, axes):
    return lax.all_to_all(blocks, axes, 0, 0, tiled=True)


def dot(a, b):
    return jnp.dot(a, b, preferred_element_type=F32)


def dot_nt(a, b):
    return lax.dot_general(a, b, (((1,), (1,)), ((), ())), preferred_element_type=F32)


def unpack_kernel(place, received, kept, latent, rope, sent, packed, piece, rope_out, *, sizes):
    n_piece, n_all, own_rows, copies = sizes
    zh, yl = place[0], place[1]
    four = kept.shape[0]
    ours = pl.ds(pl.multiple_of(zh * n_all, 16), n_all)
    theirs = pl.ds(pl.multiple_of((1 - zh) * n_all, 16), n_all)
    at = n_piece
    for h in range(four):
        mine, other = kept[h], received[at : at + n_all]
        for copy in range(copies):
            sent[copy, h, ours] = mine
            sent[copy, h, theirs] = other
        at += n_all
    ours = pl.ds(pl.multiple_of(zh * own_rows, 16), own_rows)
    theirs = pl.ds(pl.multiple_of((1 - zh) * own_rows, 16), own_rows)
    to = n_piece
    for i in range(latent.shape[0]):
        packed[pl.ds(pl.multiple_of(to + zh * own_rows, 16), own_rows)] = latent[i]
        packed[pl.ds(pl.multiple_of(to + (1 - zh) * own_rows, 16), own_rows)] = received[
            at : at + own_rows
        ]
        to += 2 * own_rows
        at += own_rows
    lower = [rope[0], received[at : at + own_rows]]
    upper = [rope[1], received[at + own_rows : at + 2 * own_rows]]
    stay = [jnp.where(yl == 0, x, y) for x, y in zip(lower, upper)]
    go = [jnp.where(yl == 0, y, x) for x, y in zip(lower, upper)]
    rope_out[ours] = stay[0]
    rope_out[theirs] = stay[1]
    packed[pl.ds(pl.multiple_of(to + zh * own_rows, 16), own_rows)] = go[0]
    packed[pl.ds(pl.multiple_of(to + (1 - zh) * own_rows, 16), own_rows)] = go[1]
    packed[:n_piece] = received[:n_piece]
    piece[...] = received[:n_piece]


def attend_kernel(
    place,
    ours,
    theirs,
    weights,
    rope_ours,
    lengths,
    kv0,
    kv1,
    kv2,
    kv3,
    keep_out,
    give_out,
    query_rows,
    rope,
    scores,
    *,
    sizes,
    temper,
):
    rows, heads, n_uq, n_uk, n_uv, width, n_starts = sizes
    caches = (kv0, kv1, kv2, kv3)
    zh, yl, starts = place[0], place[1], [place[2 + i] for i in range(n_starts)]
    per_block = kv0.shape[1]
    chunk = per_block * len(caches) // n_starts
    half = rows // 2
    mine = pl.ds(pl.multiple_of(yl * half, 16), half)
    other = pl.ds(pl.multiple_of((1 - yl) * half, 16), half)
    at = kv0.shape[0]
    lane_count = ours.shape[1]
    for i in range(query_rows.shape[1] // lane_count):
        lanes_here = slice(i * lane_count, (i + 1) * lane_count)
        query_rows[mine, lanes_here] = ours[at : at + half]
        query_rows[other, lanes_here] = theirs[at : at + half]
        at += half
    rope[mine, :] = rope_ours[...]
    rope[other, :] = theirs[at : at + half]
    query = query_rows[...]
    limit = lengths[...]
    lanes = lax.broadcasted_iota(jnp.int32, (rows, chunk), 1)
    values = []
    for h in range(heads):
        w_uq = weights[:, h, :, 0:n_uq, :].reshape(-1, weights.shape[-1])
        w_uk = weights[:, h, :, n_uq : n_uq + n_uk, :].reshape(-1, weights.shape[-1])
        q_nope = dot(query, w_uq).astype(BF16)
        q_lat = dot_nt(q_nope, w_uk).astype(BF16)
        rope_width = kv0.shape[0] - width
        q_rope = rope[:, h * rope_width : (h + 1) * rope_width]
        top = jnp.full((rows, 1), -1e30, F32)
        for b, cache in enumerate(caches):
            s = dot(q_lat, cache[:width, :]) + dot(q_rope, cache[width:, :])
            s = s * temper
            for i in range(per_block // chunk):
                k = b * (per_block // chunk) + i
                piece = s[:, i * chunk : (i + 1) * chunk]
                piece = jnp.where(lanes + starts[k] < limit, piece, -1e30)
                top = jnp.maximum(top, jnp.max(piece, axis=1, keepdims=True))
                scores[:, k * chunk : (k + 1) * chunk] = piece
        total = jnp.zeros((rows, 1), F32)
        context = jnp.zeros((rows, width), F32)
        for b, cache in enumerate(caches):
            p = jnp.exp(scores[:, b * per_block : (b + 1) * per_block] - top)
            total = total + jnp.sum(p, axis=1, keepdims=True)
            context = context + dot_nt(p.astype(BF16), cache[:width, :])
        context = (context / total).astype(BF16)
        w_uv = weights[:, h, :, n_uq + n_uk :, :].reshape(-1, weights.shape[-1])
        values.append(dot(context, w_uv).astype(BF16))
    vdim = values[0].shape[1]
    wide = heads * vdim
    to = lax.broadcasted_iota(jnp.int32, (wide, wide), 1)
    source = lax.broadcasted_iota(jnp.int32, (wide, wide), 0)
    side = to // (wide // 2)
    head = to % (wide // 2) // (vdim // 2)
    item = to % (vdim // 2)
    wanted = head * vdim + item // 4 * 8 + jnp.where(side == 0, zh, 1 - zh) * 4 + item % 4
    move = jnp.where(source == wanted, 1.0, 0.0).astype(BF16)
    moved = dot(jnp.concatenate(values, axis=1), move).astype(BF16)
    keep_out[...] = moved[:, : wide // 2]
    give_out[...] = moved[:, wide // 2 :]


def project_kernel(values, weights, out):
    total = None
    half = values.shape[3]
    for y in range(values.shape[1]):
        rows = values[:, y].reshape(-1, half)
        part = dot(rows, weights[y * half : (y + 1) * half, :])
        total = part if total is None else total + part
    out[...] = total.astype(BF16)


def local(query_latent, query_rope, lengths, kv_cache, w_uq, w_uk, w_uv, w_out):
    yl, zh, zll, core = (lax.axis_index(a) for a in ("yl", "zh", "zll", "c"))
    plane = 16
    cache = kv_cache.T
    kv_width, tokens = cache.shape
    latent_width = w_uk.shape[1] * 32
    rope_width = kv_width - latent_width
    lanes = w_uq.shape[2]
    temper = 1.0 / math.sqrt(lanes + rope_width)
    n_uq, n_uk, n_uv = w_uq.shape[1], w_uk.shape[1], w_uv.shape[1]
    n_all = n_uq + n_uk + n_uv
    own_rows = query_latent.shape[0]
    heads_in = w_uq.shape[0]
    four, heads = heads_in // 2, heads_in // 4

    quarter = tokens // 4
    piece = lax.dynamic_slice_in_dim(cache, (core * 2 + zll) * quarter, quarter, 1)
    stacked = jnp.concatenate([w_uq, w_uk, w_uv], axis=1)
    kept = lax.dynamic_slice_in_dim(stacked, zh * four, four, 0)
    given = lax.dynamic_slice_in_dim(stacked, (1 - zh) * four, four, 0)
    latent = jnp.transpose(query_latent.reshape(own_rows, -1, lanes), (1, 0, 2))
    rope = jnp.transpose(query_rope.reshape(own_rows, -1, lanes), (1, 0, 2))
    rope_kept = lax.dynamic_slice_in_dim(rope, zh * 2, 2, 0)
    rope_given = lax.dynamic_slice_in_dim(rope, (1 - zh) * 2, 2, 0)
    sent = [piece, given, latent, rope_given]
    packed = pack(sent)
    near = swap(cache, "yl")
    received = swap(pack(sent), "zh")
    place = jnp.stack([zh, yl]).astype(jnp.int32)
    vmem = pl.BlockSpec(memory_space=pltpu.VMEM)
    smem = pl.BlockSpec(memory_space=pltpu.SMEM)
    n_pack = kv_width + (2 * latent.shape[0] + 2) * own_rows
    sent, packed, far_piece, rope_kept = pl.pallas_call(
        lambda *refs: unpack_kernel(*refs, sizes=(kv_width, n_all, own_rows, plane // 2)),
        out_shape=(
            jax.ShapeDtypeStruct((plane // 2, four, 2 * n_all, lanes), BF16),
            jax.ShapeDtypeStruct((n_pack, lanes), BF16),
            jax.ShapeDtypeStruct((kv_width, quarter), BF16),
            jax.ShapeDtypeStruct((2 * own_rows, lanes), BF16),
        ),
        in_specs=[smem] + [vmem] * 4,
        out_specs=(vmem,) * 4,
        compiler_params=pltpu.CompilerParams(vmem_limit_bytes=VMEM_LIMIT),
        cost_estimate=pl.CostEstimate(
            flops=UNPACK_FLOPS, bytes_accessed=3 * 10**6, transcendentals=0
        ),
        name="unpack",
    )(place, received, kept, latent, rope_kept)

    vpart, width = w_out.shape[1:]
    columns = width // plane
    out_proj = w_out.reshape(heads_in * vpart, plane, columns)
    out_proj = exchange(jnp.transpose(out_proj, (1, 0, 2)), PLANE)
    sent, packed, far_piece, near, out_proj = lax.optimization_barrier(
        (sent, packed, far_piece, near, out_proj)
    )

    weights = exchange(sent.reshape(plane * heads, 2 * n_all, lanes), PLANE)
    weights = weights.reshape(plane, heads, 2, n_all, lanes)

    packed_y = swap(packed, "yl")
    piece_z = swap(far_piece, "zll")
    piece_yz = lax.ppermute(far_piece, ("yl", "zll"), [(0, 3), (1, 2), (2, 1), (3, 0)])
    far = jnp.concatenate([far_piece, packed_y[:kv_width], piece_z, piece_yz], axis=1)
    far_other = swap(far, "c")

    starts = []
    for ylo in (yl, 1 - yl):
        for i in range(4):
            starts.append((ylo * 2 + zh) * tokens + i * quarter)
    for co in (core, 1 - core):
        for zo in (zll, 1 - zll):
            for ylo in (yl, 1 - yl):
                starts.append((ylo * 2 + 1 - zh) * tokens + (co * 2 + zo) * quarter)
    place = jnp.stack([zh, yl] + starts).astype(jnp.int32)

    rows = 4 * own_rows
    sequence = lax.axis_index("x") * 2 + lax.axis_index("yh")
    row_lengths = lax.dynamic_slice_in_dim(lengths, sequence * rows, rows, 0)[:, None]
    keep, give = pl.pallas_call(
        lambda *refs: attend_kernel(
            *refs,
            sizes=(rows, heads, n_uq, n_uk, n_uv, latent_width, len(starts)),
            temper=temper,
        ),
        out_shape=(jax.ShapeDtypeStruct((rows, lanes), BF16),) * 2,
        in_specs=[smem] + [vmem] * 9,
        out_specs=(vmem,) * 2,
        scratch_shapes=[
            pltpu.VMEM((rows, query_latent.shape[1]), BF16),
            pltpu.VMEM((rows, lanes), BF16),
            pltpu.VMEM((rows, 4 * tokens), F32),
        ],
        compiler_params=pltpu.CompilerParams(vmem_limit_bytes=VMEM_LIMIT),
        cost_estimate=pl.CostEstimate(flops=10**9, bytes_accessed=5 * 10**6, transcendentals=0),
        name="attend",
    )(place, packed, packed_y, weights, rope_kept, row_lengths, cache, near, far, far_other)

    values = ordered(keep, swap(give, "zh"), zh, 1)
    gathered = exchange(
        jnp.broadcast_to(values[None], (plane,) + values.shape).reshape(-1, values.shape[1]), PLANE
    ).reshape(plane // 2, 2, rows, heads * lanes)
    out_proj = out_proj.reshape(plane, 2, 2, heads, vpart, columns)
    out_proj = jnp.transpose(out_proj, (2, 1, 3, 0, 4, 5)).reshape(-1, columns)
    all_rows = plane // 2 * rows
    partial_out = pl.pallas_call(
        project_kernel,
        out_shape=jax.ShapeDtypeStruct((all_rows, columns), BF16),
        in_specs=[vmem, vmem],
        out_specs=vmem,
        compiler_params=pltpu.CompilerParams(vmem_limit_bytes=VMEM_LIMIT),
        cost_estimate=pl.CostEstimate(flops=2 * 10**8, bytes_accessed=2 * 10**6, transcendentals=0),
        name="project",
    )(gathered, out_proj)

    total = exchange(partial_out, "c").reshape(2, all_rows // 2, columns)
    total = jnp.sum(total.astype(F32), axis=0).astype(BF16)
    total = exchange(total, COLUMN).reshape(16, all_rows // 32, columns)
    total = jnp.sum(total.astype(F32), axis=0).astype(BF16)
    route = []
    for xy in range(16):
        for z_hi in range(2):
            for z_lo in range(8):
                for c in range(2):
                    source = ((xy * 2 + z_hi) * 8 + z_lo) * 2 + c
                    route.append((source, (c * 16 + z_lo * 2 + z_hi) * 16 + xy))
    return lax.ppermute(total, AXES, route)


def solution(mesh):
    fine = Mesh(mesh.devices.reshape(SIZES), AXES)
    placed = (
        P(FSDP, None),
        P(FSDP, HEAD, None),
        P(),
        P(FSDP, None),
        P(HEAD, FSDP, None),
        P(HEAD, FSDP, None),
        P(HEAD, FSDP, None),
        P(HEAD, FSDP, None),
    )
    return jax.shard_map(
        local, mesh=fine, in_specs=placed, out_specs=P(FSDP, HEAD), check_vma=False
    )
```

```python
import math

import jax
import jax.numpy as jnp
from jax import lax
from jax.experimental import pallas as pl
from jax.experimental.pallas import tpu as pltpu
from jax.sharding import Mesh, PartitionSpec as P

AXES = ("x", "yh", "yl", "zh", "zlh", "zll", "c")
SIZES = (4, 2, 2, 2, 4, 2, 2)
FSDP = ("x", "yh", "yl", "zh")
HEAD = ("zlh", "zll", "c")
PLANE = ("x", "yh", "yl")
COLUMN = ("zlh", "zll", "zh")
BF16 = jnp.bfloat16
F32 = jnp.float32
VMEM_LIMIT = 40 * 1024 * 1024
PACK_LIMIT = 60 * 1024 * 1024
UNPACK_FLOPS = 2 * 10**10


def swap(block, axis):
    return lax.ppermute(block, axis, [(0, 1), (1, 0)])


def exchange(blocks, axes):
    return lax.all_to_all(blocks, axes, 0, 0, tiled=True)


def dot(a, b):
    return jnp.dot(a, b, preferred_element_type=F32)


def dot_nt(a, b):
    return lax.dot_general(a, b, (((1,), (1,)), ((), ())), preferred_element_type=F32)


def head_pairs(rope):
    return [
        jnp.concatenate([rope[:, 2 * p, :], rope[:, 2 * p + 1, :]], axis=1)
        for p in range(rope.shape[1] // 2)
    ]


def pack_kernel(
    place, cache, w_uq, w_uk, w_uv, latent, rope, out, half_out, uq, uk, uv, latent_in, rope_in, sems
):
    zh, quarter = place[0], place[2]
    lanes, wide = out.shape[1], half_out.shape[1]
    width = cache.shape[0]
    four = uq.shape[0]
    given = pl.ds((1 - zh) * four, four)
    copies = [
        (cache.at[:, pl.ds(pl.multiple_of(quarter * lanes, lanes), lanes)], out.at[pl.ds(0, width)]),
        (w_uq.at[given], uq),
        (w_uk.at[given], uk),
        (w_uv.at[given], uv),
        (latent, latent_in),
        (rope, rope_in),
        (cache.at[:, pl.ds(pl.multiple_of(place[3] * wide, wide), wide)], half_out),
    ]
    copies = [pltpu.make_async_copy(x, y, sems.at[i]) for i, (x, y) in enumerate(copies)]
    for copy in copies:
        copy.start()
    for copy in copies:
        copy.wait()
    at = width
    for h in range(four):
        for w in (uq, uk, uv):
            out[at : at + w.shape[1]] = w[h]
            at += w.shape[1]
    rows = latent_in.shape[0]
    for i in range(latent_in.shape[1] // lanes):
        out[at : at + rows] = latent_in[:, i * lanes : (i + 1) * lanes]
        at += rows
    pairs = head_pairs(rope_in)
    for p in range(len(pairs) // 2):
        out[at : at + rows] = jnp.where(zh == 0, pairs[p + len(pairs) // 2], pairs[p])
        at += rows


def unpack_kernel(
    place, received, w_uq, w_uk, w_uv, latent, rope, sent, packed, piece, rope_out, *, sizes
):
    n_piece, copies = sizes
    zh, yl = place[0], place[1]
    four = w_uq.shape[0] // 2
    n_all = w_uq.shape[1] + w_uk.shape[1] + w_uv.shape[1]
    own_rows = latent.shape[0]
    lanes = packed.shape[1]
    theirs = pl.ds(pl.multiple_of((1 - zh) * n_all, 16), n_all)
    at = n_piece
    for h in range(four):
        other = received[at : at + n_all]
        for copy in range(copies):
            sent[copy, h, theirs] = other
        at += n_all
        to = zh * n_all
        for w in (w_uq, w_uk, w_uv):
            mine = w[zh * four + h]
            for copy in range(copies):
                sent[copy, h, pl.ds(pl.multiple_of(to, 16), w.shape[1])] = mine
            to += w.shape[1]
    ours = pl.ds(pl.multiple_of(zh * own_rows, 16), own_rows)
    theirs = pl.ds(pl.multiple_of((1 - zh) * own_rows, 16), own_rows)
    to = n_piece
    for i in range(latent.shape[1] // lanes):
        packed[pl.ds(pl.multiple_of(to + zh * own_rows, 16), own_rows)] = latent[
            :, i * lanes : (i + 1) * lanes
        ]
        packed[pl.ds(pl.multiple_of(to + (1 - zh) * own_rows, 16), own_rows)] = received[
            at : at + own_rows
        ]
        to += 2 * own_rows
        at += own_rows
    pairs = head_pairs(rope)
    lower = [jnp.where(zh == 0, pairs[0], pairs[2]), received[at : at + own_rows]]
    upper = [jnp.where(zh == 0, pairs[1], pairs[3]), received[at + own_rows : at + 2 * own_rows]]
    stay = [jnp.where(yl == 0, x, y) for x, y in zip(lower, upper)]
    go = [jnp.where(yl == 0, y, x) for x, y in zip(lower, upper)]
    rope_out[ours] = stay[0]
    rope_out[theirs] = stay[1]
    packed[pl.ds(pl.multiple_of(to + zh * own_rows, 16), own_rows)] = go[0]
    packed[pl.ds(pl.multiple_of(to + (1 - zh) * own_rows, 16), own_rows)] = go[1]
    packed[:n_piece] = received[:n_piece]
    piece[...] = received[:n_piece]


def attend_kernel(
    place,
    ours,
    theirs,
    weights,
    rope_ours,
    lengths,
    kv0,
    kv1,
    kv2,
    kv3,
    kv4,
    value_out,
    query_rows,
    rope,
    scores,
    *,
    sizes,
    temper,
):
    rows, heads, n_uq, n_uk, n_uv, width, n_starts = sizes
    caches = (kv0, kv1, kv2, kv3, kv4)
    yl, starts = place[1], [place[3 + i] for i in range(n_starts)]
    spans, tokens = [], 0
    for cache in caches:
        spans.append((tokens, tokens + cache.shape[1]))
        tokens += cache.shape[1]
    chunk = tokens // n_starts
    half = rows // 2
    mine = pl.ds(pl.multiple_of(yl * half, 16), half)
    other = pl.ds(pl.multiple_of((1 - yl) * half, 16), half)
    at = kv0.shape[0]
    lane_count = ours.shape[1]
    for i in range(query_rows.shape[1] // lane_count):
        lanes_here = slice(i * lane_count, (i + 1) * lane_count)
        query_rows[mine, lanes_here] = ours[at : at + half]
        query_rows[other, lanes_here] = theirs[at : at + half]
        at += half
    rope[mine, :] = rope_ours[...]
    rope[other, :] = theirs[at : at + half]
    query = query_rows[...]
    limit = lengths[...]
    lanes = lax.broadcasted_iota(jnp.int32, (rows, chunk), 1)
    values = []
    for h in range(heads):
        w_uq = weights[:, h, :, 0:n_uq, :].reshape(-1, weights.shape[-1])
        w_uk = weights[:, h, :, n_uq : n_uq + n_uk, :].reshape(-1, weights.shape[-1])
        q_nope = dot(query, w_uq).astype(BF16)
        q_lat = dot_nt(q_nope, w_uk).astype(BF16)
        rope_width = kv0.shape[0] - width
        q_rope = rope[:, h * rope_width : (h + 1) * rope_width]
        top = jnp.full((rows, 1), -1e30, F32)
        for (begin, end), cache in zip(spans, caches):
            s = dot(q_lat, cache[:width, :]) + dot(q_rope, cache[width:, :])
            s = s * temper
            for k in range(begin // chunk, end // chunk):
                piece = s[:, k * chunk - begin : (k + 1) * chunk - begin]
                piece = jnp.where(lanes + starts[k] < limit, piece, -1e30)
                top = jnp.maximum(top, jnp.max(piece, axis=1, keepdims=True))
                scores[:, k * chunk : (k + 1) * chunk] = piece
        total = jnp.zeros((rows, 1), F32)
        context = jnp.zeros((rows, width), F32)
        for (begin, end), cache in zip(spans, caches):
            p = jnp.exp(scores[:, begin:end] - top)
            total = total + jnp.sum(p, axis=1, keepdims=True)
            context = context + dot_nt(p.astype(BF16), cache[:width, :])
        context = (context / total).astype(BF16)
        w_uv = weights[:, h, :, n_uq + n_uk :, :].reshape(-1, weights.shape[-1])
        values.append(dot(context, w_uv).astype(BF16))
    vdim = values[0].shape[1]
    wide = heads * vdim
    to = lax.broadcasted_iota(jnp.int32, (wide, wide), 1)
    source = lax.broadcasted_iota(jnp.int32, (wide, wide), 0)
    head = to % (wide // 2) // (vdim // 2)
    item = to % (vdim // 2)
    wanted = head * vdim + item // 4 * 8 + to // (wide // 2) * 4 + item % 4
    move = jnp.where(source == wanted, 1.0, 0.0).astype(BF16)
    moved = dot(jnp.concatenate(values, axis=1), move).astype(BF16)
    for z in range(2):
        for c in range(2):
            value_out[z * 2 + c] = moved[
                c * half : (c + 1) * half, z * wide // 2 : (z + 1) * wide // 2
            ]


def project_kernel(place, values, ours, theirs, out):
    core = place[3]
    lanes = values.shape[-1]
    total = None
    for y in range(values.shape[1]):
        for z in range(2):
            for weights, c in ((ours, core), (theirs, 1 - core)):
                rows = values[:, y, z * 2 + c].reshape(-1, lanes)
                part = dot(rows, weights[y, z])
                total = part if total is None else total + part
    out[...] = total.astype(BF16)


def local(query_latent, query_rope, lengths, kv_cache, w_uq, w_uk, w_uv, w_out):
    yl, zh, zll, core = (lax.axis_index(a) for a in ("yl", "zh", "zll", "c"))
    plane = 16
    cache = kv_cache.T
    kv_width, tokens = cache.shape
    latent_width = w_uk.shape[1] * 32
    rope_width = kv_width - latent_width
    lanes = w_uq.shape[2]
    temper = 1.0 / math.sqrt(lanes + rope_width)
    n_uq, n_uk, n_uv = w_uq.shape[1], w_uk.shape[1], w_uv.shape[1]
    n_all = n_uq + n_uk + n_uv
    own_rows = query_latent.shape[0]
    heads_in = w_uq.shape[0]
    four, heads = heads_in // 2, heads_in // 4

    quarter = tokens // 4
    starts = []
    for i in range(4):
        starts.append((yl * 2 + zh) * tokens + i * quarter)
    for co in (core, 1 - core):
        for i in range(2):
            starts.append(((1 - yl) * 2 + zh) * tokens + (co * 2 + i) * quarter)
    for co in (core, 1 - core):
        for zo in (zll, 1 - zll):
            for ylo in (yl, 1 - yl):
                starts.append((ylo * 2 + 1 - zh) * tokens + (co * 2 + zo) * quarter)
    place = jnp.stack([zh, yl, core * 2 + zll, core]).astype(jnp.int32)
    vmem = pl.BlockSpec(memory_space=pltpu.VMEM)
    smem = pl.BlockSpec(memory_space=pltpu.SMEM)
    raw = (w_uq, w_uk, w_uv, query_latent, query_rope)
    latent_chunks = query_latent.shape[1] // lanes
    n_sent = kv_width + four * n_all + (latent_chunks + 2) * own_rows
    packed, near = pl.pallas_call(
        pack_kernel,
        out_shape=(
            jax.ShapeDtypeStruct((n_sent, lanes), BF16),
            jax.ShapeDtypeStruct((kv_width, tokens // 2), BF16),
        ),
        in_specs=[smem] + [pl.BlockSpec(memory_space=pltpu.HBM)] * 6,
        out_specs=(vmem,) * 2,
        scratch_shapes=[pltpu.VMEM((four,) + w.shape[1:], BF16) for w in raw[:3]]
        + [pltpu.VMEM(x.shape, BF16) for x in raw[3:]]
        + [pltpu.SemaphoreType.DMA((7,))],
        compiler_params=pltpu.CompilerParams(vmem_limit_bytes=PACK_LIMIT),
        cost_estimate=pl.CostEstimate(flops=10**6, bytes_accessed=10**6, transcendentals=0),
        name="pack",
    )(place, cache, *raw)
    near = swap(near, "yl")
    received = swap(packed, "zh")
    n_pack = kv_width + (2 * latent_chunks + 2) * own_rows
    sent, packed, far_piece, rope_kept = pl.pallas_call(
        lambda *refs: unpack_kernel(*refs, sizes=(kv_width, plane // 2)),
        out_shape=(
            jax.ShapeDtypeStruct((plane // 2, four, 2 * n_all, lanes), BF16),
            jax.ShapeDtypeStruct((n_pack, lanes), BF16),
            jax.ShapeDtypeStruct((kv_width, quarter), BF16),
            jax.ShapeDtypeStruct((2 * own_rows, lanes), BF16),
        ),
        in_specs=[smem] + [vmem] * 6,
        out_specs=(vmem,) * 4,
        compiler_params=pltpu.CompilerParams(vmem_limit_bytes=VMEM_LIMIT),
        cost_estimate=pl.CostEstimate(
            flops=UNPACK_FLOPS, bytes_accessed=3 * 10**6, transcendentals=0
        ),
        name="unpack",
    )(place, received, *raw)

    vpart, width = w_out.shape[1:]
    columns = width // plane
    out_proj = w_out.reshape(heads_in * vpart, plane, columns)
    out_proj = exchange(jnp.transpose(out_proj, (1, 0, 2)), PLANE)
    sent, packed, far_piece, near, out_proj = lax.optimization_barrier(
        (sent, packed, far_piece, near, out_proj)
    )
    out_proj = out_proj.reshape(plane, 2, 2, heads, vpart, columns)
    out_proj = jnp.transpose(out_proj, (2, 1, 3, 0, 4, 5)).reshape(2, 2, -1, columns)

    weights = exchange(sent.reshape(plane * heads, 2 * n_all, lanes), PLANE)
    weights = weights.reshape(plane, heads, 2, n_all, lanes)

    packed_y = swap(packed, "yl")
    piece_z = swap(far_piece, "zll")
    piece_yz = lax.ppermute(far_piece, ("yl", "zll"), [(0, 3), (1, 2), (2, 1), (3, 0)])
    far = jnp.concatenate([far_piece, packed_y[:kv_width], piece_z, piece_yz], axis=1)
    near_other = swap(near, "c")
    far, near_other, out_proj = lax.optimization_barrier((far, near_other, out_proj))
    far_other = swap(far, "c")
    out_proj_other = swap(out_proj, "c")

    rows = 4 * own_rows
    sequence = lax.axis_index("x") * 2 + lax.axis_index("yh")
    row_lengths = lax.dynamic_slice_in_dim(lengths, sequence * rows, rows, 0)[:, None]
    weights, out_proj_other = lax.optimization_barrier((weights, out_proj_other))
    place_all = jnp.stack([zh, yl, core] + starts).astype(jnp.int32)
    values = pl.pallas_call(
        lambda *refs: attend_kernel(
            *refs,
            sizes=(rows, heads, n_uq, n_uk, n_uv, latent_width, len(starts)),
            temper=temper,
        ),
        out_shape=jax.ShapeDtypeStruct((4, rows // 2, lanes), BF16),
        in_specs=[smem] + [vmem] * 10,
        out_specs=vmem,
        scratch_shapes=[
            pltpu.VMEM((rows, query_latent.shape[1]), BF16),
            pltpu.VMEM((rows, lanes), BF16),
            pltpu.VMEM((rows, 4 * tokens), F32),
        ],
        compiler_params=pltpu.CompilerParams(vmem_limit_bytes=VMEM_LIMIT),
        cost_estimate=pl.CostEstimate(flops=10**9, bytes_accessed=5 * 10**6, transcendentals=0),
        name="attend",
    )(place_all, packed, packed_y, weights, rope_kept, row_lengths, cache, near, near_other, far, far_other)

    values = exchange(values, ("zh", "c"))
    gathered = exchange(
        jnp.broadcast_to(values[None], (plane,) + values.shape).reshape((-1,) + values.shape[1:]),
        PLANE,
    ).reshape((plane // 2, 2) + values.shape)
    half_rows = plane // 2 * rows // 2
    partial_out = pl.pallas_call(
        project_kernel,
        out_shape=jax.ShapeDtypeStruct((half_rows, columns), BF16),
        in_specs=[smem] + [vmem] * 3,
        out_specs=vmem,
        compiler_params=pltpu.CompilerParams(vmem_limit_bytes=VMEM_LIMIT),
        cost_estimate=pl.CostEstimate(flops=2 * 10**8, bytes_accessed=2 * 10**6, transcendentals=0),
        name="project",
    )(place, gathered, out_proj, out_proj_other)

    total = exchange(partial_out, COLUMN).reshape(16, half_rows // 16, columns)
    total = jnp.sum(total.astype(F32), axis=0).astype(BF16)
    route = []
    for xy in range(16):
        for z_hi in range(2):
            for z_lo in range(8):
                for c in range(2):
                    source = ((xy * 2 + z_hi) * 8 + z_lo) * 2 + c
                    route.append((source, (z_lo * 4 + c * 2 + z_hi) * 16 + xy))
    return lax.ppermute(total, AXES, route)


def solution(mesh):
    fine = Mesh(mesh.devices.reshape(SIZES), AXES)
    placed = (
        P(FSDP, None),
        P(FSDP, HEAD, None),
        P(),
        P(FSDP, None),
        P(HEAD, FSDP, None),
        P(HEAD, FSDP, None),
        P(HEAD, FSDP, None),
        P(HEAD, FSDP, None),
    )
    return jax.shard_map(
        local, mesh=fine, in_specs=placed, out_specs=P(FSDP, HEAD), check_vma=False
    )
```

```python
import math

import jax
import jax.numpy as jnp
from jax import lax
from jax.experimental import pallas as pl
from jax.experimental.pallas import tpu as pltpu
from jax.sharding import Mesh, PartitionSpec as P

AXES = ("x", "yh", "yl", "zh", "zlh", "zll", "c")
SIZES = (4, 2, 2, 2, 4, 2, 2)
FSDP = ("x", "yh", "yl", "zh")
HEAD = ("zlh", "zll", "c")
PLANE = ("x", "yh", "yl")
COLUMN = ("zlh", "zll", "zh")
BF16 = jnp.bfloat16
F32 = jnp.float32
VMEM_LIMIT = 16 * 1024 * 1024
PACK_LIMIT = 60 * 1024 * 1024
UNPACK_FLOPS = 2 * 10**10


def swap(block, axis):
    return lax.ppermute(block, axis, [(0, 1), (1, 0)])


def ordered(ours, theirs, position, dim):
    return jnp.where(
        position == 1,
        jnp.concatenate([theirs, ours], axis=dim),
        jnp.concatenate([ours, theirs], axis=dim),
    )


def exchange(blocks, axes):
    return lax.all_to_all(blocks, axes, 0, 0, tiled=True)


def dot(a, b):
    return jnp.dot(a, b, preferred_element_type=F32)


def dot_nt(a, b):
    return lax.dot_general(a, b, (((1,), (1,)), ((), ())), preferred_element_type=F32)


def head_pairs(rope):
    return [
        jnp.concatenate([rope[:, 2 * p, :], rope[:, 2 * p + 1, :]], axis=1)
        for p in range(rope.shape[1] // 2)
    ]


def pack_kernel(
    place, cache, w_uq, w_uk, w_uv, latent, rope, out, uq, uk, uv, latent_in, rope_in, sems
):
    zh, quarter = place[0], place[2]
    lanes = out.shape[1]
    width = cache.shape[0]
    four = uq.shape[0]
    given = pl.ds((1 - zh) * four, four)
    copies = [
        (cache.at[:, pl.ds(pl.multiple_of(quarter * lanes, lanes), lanes)], out.at[pl.ds(0, width)]),
        (w_uq.at[given], uq),
        (w_uk.at[given], uk),
        (w_uv.at[given], uv),
        (latent, latent_in),
        (rope, rope_in),
    ]
    copies = [pltpu.make_async_copy(x, y, sems.at[i]) for i, (x, y) in enumerate(copies)]
    for copy in copies:
        copy.start()
    for copy in copies:
        copy.wait()
    at = width
    for h in range(four):
        for w in (uq, uk, uv):
            out[at : at + w.shape[1]] = w[h]
            at += w.shape[1]
    rows = latent_in.shape[0]
    for i in range(latent_in.shape[1] // lanes):
        out[at : at + rows] = latent_in[:, i * lanes : (i + 1) * lanes]
        at += rows
    pairs = head_pairs(rope_in)
    for p in range(len(pairs) // 2):
        out[at : at + rows] = jnp.where(zh == 0, pairs[p + len(pairs) // 2], pairs[p])
        at += rows


def spread_kernel(place, w_uq, w_uk, w_uv, w_out, out):
    zh = place[0]
    copies, lanes = out.shape[0], out.shape[2]
    four = w_uq.shape[0] // 2
    for h in range(four):
        at = h % (four // 2) * (w_uq.shape[1] + w_uk.shape[1] + w_uv.shape[1])
        for w in (w_uq, w_uk, w_uv):
            block = w[zh * four + h]
            for copy in range(h // (four // 2), copies, 2):
                out[copy, at : at + w.shape[1]] = block
            at += w.shape[1]
    rows, columns = w_out.shape[0], w_out.shape[1] // copies
    for copy in range(copies):
        to = at
        for begin in range(0, columns, lanes):
            width = min(lanes, columns - begin)
            block = w_out[:, copy * columns + begin : copy * columns + begin + width]
            if width < lanes:
                block = jnp.concatenate([block, jnp.zeros((rows, lanes - width), BF16)], axis=1)
            out[copy, to : to + rows] = block
            to += rows


def order_kernel(received, out):
    rows, columns = out.shape
    copies, lanes = received.shape[0], received.shape[2]
    each = rows // copies
    count = -(-columns // lanes)
    first = received.shape[1] - count * each
    blocks = [
        received[:, first + i * each : first + (i + 1) * each].reshape(rows, lanes)
        for i in range(count)
    ]
    weights = jnp.concatenate(blocks, axis=1)[:, :columns]
    to = lax.broadcasted_iota(jnp.int32, (rows, rows), 0)
    source = lax.broadcasted_iota(jnp.int32, (rows, rows), 1)
    y, z, j, xy, v = to // 256, to // 128 % 2, to // 64 % 2, to // 4 % 16, to % 4
    move = jnp.where(source == xy * 32 + (z * 4 + y * 2 + j) * 4 + v, 1.0, 0.0).astype(BF16)
    out[...] = dot(move, weights).astype(BF16)


def unpack_kernel(
    place, received, latent, rope, sent, packed, piece, rope_out, *, sizes
):
    n_piece, n_all, copies = sizes
    zh, yl = place[0], place[1]
    own_rows = latent.shape[0]
    lanes = packed.shape[1]
    at = n_piece
    for h in range(sent.shape[1]):
        other = received[at : at + n_all]
        for copy in range(copies):
            sent[copy, h] = other
        at += n_all
    ours = pl.ds(pl.multiple_of(zh * own_rows, 16), own_rows)
    theirs = pl.ds(pl.multiple_of((1 - zh) * own_rows, 16), own_rows)
    to = n_piece
    for i in range(latent.shape[1] // lanes):
        packed[pl.ds(pl.multiple_of(to + zh * own_rows, 16), own_rows)] = latent[
            :, i * lanes : (i + 1) * lanes
        ]
        packed[pl.ds(pl.multiple_of(to + (1 - zh) * own_rows, 16), own_rows)] = received[
            at : at + own_rows
        ]
        to += 2 * own_rows
        at += own_rows
    pairs = head_pairs(rope)
    lower = [jnp.where(zh == 0, pairs[0], pairs[2]), received[at : at + own_rows]]
    upper = [jnp.where(zh == 0, pairs[1], pairs[3]), received[at + own_rows : at + 2 * own_rows]]
    stay = [jnp.where(yl == 0, x, y) for x, y in zip(lower, upper)]
    go = [jnp.where(yl == 0, y, x) for x, y in zip(lower, upper)]
    rope_out[ours] = stay[0]
    rope_out[theirs] = stay[1]
    packed[pl.ds(pl.multiple_of(to + zh * own_rows, 16), own_rows)] = go[0]
    packed[pl.ds(pl.multiple_of(to + (1 - zh) * own_rows, 16), own_rows)] = go[1]
    packed[:n_piece] = received[:n_piece]
    piece[...] = received[:n_piece]


def attend_kernel(
    place,
    ours,
    theirs,
    weights_ours,
    weights_theirs,
    rope_ours,
    lengths,
    kv0,
    kv1,
    kv2,
    kv3,
    keep_out,
    give_out,
    query_rows,
    rope,
    scores,
    weights,
    *,
    sizes,
    temper,
):
    rows, heads, n_uq, n_uk, n_uv, width, n_starts = sizes
    caches = (kv0, kv1, kv2, kv3)
    zh, yl, starts = place[0], place[1], [place[2 + i] for i in range(n_starts)]
    n_all = n_uq + n_uk + n_uv
    for h in range(heads):
        weights[:, h, zh] = weights_ours[:, h * n_all : (h + 1) * n_all]
        weights[:, h, 1 - zh] = weights_theirs[:, h]
    per_block = kv0.shape[1]
    chunk = per_block * len(caches) // n_starts
    half = rows // 2
    mine = pl.ds(pl.multiple_of(yl * half, 16), half)
    other = pl.ds(pl.multiple_of((1 - yl) * half, 16), half)
    at = kv0.shape[0]
    lane_count = ours.shape[1]
    for i in range(query_rows.shape[1] // lane_count):
        lanes_here = slice(i * lane_count, (i + 1) * lane_count)
        query_rows[mine, lanes_here] = ours[at : at + half]
        query_rows[other, lanes_here] = theirs[at : at + half]
        at += half
    rope[mine, :] = rope_ours[...]
    rope[other, :] = theirs[at : at + half]
    query = query_rows[...]
    limit = lengths[...]
    lanes = lax.broadcasted_iota(jnp.int32, (rows, chunk), 1)
    values = []
    for h in range(heads):
        w_uq = weights[:, h, :, 0:n_uq, :].reshape(-1, weights.shape[-1])
        w_uk = weights[:, h, :, n_uq : n_uq + n_uk, :].reshape(-1, weights.shape[-1])
        q_nope = dot(query, w_uq).astype(BF16)
        q_lat = dot_nt(q_nope, w_uk).astype(BF16)
        rope_width = kv0.shape[0] - width
        q_rope = rope[:, h * rope_width : (h + 1) * rope_width]
        top = jnp.full((rows, 1), -1e30, F32)
        for b, cache in enumerate(caches):
            s = dot(q_lat, cache[:width, :]) + dot(q_rope, cache[width:, :])
            s = s * temper
            for i in range(per_block // chunk):
                k = b * (per_block // chunk) + i
                piece = s[:, i * chunk : (i + 1) * chunk]
                piece = jnp.where(lanes + starts[k] < limit, piece, -1e30)
                top = jnp.maximum(top, jnp.max(piece, axis=1, keepdims=True))
                scores[:, k * chunk : (k + 1) * chunk] = piece
        total = jnp.zeros((rows, 1), F32)
        context = jnp.zeros((rows, width), F32)
        for b, cache in enumerate(caches):
            p = jnp.exp(scores[:, b * per_block : (b + 1) * per_block] - top)
            total = total + jnp.sum(p, axis=1, keepdims=True)
            context = context + dot_nt(p.astype(BF16), cache[:width, :])
        context = (context / total).astype(BF16)
        w_uv = weights[:, h, :, n_uq + n_uk :, :].reshape(-1, weights.shape[-1])
        values.append(dot(context, w_uv).astype(BF16))
    vdim = values[0].shape[1]
    wide = heads * vdim
    to = lax.broadcasted_iota(jnp.int32, (wide, wide), 1)
    source = lax.broadcasted_iota(jnp.int32, (wide, wide), 0)
    side = to // (wide // 2)
    head = to % (wide // 2) // (vdim // 2)
    item = to % (vdim // 2)
    wanted = head * vdim + item // 4 * 8 + jnp.where(side == 0, zh, 1 - zh) * 4 + item % 4
    move = jnp.where(source == wanted, 1.0, 0.0).astype(BF16)
    moved = dot(jnp.concatenate(values, axis=1), move).astype(BF16)
    keep_out[...] = moved[:, : wide // 2]
    give_out[...] = moved[:, wide // 2 :]


def project_kernel(values, weights, out):
    total = None
    half = values.shape[3]
    for y in range(values.shape[1]):
        rows = values[:, y].reshape(-1, half)
        part = dot(rows, weights[y * half : (y + 1) * half, :])
        total = part if total is None else total + part
    out[...] = total.astype(BF16)


def local(query_latent, query_rope, lengths, kv_cache, w_uq, w_uk, w_uv, w_out):
    yl, zh, zll, core = (lax.axis_index(a) for a in ("yl", "zh", "zll", "c"))
    plane = 16
    cache = kv_cache.T
    kv_width, tokens = cache.shape
    latent_width = w_uk.shape[1] * 32
    rope_width = kv_width - latent_width
    lanes = w_uq.shape[2]
    temper = 1.0 / math.sqrt(lanes + rope_width)
    n_uq, n_uk, n_uv = w_uq.shape[1], w_uk.shape[1], w_uv.shape[1]
    n_all = n_uq + n_uk + n_uv
    own_rows = query_latent.shape[0]
    heads_in = w_uq.shape[0]
    four, heads = heads_in // 2, heads_in // 4

    quarter = tokens // 4
    place = jnp.stack([zh, yl, core * 2 + zll]).astype(jnp.int32)
    vmem = pl.BlockSpec(memory_space=pltpu.VMEM)
    smem = pl.BlockSpec(memory_space=pltpu.SMEM)
    weights = (w_uq, w_uk, w_uv)
    queries = (query_latent, query_rope)
    latent_chunks = query_latent.shape[1] // lanes
    n_sent = kv_width + four * n_all + (latent_chunks + 2) * own_rows
    packed = pl.pallas_call(
        pack_kernel,
        out_shape=jax.ShapeDtypeStruct((n_sent, lanes), BF16),
        in_specs=[smem] + [pl.BlockSpec(memory_space=pltpu.HBM)] * 6,
        out_specs=vmem,
        scratch_shapes=[pltpu.VMEM((four,) + w.shape[1:], BF16) for w in weights]
        + [pltpu.VMEM(x.shape, BF16) for x in queries]
        + [pltpu.SemaphoreType.DMA((6,))],
        compiler_params=pltpu.CompilerParams(vmem_limit_bytes=PACK_LIMIT),
        cost_estimate=pl.CostEstimate(flops=10**6, bytes_accessed=10**6, transcendentals=0),
        name="pack",
    )(place, cache, *weights, *queries)
    near = swap(cache, "yl")
    received = swap(packed, "zh")

    vpart, width = w_out.shape[1:]
    columns = width // plane
    w_rows = heads_in * vpart
    n_spread = heads * n_all + -(-columns // lanes) * w_rows
    spread = pl.pallas_call(
        spread_kernel,
        out_shape=jax.ShapeDtypeStruct((plane, n_spread, lanes), BF16),
        in_specs=[smem] + [vmem] * 4,
        out_specs=vmem,
        compiler_params=pltpu.CompilerParams(vmem_limit_bytes=VMEM_LIMIT),
        cost_estimate=pl.CostEstimate(flops=10**6, bytes_accessed=10**6, transcendentals=0),
        name="spread",
    )(place, *weights, w_out.reshape(w_rows, width))
    spread = exchange(spread, PLANE)

    n_pack = kv_width + (2 * latent_chunks + 2) * own_rows
    received, near = lax.optimization_barrier((received, near))
    sent, packed, far_piece, rope_kept = pl.pallas_call(
        lambda *refs: unpack_kernel(*refs, sizes=(kv_width, n_all, plane // 2)),
        out_shape=(
            jax.ShapeDtypeStruct((plane // 2, four, n_all, lanes), BF16),
            jax.ShapeDtypeStruct((n_pack, lanes), BF16),
            jax.ShapeDtypeStruct((kv_width, quarter), BF16),
            jax.ShapeDtypeStruct((2 * own_rows, lanes), BF16),
        ),
        in_specs=[smem] + [vmem] * 3,
        out_specs=(vmem,) * 4,
        compiler_params=pltpu.CompilerParams(vmem_limit_bytes=VMEM_LIMIT),
        cost_estimate=pl.CostEstimate(
            flops=UNPACK_FLOPS, bytes_accessed=3 * 10**6, transcendentals=0
        ),
        name="unpack",
    )(place, received, *queries)
    sent, packed, far_piece, spread = lax.optimization_barrier((sent, packed, far_piece, spread))

    weights_far = exchange(sent.reshape(plane * heads, n_all, lanes), PLANE)
    weights_far = weights_far.reshape(plane, heads, n_all, lanes)

    packed_y = swap(packed, "yl")
    piece_z = swap(far_piece, "zll")
    piece_yz = lax.ppermute(far_piece, ("yl", "zll"), [(0, 3), (1, 2), (2, 1), (3, 0)])
    far = jnp.concatenate([far_piece, packed_y[:kv_width], piece_z, piece_yz], axis=1)
    far_other = swap(far, "c")

    starts = []
    for ylo in (yl, 1 - yl):
        for i in range(4):
            starts.append((ylo * 2 + zh) * tokens + i * quarter)
    for co in (core, 1 - core):
        for zo in (zll, 1 - zll):
            for ylo in (yl, 1 - yl):
                starts.append((ylo * 2 + 1 - zh) * tokens + (co * 2 + zo) * quarter)
    place = jnp.stack([zh, yl] + starts).astype(jnp.int32)

    rows = 4 * own_rows
    sequence = lax.axis_index("x") * 2 + lax.axis_index("yh")
    row_lengths = lax.dynamic_slice_in_dim(lengths, sequence * rows, rows, 0)[:, None]
    keep, give = pl.pallas_call(
        lambda *refs: attend_kernel(
            *refs,
            sizes=(rows, heads, n_uq, n_uk, n_uv, latent_width, len(starts)),
            temper=temper,
        ),
        out_shape=(jax.ShapeDtypeStruct((rows, lanes), BF16),) * 2,
        in_specs=[smem] + [vmem] * 10,
        out_specs=(vmem,) * 2,
        scratch_shapes=[
            pltpu.VMEM((rows, query_latent.shape[1]), BF16),
            pltpu.VMEM((rows, lanes), BF16),
            pltpu.VMEM((rows, 4 * tokens), F32),
            pltpu.VMEM((plane, heads, 2, n_all, lanes), BF16),
        ],
        compiler_params=pltpu.CompilerParams(vmem_limit_bytes=VMEM_LIMIT),
        cost_estimate=pl.CostEstimate(flops=10**9, bytes_accessed=5 * 10**6, transcendentals=0),
        name="attend",
    )(place, packed, packed_y, spread, weights_far, rope_kept, row_lengths, cache, near, far, far_other)

    values = ordered(keep, swap(give, "zh"), zh, 1)
    gathered = exchange(
        jnp.broadcast_to(values[None], (plane,) + values.shape).reshape(-1, values.shape[1]), PLANE
    ).reshape(plane // 2, 2, rows, heads * lanes)
    out_proj = pl.pallas_call(
        order_kernel,
        out_shape=jax.ShapeDtypeStruct((plane * w_rows, columns), BF16),
        in_specs=[vmem],
        out_specs=vmem,
        compiler_params=pltpu.CompilerParams(vmem_limit_bytes=VMEM_LIMIT),
        cost_estimate=pl.CostEstimate(flops=2 * 10**8, bytes_accessed=2 * 10**6, transcendentals=0),
        name="order",
    )(spread)
    all_rows = plane // 2 * rows
    partial_out = pl.pallas_call(
        project_kernel,
        out_shape=jax.ShapeDtypeStruct((all_rows, columns), BF16),
        in_specs=[vmem, vmem],
        out_specs=vmem,
        compiler_params=pltpu.CompilerParams(vmem_limit_bytes=VMEM_LIMIT),
        cost_estimate=pl.CostEstimate(flops=2 * 10**8, bytes_accessed=2 * 10**6, transcendentals=0),
        name="project",
    )(gathered, out_proj)

    total = exchange(partial_out, "c").reshape(2, all_rows // 2, columns)
    total = jnp.sum(total.astype(F32), axis=0).astype(BF16)
    total = exchange(total, COLUMN).reshape(16, all_rows // 32, columns)
    total = jnp.sum(total.astype(F32), axis=0).astype(BF16)
    route = []
    for xy in range(16):
        for z_hi in range(2):
            for z_lo in range(8):
                for c in range(2):
                    source = ((xy * 2 + z_hi) * 8 + z_lo) * 2 + c
                    route.append((source, (c * 16 + z_lo * 2 + z_hi) * 16 + xy))
    return lax.ppermute(total, AXES, route)


def solution(mesh):
    fine = Mesh(mesh.devices.reshape(SIZES), AXES)
    placed = (
        P(FSDP, None),
        P(FSDP, HEAD, None),
        P(),
        P(FSDP, None),
        P(HEAD, FSDP, None),
        P(HEAD, FSDP, None),
        P(HEAD, FSDP, None),
        P(HEAD, FSDP, None),
    )
    return jax.shard_map(
        local, mesh=fine, in_specs=placed, out_specs=P(FSDP, HEAD), check_vma=False
    )
```

```python
import math

import jax
import jax.numpy as jnp
from jax import lax
from jax.experimental import pallas as pl
from jax.experimental.pallas import tpu as pltpu
from jax.sharding import Mesh, PartitionSpec as P

AXES = ("x", "yh", "yl", "zh", "zlh", "zll", "c")
SIZES = (4, 2, 2, 2, 4, 2, 2)
FSDP = ("x", "yh", "yl", "zh")
HEAD = ("zlh", "zll", "c")
PLANE = ("x", "yh", "yl")
COLUMN = ("zh", "zlh", "zll")
BF16 = jnp.bfloat16
F32 = jnp.float32
VMEM_LIMIT = 16 * 1024 * 1024
PACK_LIMIT = 60 * 1024 * 1024
UNPACK_FLOPS = 2 * 10**10


def swap(block, axis):
    return lax.ppermute(block, axis, [(0, 1), (1, 0)])


def ordered(ours, theirs, position, dim):
    return jnp.where(
        position == 1,
        jnp.concatenate([theirs, ours], axis=dim),
        jnp.concatenate([ours, theirs], axis=dim),
    )


def exchange(blocks, axes):
    return lax.all_to_all(blocks, axes, 0, 0, tiled=True)


def dot(a, b):
    return jnp.dot(a, b, preferred_element_type=F32)


def dot_nt(a, b):
    return lax.dot_general(a, b, (((1,), (1,)), ((), ())), preferred_element_type=F32)


def head_pairs(rope):
    return [
        jnp.concatenate([rope[:, 2 * p, :], rope[:, 2 * p + 1, :]], axis=1)
        for p in range(rope.shape[1] // 2)
    ]


def pack_kernel(
    place, cache, w_uq, w_uk, w_uv, latent, rope, out, uq, uk, uv, latent_in, rope_in, sems
):
    zh, quarter = place[0], place[2]
    lanes = out.shape[1]
    width = cache.shape[0]
    four = uq.shape[0]
    given = pl.ds((1 - zh) * four, four)
    copies = [
        (cache.at[:, pl.ds(pl.multiple_of(quarter * lanes, lanes), lanes)], out.at[pl.ds(0, width)]),
        (w_uq.at[given], uq),
        (w_uk.at[given], uk),
        (w_uv.at[given], uv),
        (latent, latent_in),
        (rope, rope_in),
    ]
    copies = [pltpu.make_async_copy(x, y, sems.at[i]) for i, (x, y) in enumerate(copies)]
    for copy in copies:
        copy.start()
    for copy in copies:
        copy.wait()
    at = width
    for h in range(four):
        for w in (uq, uk, uv):
            out[at : at + w.shape[1]] = w[h]
            at += w.shape[1]
    rows = latent_in.shape[0]
    for i in range(latent_in.shape[1] // lanes):
        out[at : at + rows] = latent_in[:, i * lanes : (i + 1) * lanes]
        at += rows
    pairs = head_pairs(rope_in)
    for p in range(len(pairs) // 2):
        out[at : at + rows] = jnp.where(zh == 0, pairs[p + len(pairs) // 2], pairs[p])
        at += rows


def spread_kernel(place, w_uq, w_uk, w_uv, w_out, out):
    zh = place[0]
    copies, lanes = out.shape[0], out.shape[2]
    four = w_uq.shape[0] // 2
    for h in range(four):
        at = h % (four // 2) * (w_uq.shape[1] + w_uk.shape[1] + w_uv.shape[1])
        for w in (w_uq, w_uk, w_uv):
            block = w[zh * four + h]
            for copy in range(h // (four // 2), copies, 2):
                out[copy, at : at + w.shape[1]] = block
            at += w.shape[1]
    rows, columns = w_out.shape[0], w_out.shape[1] // copies
    for copy in range(copies):
        to = at
        for begin in range(0, columns, lanes):
            width = min(lanes, columns - begin)
            block = w_out[:, copy * columns + begin : copy * columns + begin + width]
            if width < lanes:
                block = jnp.concatenate([block, jnp.zeros((rows, lanes - width), BF16)], axis=1)
            out[copy, to : to + rows] = block
            to += rows


def order_kernel(received, out):
    rows, columns = out.shape
    copies, lanes = received.shape[0], received.shape[2]
    each = rows // copies
    count = -(-columns // lanes)
    first = received.shape[1] - count * each
    blocks = [
        received[:, first + i * each : first + (i + 1) * each].reshape(rows, lanes)
        for i in range(count)
    ]
    weights = jnp.concatenate(blocks, axis=1)[:, :columns]
    to = lax.broadcasted_iota(jnp.int32, (rows, rows), 0)
    source = lax.broadcasted_iota(jnp.int32, (rows, rows), 1)
    y, z, j, xy, v = to // 256, to // 128 % 2, to // 64 % 2, to // 4 % 16, to % 4
    move = jnp.where(source == xy * 32 + (z * 4 + y * 2 + j) * 4 + v, 1.0, 0.0).astype(BF16)
    out[...] = dot(move, weights).astype(BF16)


def unpack_kernel(
    place, received, latent, rope, sent, packed, piece, rope_out, *, sizes
):
    n_piece, n_all, copies = sizes
    zh, yl = place[0], place[1]
    own_rows = latent.shape[0]
    lanes = packed.shape[1]
    at = n_piece
    for h in range(sent.shape[1]):
        other = received[at : at + n_all]
        for copy in range(copies):
            sent[copy, h] = other
        at += n_all
    ours = pl.ds(pl.multiple_of(zh * own_rows, 16), own_rows)
    theirs = pl.ds(pl.multiple_of((1 - zh) * own_rows, 16), own_rows)
    to = n_piece
    for i in range(latent.shape[1] // lanes):
        packed[pl.ds(pl.multiple_of(to + zh * own_rows, 16), own_rows)] = latent[
            :, i * lanes : (i + 1) * lanes
        ]
        packed[pl.ds(pl.multiple_of(to + (1 - zh) * own_rows, 16), own_rows)] = received[
            at : at + own_rows
        ]
        to += 2 * own_rows
        at += own_rows
    pairs = head_pairs(rope)
    lower = [jnp.where(zh == 0, pairs[0], pairs[2]), received[at : at + own_rows]]
    upper = [jnp.where(zh == 0, pairs[1], pairs[3]), received[at + own_rows : at + 2 * own_rows]]
    stay = [jnp.where(yl == 0, x, y) for x, y in zip(lower, upper)]
    go = [jnp.where(yl == 0, y, x) for x, y in zip(lower, upper)]
    rope_out[ours] = stay[0]
    rope_out[theirs] = stay[1]
    packed[pl.ds(pl.multiple_of(to + zh * own_rows, 16), own_rows)] = go[0]
    packed[pl.ds(pl.multiple_of(to + (1 - zh) * own_rows, 16), own_rows)] = go[1]
    packed[:n_piece] = received[:n_piece]
    piece[...] = received[:n_piece]


def attend_kernel(
    place,
    ours,
    theirs,
    weights_ours,
    weights_theirs,
    rope_ours,
    lengths,
    kv0,
    kv1,
    kv2,
    kv3,
    keep_out,
    give_out,
    query_rows,
    rope,
    scores,
    weights,
    *,
    sizes,
    temper,
):
    rows, heads, n_uq, n_uk, n_uv, width = sizes
    caches = (kv0, kv1, kv2, kv3)
    zh, yl, core = place[0], place[1], place[3]
    zll = place[2] - core * 2
    quarter = kv0.shape[1] // 4
    starts = []
    for ylo in (yl, 1 - yl):
        for i in range(4):
            starts.append((ylo * 2 + zh) * kv0.shape[1] + i * quarter)
    for co in (core, 1 - core):
        for zo in (zll, 1 - zll):
            for ylo in (yl, 1 - yl):
                starts.append((ylo * 2 + 1 - zh) * kv0.shape[1] + (co * 2 + zo) * quarter)
    n_all = n_uq + n_uk + n_uv
    for h in range(heads):
        weights[:, h, zh] = weights_ours[:, h * n_all : (h + 1) * n_all]
        weights[:, h, 1 - zh] = weights_theirs[:, h]
    per_block = kv0.shape[1]
    chunk = quarter
    half = rows // 2
    mine = pl.ds(pl.multiple_of(yl * half, 16), half)
    other = pl.ds(pl.multiple_of((1 - yl) * half, 16), half)
    at = kv0.shape[0]
    lane_count = ours.shape[1]
    for i in range(query_rows.shape[1] // lane_count):
        lanes_here = slice(i * lane_count, (i + 1) * lane_count)
        query_rows[mine, lanes_here] = ours[at : at + half]
        query_rows[other, lanes_here] = theirs[at : at + half]
        at += half
    rope[mine, :] = rope_ours[...]
    rope[other, :] = theirs[at : at + half]
    query = query_rows[...]
    diagonal = lax.broadcasted_iota(jnp.int32, (rows, rows), 0) == lax.broadcasted_iota(
        jnp.int32, (rows, rows), 1
    )
    limit = jnp.sum(
        jnp.where(diagonal, lengths[pl.ds(place[4], 1), :], 0), axis=1, keepdims=True
    )
    limit = jnp.concatenate([limit] * heads, axis=0)
    all_rows = heads * rows
    lanes = lax.broadcasted_iota(jnp.int32, (all_rows, chunk), 1)
    rope_width = kv0.shape[0] - width
    q_lat = []
    for h in range(heads):
        w_uq = weights[:, h, :, 0:n_uq, :].reshape(-1, weights.shape[-1])
        w_uk = weights[:, h, :, n_uq : n_uq + n_uk, :].reshape(-1, weights.shape[-1])
        q_nope = dot(query, w_uq).astype(BF16)
        q_lat.append(dot_nt(q_nope, w_uk).astype(BF16))
    q_lat = jnp.concatenate(q_lat, axis=0)
    q_rope = jnp.concatenate(
        [rope[:, h * rope_width : (h + 1) * rope_width] for h in range(heads)], axis=0
    )
    top = jnp.full((all_rows, 1), -1e30, F32)
    for b, cache in enumerate(caches):
        s = dot(q_lat, cache[:width, :]) + dot(q_rope, cache[width:, :])
        s = s * temper
        for i in range(per_block // chunk):
            k = b * (per_block // chunk) + i
            piece = s[:, i * chunk : (i + 1) * chunk]
            piece = jnp.where(lanes + starts[k] < limit, piece, -1e30)
            top = jnp.maximum(top, jnp.max(piece, axis=1, keepdims=True))
            scores[:, k * chunk : (k + 1) * chunk] = piece
    total = jnp.zeros((all_rows, 1), F32)
    context = jnp.zeros((all_rows, width), F32)
    for b, cache in enumerate(caches):
        p = jnp.exp(scores[:, b * per_block : (b + 1) * per_block] - top)
        total = total + jnp.sum(p, axis=1, keepdims=True)
        context = context + dot_nt(p.astype(BF16), cache[:width, :])
    context = (context / total).astype(BF16)
    values = []
    for h in range(heads):
        w_uv = weights[:, h, :, n_uq + n_uk :, :].reshape(-1, weights.shape[-1])
        values.append(dot(context[h * rows : (h + 1) * rows], w_uv).astype(BF16))
    vdim = values[0].shape[1]
    wide = heads * vdim
    to = lax.broadcasted_iota(jnp.int32, (wide, wide), 1)
    source = lax.broadcasted_iota(jnp.int32, (wide, wide), 0)
    side = to // (wide // 2)
    head = to % (wide // 2) // (vdim // 2)
    item = to % (vdim // 2)
    wanted = head * vdim + item // 4 * 8 + jnp.where(side == 0, zh, 1 - zh) * 4 + item % 4
    move = jnp.where(source == wanted, 1.0, 0.0).astype(BF16)
    moved = dot(jnp.concatenate(values, axis=1), move).astype(BF16)
    keep_out[...] = moved[:, : wide // 2]
    give_out[...] = moved[:, wide // 2 :]


def project_kernel(place, values, weights, keep_out, give_out, total):
    core = place[3]
    half = values.shape[3]
    for y in range(values.shape[1]):
        rows = values[:, y].reshape(-1, half)
        part = dot(rows, weights[y * half : (y + 1) * half, :])
        if y == 0:
            total[...] = part
        else:
            total[...] += part
    high, low, rows, columns = keep_out.shape
    for c, out in ((core, keep_out), (1 - core, give_out)):
        mine = total[pl.ds(pl.multiple_of(c * high * low * rows, rows), high * low * rows)]
        mine = mine.astype(BF16).reshape(low, high, rows, columns)
        for z in range(high):
            out[z] = mine[:, z]


def local(query_latent, query_rope, lengths, kv_cache, w_uq, w_uk, w_uv, w_out):
    yl, zh, zll, core = (lax.axis_index(a) for a in ("yl", "zh", "zll", "c"))
    plane = 16
    cache = kv_cache.T
    kv_width, tokens = cache.shape
    latent_width = w_uk.shape[1] * 32
    rope_width = kv_width - latent_width
    lanes = w_uq.shape[2]
    temper = 1.0 / math.sqrt(lanes + rope_width)
    n_uq, n_uk, n_uv = w_uq.shape[1], w_uk.shape[1], w_uv.shape[1]
    n_all = n_uq + n_uk + n_uv
    own_rows = query_latent.shape[0]
    heads_in = w_uq.shape[0]
    four, heads = heads_in // 2, heads_in // 4

    quarter = tokens // 4
    sequence = lax.axis_index("x") * 2 + lax.axis_index("yh")
    place = jnp.stack([zh, yl, core * 2 + zll, core, sequence]).astype(jnp.int32)
    vmem = pl.BlockSpec(memory_space=pltpu.VMEM)
    smem = pl.BlockSpec(memory_space=pltpu.SMEM)
    weights = (w_uq, w_uk, w_uv)
    queries = (query_latent, query_rope)
    latent_chunks = query_latent.shape[1] // lanes
    n_sent = kv_width + four * n_all + (latent_chunks + 2) * own_rows
    packed = pl.pallas_call(
        pack_kernel,
        out_shape=jax.ShapeDtypeStruct((n_sent, lanes), BF16),
        in_specs=[smem] + [pl.BlockSpec(memory_space=pltpu.HBM)] * 6,
        out_specs=vmem,
        scratch_shapes=[pltpu.VMEM((four,) + w.shape[1:], BF16) for w in weights]
        + [pltpu.VMEM(x.shape, BF16) for x in queries]
        + [pltpu.SemaphoreType.DMA((6,))],
        compiler_params=pltpu.CompilerParams(vmem_limit_bytes=PACK_LIMIT),
        cost_estimate=pl.CostEstimate(flops=10**6, bytes_accessed=10**6, transcendentals=0),
        name="pack",
    )(place, cache, *weights, *queries)
    near = swap(cache, "yl")
    received = swap(packed, "zh")

    vpart, width = w_out.shape[1:]
    columns = width // plane
    w_rows = heads_in * vpart
    n_spread = heads * n_all + -(-columns // lanes) * w_rows
    spread = pl.pallas_call(
        spread_kernel,
        out_shape=jax.ShapeDtypeStruct((plane, n_spread, lanes), BF16),
        in_specs=[smem] + [vmem] * 4,
        out_specs=vmem,
        compiler_params=pltpu.CompilerParams(vmem_limit_bytes=VMEM_LIMIT),
        cost_estimate=pl.CostEstimate(flops=10**6, bytes_accessed=10**6, transcendentals=0),
        name="spread",
    )(place, *weights, w_out.reshape(w_rows, width))
    spread = exchange(spread, PLANE)

    n_pack = kv_width + (2 * latent_chunks + 2) * own_rows
    sent, packed, far_piece, rope_kept = pl.pallas_call(
        lambda *refs: unpack_kernel(*refs, sizes=(kv_width, n_all, plane // 2)),
        out_shape=(
            jax.ShapeDtypeStruct((plane // 2, four, n_all, lanes), BF16),
            jax.ShapeDtypeStruct((n_pack, lanes), BF16),
            jax.ShapeDtypeStruct((kv_width, quarter), BF16),
            jax.ShapeDtypeStruct((2 * own_rows, lanes), BF16),
        ),
        in_specs=[smem] + [vmem] * 3,
        out_specs=(vmem,) * 4,
        compiler_params=pltpu.CompilerParams(vmem_limit_bytes=VMEM_LIMIT),
        cost_estimate=pl.CostEstimate(
            flops=UNPACK_FLOPS, bytes_accessed=3 * 10**6, transcendentals=0
        ),
        name="unpack",
    )(place, received, *queries)
    rows = 4 * own_rows
    row_lengths = lengths.reshape(-1, rows)
    sent, packed, far_piece, spread, near, row_lengths = lax.optimization_barrier(
        (sent, packed, far_piece, spread, near, row_lengths)
    )

    weights_far = exchange(sent.reshape(plane * heads, n_all, lanes), PLANE)
    weights_far = weights_far.reshape(plane, heads, n_all, lanes)

    packed_y = swap(packed, "yl")
    piece_z = swap(far_piece, "zll")
    piece_yz = lax.ppermute(far_piece, ("yl", "zll"), [(0, 3), (1, 2), (2, 1), (3, 0)])
    far = jnp.concatenate([far_piece, packed_y[:kv_width], piece_z, piece_yz], axis=1)
    far_other = swap(far, "c")

    keep, give = pl.pallas_call(
        lambda *refs: attend_kernel(
            *refs,
            sizes=(rows, heads, n_uq, n_uk, n_uv, latent_width),
            temper=temper,
        ),
        out_shape=(jax.ShapeDtypeStruct((rows, lanes), BF16),) * 2,
        in_specs=[smem] + [vmem] * 10,
        out_specs=(vmem,) * 2,
        scratch_shapes=[
            pltpu.VMEM((rows, query_latent.shape[1]), BF16),
            pltpu.VMEM((rows, lanes), BF16),
            pltpu.VMEM((heads * rows, 4 * tokens), F32),
            pltpu.VMEM((plane, heads, 2, n_all, lanes), BF16),
        ],
        compiler_params=pltpu.CompilerParams(vmem_limit_bytes=VMEM_LIMIT),
        cost_estimate=pl.CostEstimate(flops=10**9, bytes_accessed=5 * 10**6, transcendentals=0),
        name="attend",
    )(place, packed, packed_y, spread, weights_far, rope_kept, row_lengths, cache, near, far, far_other)

    values = ordered(keep, swap(give, "zh"), zh, 1)
    gathered = exchange(
        jnp.broadcast_to(values[None], (plane,) + values.shape).reshape(-1, values.shape[1]), PLANE
    ).reshape(plane // 2, 2, rows, heads * lanes)
    out_proj = pl.pallas_call(
        order_kernel,
        out_shape=jax.ShapeDtypeStruct((plane * w_rows, columns), BF16),
        in_specs=[vmem],
        out_specs=vmem,
        compiler_params=pltpu.CompilerParams(vmem_limit_bytes=VMEM_LIMIT),
        cost_estimate=pl.CostEstimate(flops=2 * 10**8, bytes_accessed=2 * 10**6, transcendentals=0),
        name="order",
    )(spread)
    all_rows = plane // 2 * rows
    keep, give = pl.pallas_call(
        project_kernel,
        out_shape=(jax.ShapeDtypeStruct((2, 8, all_rows // 32, columns), BF16),) * 2,
        in_specs=[smem] + [vmem] * 2,
        out_specs=(vmem,) * 2,
        scratch_shapes=[pltpu.VMEM((all_rows, columns), F32)],
        compiler_params=pltpu.CompilerParams(vmem_limit_bytes=VMEM_LIMIT),
        cost_estimate=pl.CostEstimate(flops=2 * 10**8, bytes_accessed=2 * 10**6, transcendentals=0),
        name="project",
    )(place, gathered, out_proj)

    total = (keep.astype(F32) + swap(give, "c").astype(F32)).astype(BF16)
    total = exchange(total.reshape((16,) + total.shape[2:]), COLUMN)
    total = jnp.sum(total.astype(F32), axis=0).astype(BF16)
    route = []
    for xy in range(16):
        for z_hi in range(2):
            for z_lo in range(8):
                for c in range(2):
                    source = ((xy * 2 + z_hi) * 8 + z_lo) * 2 + c
                    route.append((source, (c * 16 + z_lo * 2 + z_hi) * 16 + xy))
    return lax.ppermute(total, AXES, route)


def solution(mesh):
    fine = Mesh(mesh.devices.reshape(SIZES), AXES)
    placed = (
        P(FSDP, None),
        P(FSDP, HEAD, None),
        P(),
        P(FSDP, None),
        P(HEAD, FSDP, None),
        P(HEAD, FSDP, None),
        P(HEAD, FSDP, None),
        P(HEAD, FSDP, None),
    )
    return jax.shard_map(
        local, mesh=fine, in_specs=placed, out_specs=P(FSDP, HEAD), check_vma=False
    )
```

```python
import math

import jax
import jax.numpy as jnp
import numpy as np
from jax import lax
from jax.experimental import pallas as pl
from jax.experimental.pallas import tpu as pltpu
from jax.sharding import Mesh, PartitionSpec as P

AXES = ("x", "yh", "yl", "zh", "zlh", "zll", "c")
SIZES = (4, 2, 2, 2, 4, 2, 2)
FSDP = ("x", "yh", "yl", "zh")
HEAD = ("zlh", "zll", "c")
PLANE = ("x", "yh", "yl")
RING = ("yh", "yl")
COLUMN = ("zh", "zlh", "zll")
BF16 = jnp.bfloat16
F32 = jnp.float32
VMEM_LIMIT = 16 * 1024 * 1024
PACK_LIMIT = 60 * 1024 * 1024
UNPACK_FLOPS = 2 * 10**10


def swap(block, axis):
    return lax.ppermute(block, axis, [(0, 1), (1, 0)])


def ordered(ours, theirs, position, dim):
    return jnp.where(
        position == 1,
        jnp.concatenate([theirs, ours], axis=dim),
        jnp.concatenate([ours, theirs], axis=dim),
    )


def exchange(blocks, axes):
    return lax.all_to_all(blocks, axes, 0, 0, tiled=True)


def dot(a, b):
    return jnp.dot(a, b, preferred_element_type=F32)


def dot_nt(a, b):
    return lax.dot_general(a, b, (((1,), (1,)), ((), ())), preferred_element_type=F32)


def head_pairs(rope):
    return [
        jnp.concatenate([rope[:, 2 * p, :], rope[:, 2 * p + 1, :]], axis=1)
        for p in range(rope.shape[1] // 2)
    ]


def pack_kernel(
    place, cache, w_uq, w_uk, w_uv, latent, rope, out, uq, uk, uv, latent_in, rope_in, sems
):
    zh, quarter = place[0], place[2]
    lanes = out.shape[1]
    width = cache.shape[0]
    four = uq.shape[0]
    given = pl.ds((1 - zh) * four, four)
    copies = [
        (cache.at[:, pl.ds(pl.multiple_of(quarter * lanes, lanes), lanes)], out.at[pl.ds(0, width)]),
        (w_uq.at[given], uq),
        (w_uk.at[given], uk),
        (w_uv.at[given], uv),
        (latent, latent_in),
        (rope, rope_in),
    ]
    copies = [pltpu.make_async_copy(x, y, sems.at[i]) for i, (x, y) in enumerate(copies)]
    for copy in copies:
        copy.start()
    for copy in copies:
        copy.wait()
    at = width
    for h in range(four):
        for w in (uq, uk, uv):
            out[at : at + w.shape[1]] = w[h]
            at += w.shape[1]
    rows = latent_in.shape[0]
    for i in range(latent_in.shape[1] // lanes):
        out[at : at + rows] = latent_in[:, i * lanes : (i + 1) * lanes]
        at += rows
    pairs = head_pairs(rope_in)
    for p in range(len(pairs) // 2):
        out[at : at + rows] = jnp.where(zh == 0, pairs[p + len(pairs) // 2], pairs[p])
        at += rows


def spread_kernel(place, w_uq, w_uk, w_uv, w_out, out):
    zh = place[0]
    copies, lanes = out.shape[0], out.shape[2]
    four = w_uq.shape[0] // 2
    for h in range(four):
        at = h % (four // 2) * (w_uq.shape[1] + w_uk.shape[1] + w_uv.shape[1])
        for w in (w_uq, w_uk, w_uv):
            block = w[zh * four + h]
            for copy in range(h // (four // 2), copies, 2):
                out[copy, at : at + w.shape[1]] = block
            at += w.shape[1]
    rows, columns = w_out.shape[0], (out.shape[1] - at) // w_out.shape[0] * lanes
    parts = w_out.shape[1] // columns
    for copy in range(copies):
        begin = copy % parts * columns
        for i in range(columns // lanes):
            block = w_out[:, begin + i * lanes : begin + (i + 1) * lanes]
            out[copy, at + i * rows : at + (i + 1) * rows] = block


def repeat_kernel(received, sent, *, first):
    copies, heads, rows = sent.shape[:3]
    for h in range(heads):
        block = received[first + h * rows : first + (h + 1) * rows]
        for copy in range(copies):
            sent[copy, h] = block


def unpack_kernel(place, received, latent, rope, packed, piece, rope_out, *, sizes):
    n_piece, at = sizes
    zh, yl = place[0], place[1]
    own_rows = latent.shape[0]
    lanes = packed.shape[1]
    ours = pl.ds(pl.multiple_of(zh * own_rows, 16), own_rows)
    theirs = pl.ds(pl.multiple_of((1 - zh) * own_rows, 16), own_rows)
    to = n_piece
    for i in range(latent.shape[1] // lanes):
        packed[pl.ds(pl.multiple_of(to + zh * own_rows, 16), own_rows)] = latent[
            :, i * lanes : (i + 1) * lanes
        ]
        packed[pl.ds(pl.multiple_of(to + (1 - zh) * own_rows, 16), own_rows)] = received[
            at : at + own_rows
        ]
        to += 2 * own_rows
        at += own_rows
    pairs = head_pairs(rope)
    lower = [jnp.where(zh == 0, pairs[0], pairs[2]), received[at : at + own_rows]]
    upper = [jnp.where(zh == 0, pairs[1], pairs[3]), received[at + own_rows : at + 2 * own_rows]]
    stay = [jnp.where(yl == 0, x, y) for x, y in zip(lower, upper)]
    go = [jnp.where(yl == 0, y, x) for x, y in zip(lower, upper)]
    rope_out[ours] = stay[0]
    rope_out[theirs] = stay[1]
    packed[pl.ds(pl.multiple_of(to + zh * own_rows, 16), own_rows)] = go[0]
    packed[pl.ds(pl.multiple_of(to + (1 - zh) * own_rows, 16), own_rows)] = go[1]
    packed[:n_piece] = received[:n_piece]
    piece[...] = received[:n_piece]


def attend_kernel(
    place,
    ours,
    theirs,
    weights_ours,
    weights_theirs,
    rope_ours,
    lengths,
    kv0,
    kv1,
    kv2,
    kv3,
    keep_out,
    give_out,
    query_rows,
    rope,
    scores,
    weights,
    *,
    sizes,
    temper,
):
    rows, heads, n_uq, n_uk, n_uv, width = sizes
    caches = (kv0, kv1, kv2, kv3)
    zh, yl, core = place[0], place[1], place[3]
    zll = place[2] - core * 2
    quarter = kv0.shape[1] // 4
    starts = []
    for ylo in (yl, 1 - yl):
        for i in range(4):
            starts.append((ylo * 2 + zh) * kv0.shape[1] + i * quarter)
    for co in (core, 1 - core):
        for zo in (zll, 1 - zll):
            for ylo in (yl, 1 - yl):
                starts.append((ylo * 2 + 1 - zh) * kv0.shape[1] + (co * 2 + zo) * quarter)
    n_all = n_uq + n_uk + n_uv
    for h in range(heads):
        weights[:, h, zh] = weights_ours[:, h * n_all : (h + 1) * n_all]
        weights[:, h, 1 - zh] = weights_theirs[:, h]
    per_block = kv0.shape[1]
    chunk = quarter
    half = rows // 2
    mine = pl.ds(pl.multiple_of(yl * half, 16), half)
    other = pl.ds(pl.multiple_of((1 - yl) * half, 16), half)
    at = kv0.shape[0]
    lane_count = ours.shape[1]
    for i in range(query_rows.shape[1] // lane_count):
        lanes_here = slice(i * lane_count, (i + 1) * lane_count)
        query_rows[mine, lanes_here] = ours[at : at + half]
        query_rows[other, lanes_here] = theirs[at : at + half]
        at += half
    rope[mine, :] = rope_ours[...]
    rope[other, :] = theirs[at : at + half]
    query = query_rows[...]
    diagonal = lax.broadcasted_iota(jnp.int32, (rows, rows), 0) == lax.broadcasted_iota(
        jnp.int32, (rows, rows), 1
    )
    limit = jnp.sum(
        jnp.where(diagonal, lengths[pl.ds(place[4], 1), :], 0), axis=1, keepdims=True
    )
    limit = jnp.concatenate([limit] * heads, axis=0)
    all_rows = heads * rows
    lanes = lax.broadcasted_iota(jnp.int32, (all_rows, chunk), 1)
    rope_width = kv0.shape[0] - width
    q_lat = []
    for h in range(heads):
        w_uq = weights[:, h, :, 0:n_uq, :].reshape(-1, weights.shape[-1])
        w_uk = weights[:, h, :, n_uq : n_uq + n_uk, :].reshape(-1, weights.shape[-1])
        q_nope = dot(query, w_uq).astype(BF16)
        q_lat.append(dot_nt(q_nope, w_uk).astype(BF16))
    q_lat = jnp.concatenate(q_lat, axis=0)
    q_rope = jnp.concatenate(
        [rope[:, h * rope_width : (h + 1) * rope_width] for h in range(heads)], axis=0
    )
    top = jnp.full((all_rows, 1), -1e30, F32)
    for b, cache in enumerate(caches):
        s = dot(q_lat, cache[:width, :]) + dot(q_rope, cache[width:, :])
        s = s * temper
        for i in range(per_block // chunk):
            k = b * (per_block // chunk) + i
            piece = s[:, i * chunk : (i + 1) * chunk]
            piece = jnp.where(lanes + starts[k] < limit, piece, -1e30)
            top = jnp.maximum(top, jnp.max(piece, axis=1, keepdims=True))
            scores[:, k * chunk : (k + 1) * chunk] = piece
    total = jnp.zeros((all_rows, 1), F32)
    context = jnp.zeros((all_rows, width), F32)
    for b, cache in enumerate(caches):
        p = jnp.exp(scores[:, b * per_block : (b + 1) * per_block] - top)
        total = total + jnp.sum(p, axis=1, keepdims=True)
        context = context + dot_nt(p.astype(BF16), cache[:width, :])
    context = (context / total).astype(BF16)
    values = []
    for h in range(heads):
        w_uv = weights[:, h, :, n_uq + n_uk :, :].reshape(-1, weights.shape[-1])
        values.append(dot(context[h * rows : (h + 1) * rows], w_uv).astype(BF16))
    vdim = values[0].shape[1]
    wide = heads * vdim
    to = lax.broadcasted_iota(jnp.int32, (wide, wide), 1)
    source = lax.broadcasted_iota(jnp.int32, (wide, wide), 0)
    side = to // (wide // 2)
    head = to % (wide // 2) // (vdim // 2)
    item = to % (vdim // 2)
    wanted = head * vdim + item // 4 * 8 + jnp.where(side == 0, zh, 1 - zh) * 4 + item % 4
    move = jnp.where(source == wanted, 1.0, 0.0).astype(BF16)
    moved = dot(jnp.concatenate(values, axis=1), move).astype(BF16)
    keep_out[...] = moved[:, : wide // 2]
    give_out[...] = moved[:, wide // 2 :]


def feature_order(heads, plane, items):
    count = 4 * heads * plane * items
    to = np.arange(count).reshape(plane, 2, 2, heads, items).transpose(2, 1, 3, 0, 4).reshape(-1)
    return np.equal(to[:, None], np.arange(count)[None, :]).astype(np.float32)


def project_kernel(place, values, received, order, keep_out, give_out):
    core = place[3]
    lanes = received.shape[2]
    rows = [jnp.concatenate([values[2 * i], values[2 * i + 1]], axis=1) for i in range(2)]
    rows = dot(jnp.concatenate(rows, axis=0), order[...]).astype(BF16)
    depth = rows.shape[1]
    each = depth // received.shape[0]
    blocks, _, low, _, columns = keep_out.shape
    count = 2 * columns // lanes
    first = received.shape[1] - low * count * each
    for z in range(low):
        weights = jnp.concatenate(
            [
                received[:, at : at + each].reshape(depth, lanes)
                for at in range(first + z * count * each, first + (z + 1) * count * each, each)
            ],
            axis=1,
        )
        part = dot(rows, weights)
        even, odd = part[:, :columns], part[:, columns:]
        shape = keep_out.shape[:2] + keep_out.shape[3:]
        keep_out[:, :, z] = jnp.where(core == 0, even, odd).astype(BF16).reshape(shape)
        give_out[:, :, z] = jnp.where(core == 0, odd, even).astype(BF16).reshape(shape)


def local(query_latent, query_rope, lengths, kv_cache, w_uq, w_uk, w_uv, w_out):
    yl, zh, zll, core = (lax.axis_index(a) for a in ("yl", "zh", "zll", "c"))
    plane = 16
    cache = kv_cache.T
    kv_width, tokens = cache.shape
    latent_width = w_uk.shape[1] * 32
    rope_width = kv_width - latent_width
    lanes = w_uq.shape[2]
    temper = 1.0 / math.sqrt(lanes + rope_width)
    n_uq, n_uk, n_uv = w_uq.shape[1], w_uk.shape[1], w_uv.shape[1]
    n_all = n_uq + n_uk + n_uv
    own_rows = query_latent.shape[0]
    heads_in = w_uq.shape[0]
    four, heads = heads_in // 2, heads_in // 4

    quarter = tokens // 4
    sequence = lax.axis_index("x") * 2 + lax.axis_index("yh")
    place = jnp.stack([zh, yl, core * 2 + zll, core, sequence]).astype(jnp.int32)
    vmem = pl.BlockSpec(memory_space=pltpu.VMEM)
    smem = pl.BlockSpec(memory_space=pltpu.SMEM)
    weights = (w_uq, w_uk, w_uv)
    queries = (query_latent, query_rope)
    latent_chunks = query_latent.shape[1] // lanes
    n_sent = kv_width + four * n_all + (latent_chunks + 2) * own_rows
    packed = pl.pallas_call(
        pack_kernel,
        out_shape=jax.ShapeDtypeStruct((n_sent, lanes), BF16),
        in_specs=[smem] + [pl.BlockSpec(memory_space=pltpu.HBM)] * 6,
        out_specs=vmem,
        scratch_shapes=[pltpu.VMEM((four,) + w.shape[1:], BF16) for w in weights]
        + [pltpu.VMEM(x.shape, BF16) for x in queries]
        + [pltpu.SemaphoreType.DMA((6,))],
        compiler_params=pltpu.CompilerParams(vmem_limit_bytes=PACK_LIMIT),
        cost_estimate=pl.CostEstimate(flops=10**6, bytes_accessed=10**6, transcendentals=0),
        name="pack",
    )(place, cache, *weights, *queries)
    near = swap(cache, "yl")
    received = swap(packed, "zh")

    vpart, width = w_out.shape[1:]
    columns = width // 4
    w_rows = heads_in * vpart
    n_spread = heads * n_all + columns // lanes * w_rows
    spread = pl.pallas_call(
        spread_kernel,
        out_shape=jax.ShapeDtypeStruct((plane, n_spread, lanes), BF16),
        in_specs=[smem] + [vmem] * 4,
        out_specs=vmem,
        compiler_params=pltpu.CompilerParams(vmem_limit_bytes=VMEM_LIMIT),
        cost_estimate=pl.CostEstimate(flops=10**6, bytes_accessed=10**6, transcendentals=0),
        name="spread",
    )(place, *weights, w_out.reshape(w_rows, width))
    spread = exchange(spread, PLANE)

    n_pack = kv_width + (2 * latent_chunks + 2) * own_rows
    packed, far_piece, rope_kept = pl.pallas_call(
        lambda *refs: unpack_kernel(*refs, sizes=(kv_width, kv_width + four * n_all)),
        out_shape=(
            jax.ShapeDtypeStruct((n_pack, lanes), BF16),
            jax.ShapeDtypeStruct((kv_width, quarter), BF16),
            jax.ShapeDtypeStruct((2 * own_rows, lanes), BF16),
        ),
        in_specs=[smem] + [vmem] * 3,
        out_specs=(vmem,) * 3,
        compiler_params=pltpu.CompilerParams(vmem_limit_bytes=VMEM_LIMIT),
        cost_estimate=pl.CostEstimate(
            flops=UNPACK_FLOPS, bytes_accessed=3 * 10**6, transcendentals=0
        ),
        name="unpack",
    )(place, received, *queries)
    rows = 4 * own_rows
    row_lengths = lengths.reshape(-1, rows)
    packed, far_piece, received, row_lengths = lax.optimization_barrier(
        (packed, far_piece, received, row_lengths)
    )
    received, near = lax.optimization_barrier((received, near))
    sent = pl.pallas_call(
        lambda *refs: repeat_kernel(*refs, first=kv_width),
        out_shape=jax.ShapeDtypeStruct((plane // 2, four, n_all, lanes), BF16),
        in_specs=[vmem],
        out_specs=vmem,
        compiler_params=pltpu.CompilerParams(vmem_limit_bytes=VMEM_LIMIT),
        cost_estimate=pl.CostEstimate(
            flops=UNPACK_FLOPS, bytes_accessed=3 * 10**6, transcendentals=0
        ),
        name="repeat",
    )(received)
    sent, spread = lax.optimization_barrier((sent, spread))

    weights_far = exchange(sent.reshape(plane * heads, n_all, lanes), PLANE)
    weights_far = weights_far.reshape(plane, heads, n_all, lanes)

    packed_y = swap(packed, "yl")
    piece_z = swap(far_piece, "zll")
    piece_yz = lax.ppermute(far_piece, ("yl", "zll"), [(0, 3), (1, 2), (2, 1), (3, 0)])
    far = jnp.concatenate([far_piece, packed_y[:kv_width], piece_z, piece_yz], axis=1)
    far_other = swap(far, "c")

    keep, give = pl.pallas_call(
        lambda *refs: attend_kernel(
            *refs,
            sizes=(rows, heads, n_uq, n_uk, n_uv, latent_width),
            temper=temper,
        ),
        out_shape=(jax.ShapeDtypeStruct((rows, lanes), BF16),) * 2,
        in_specs=[smem] + [vmem] * 10,
        out_specs=(vmem,) * 2,
        scratch_shapes=[
            pltpu.VMEM((rows, query_latent.shape[1]), BF16),
            pltpu.VMEM((rows, lanes), BF16),
            pltpu.VMEM((heads * rows, 4 * tokens), F32),
            pltpu.VMEM((plane, heads, 2, n_all, lanes), BF16),
        ],
        compiler_params=pltpu.CompilerParams(vmem_limit_bytes=VMEM_LIMIT),
        cost_estimate=pl.CostEstimate(flops=10**9, bytes_accessed=5 * 10**6, transcendentals=0),
        name="attend",
    )(place, packed, packed_y, spread, weights_far, rope_kept, row_lengths, cache, near, far, far_other)

    values = ordered(keep, swap(give, "zh"), zh, 1)
    gathered = exchange(
        jnp.broadcast_to(values[None], (4,) + values.shape).reshape(-1, values.shape[1]), RING
    ).reshape((4,) + values.shape)
    order = jnp.asarray(feature_order(heads, plane, vpart), BF16)
    shape = (4, 2, 2, own_rows, columns // 4)
    keep, give = pl.pallas_call(
        project_kernel,
        out_shape=(jax.ShapeDtypeStruct(shape, BF16),) * 2,
        in_specs=[smem] + [vmem] * 3,
        out_specs=(vmem,) * 2,
        compiler_params=pltpu.CompilerParams(vmem_limit_bytes=VMEM_LIMIT),
        cost_estimate=pl.CostEstimate(flops=2 * 10**8, bytes_accessed=2 * 10**6, transcendentals=0),
        name="project",
    )(place, gathered, spread, order)

    total = (keep.astype(F32) + swap(give, "c").astype(F32)).astype(BF16)
    total = jnp.transpose(exchange(total, RING), (1, 0, 2, 3, 4))
    total = exchange(total.reshape((16,) + total.shape[3:]), COLUMN)
    return jnp.sum(total.astype(F32), axis=0).astype(BF16)


def solution(mesh):
    fine = Mesh(mesh.devices.reshape(SIZES), AXES)
    placed = (
        P(FSDP, None),
        P(FSDP, HEAD, None),
        P(),
        P(FSDP, None),
        P(HEAD, FSDP, None),
        P(HEAD, FSDP, None),
        P(HEAD, FSDP, None),
        P(HEAD, FSDP, None),
    )
    return jax.shard_map(
        local, mesh=fine, in_specs=placed, out_specs=P(FSDP, HEAD), check_vma=False
    )
```

```python
import math

import jax
import jax.numpy as jnp
import numpy as np
from jax import lax
from jax.experimental import pallas as pl
from jax.experimental.pallas import tpu as pltpu
from jax.sharding import Mesh, PartitionSpec as P

AXES = ("xh", "xl", "yh", "yl", "zh", "zlh", "zll", "c")
SIZES = (2, 2, 2, 2, 2, 4, 2, 2)
FSDP = ("xh", "xl", "yh", "yl", "zh")
HEAD = ("zlh", "zll", "c")
PLANE = ("xh", "xl", "yh", "yl")
PART = ("xl", "yh", "yl")
COLUMN = ("zh", "zlh", "zll")
BF16 = jnp.bfloat16
F32 = jnp.float32
VMEM_LIMIT = 63 * 1024 * 1024
PACK_LIMIT = 63 * 1024 * 1024
UNPACK_FLOPS = 2 * 10**10


def swap(block, axis):
    return lax.ppermute(block, axis, [(0, 1), (1, 0)])


def ordered(ours, theirs, position, dim):
    return jnp.where(
        position == 1,
        jnp.concatenate([theirs, ours], axis=dim),
        jnp.concatenate([ours, theirs], axis=dim),
    )


def exchange(blocks, axes):
    return lax.all_to_all(blocks, axes, 0, 0, tiled=True)


def dot(a, b):
    return jnp.dot(a, b, preferred_element_type=F32)


def dot_nt(a, b):
    return lax.dot_general(a, b, (((1,), (1,)), ((), ())), preferred_element_type=F32)


def head_pairs(rope):
    return [
        jnp.concatenate([rope[:, 2 * p, :], rope[:, 2 * p + 1, :]], axis=1)
        for p in range(rope.shape[1] // 2)
    ]


def pack_kernel(
    place, cache, w_uq, w_uk, w_uv, latent, rope, out, uq, uk, uv, latent_in, rope_in, sems
):
    zh, quarter = place[0], place[2]
    lanes = out.shape[1]
    width = cache.shape[0]
    four = uq.shape[0]
    given = pl.ds((1 - zh) * four, four)
    copies = [
        (cache.at[:, pl.ds(pl.multiple_of(quarter * lanes, lanes), lanes)], out.at[pl.ds(0, width)]),
        (w_uq.at[given], uq),
        (w_uk.at[given], uk),
        (w_uv.at[given], uv),
        (latent, latent_in),
        (rope, rope_in),
    ]
    copies = [pltpu.make_async_copy(x, y, sems.at[i]) for i, (x, y) in enumerate(copies)]
    for copy in copies:
        copy.start()
    for copy in copies:
        copy.wait()
    at = width
    for h in range(four):
        for w in (uq, uk, uv):
            out[at : at + w.shape[1]] = w[h]
            at += w.shape[1]
    rows = latent_in.shape[0]
    for i in range(latent_in.shape[1] // lanes):
        out[at : at + rows] = latent_in[:, i * lanes : (i + 1) * lanes]
        at += rows
    pairs = head_pairs(rope_in)
    for p in range(len(pairs) // 2):
        out[at : at + rows] = jnp.where(zh == 0, pairs[p + len(pairs) // 2], pairs[p])
        at += rows


def spread_kernel(place, w_uq, w_uk, w_uv, w_out, out):
    zh = place[0]
    copies, lanes = out.shape[0], out.shape[2]
    four = w_uq.shape[0] // 2
    for h in range(four):
        at = h % (four // 2) * (w_uq.shape[1] + w_uk.shape[1] + w_uv.shape[1])
        for w in (w_uq, w_uk, w_uv):
            block = w[zh * four + h]
            for copy in range(h // (four // 2), copies, 2):
                out[copy, at : at + w.shape[1]] = block
            at += w.shape[1]
    rows, columns = w_out.shape[0], (out.shape[1] - at) // w_out.shape[0] * lanes
    parts = w_out.shape[1] // columns
    for copy in range(copies):
        begin = copy % parts * columns
        for i in range(columns // lanes):
            block = w_out[:, begin + i * lanes : begin + (i + 1) * lanes]
            out[copy, at + i * rows : at + (i + 1) * rows] = block


def unpack_kernel(
    place, received, latent, rope, sent, packed, piece, rope_out, *, sizes
):
    n_piece, n_all, copies = sizes
    zh, yl = place[0], place[1]
    own_rows = latent.shape[0]
    lanes = packed.shape[1]
    at = n_piece
    for h in range(sent.shape[1]):
        other = received[at : at + n_all]
        for copy in range(copies):
            sent[copy, h] = other
        at += n_all
    ours = pl.ds(pl.multiple_of(zh * own_rows, 16), own_rows)
    theirs = pl.ds(pl.multiple_of((1 - zh) * own_rows, 16), own_rows)
    to = n_piece
    for i in range(latent.shape[1] // lanes):
        packed[pl.ds(pl.multiple_of(to + zh * own_rows, 16), own_rows)] = latent[
            :, i * lanes : (i + 1) * lanes
        ]
        packed[pl.ds(pl.multiple_of(to + (1 - zh) * own_rows, 16), own_rows)] = received[
            at : at + own_rows
        ]
        to += 2 * own_rows
        at += own_rows
    pairs = head_pairs(rope)
    lower = [jnp.where(zh == 0, pairs[0], pairs[2]), received[at : at + own_rows]]
    upper = [jnp.where(zh == 0, pairs[1], pairs[3]), received[at + own_rows : at + 2 * own_rows]]
    stay = [jnp.where(yl == 0, x, y) for x, y in zip(lower, upper)]
    go = [jnp.where(yl == 0, y, x) for x, y in zip(lower, upper)]
    rope_out[ours] = stay[0]
    rope_out[theirs] = stay[1]
    packed[pl.ds(pl.multiple_of(to + zh * own_rows, 16), own_rows)] = go[0]
    packed[pl.ds(pl.multiple_of(to + (1 - zh) * own_rows, 16), own_rows)] = go[1]
    packed[:n_piece] = received[:n_piece]
    piece[...] = received[:n_piece]


def attend_kernel(
    place,
    ours,
    theirs,
    weights_ours,
    weights_theirs,
    rope_ours,
    lengths,
    kv0,
    kv1,
    kv2,
    kv3,
    keep_out,
    give_out,
    query_rows,
    rope,
    scores,
    weights,
    *,
    sizes,
    temper,
):
    rows, heads, n_uq, n_uk, n_uv, width = sizes
    caches = (kv0, kv1, kv2, kv3)
    zh, yl, core = place[0], place[1], place[3]
    zll = place[2] - core * 2
    quarter = kv0.shape[1] // 4
    starts = []
    for ylo in (yl, 1 - yl):
        for i in range(4):
            starts.append((ylo * 2 + zh) * kv0.shape[1] + i * quarter)
    for co in (core, 1 - core):
        for zo in (zll, 1 - zll):
            for ylo in (yl, 1 - yl):
                starts.append((ylo * 2 + 1 - zh) * kv0.shape[1] + (co * 2 + zo) * quarter)
    n_all = n_uq + n_uk + n_uv
    for h in range(heads):
        weights[:, h, zh] = weights_ours[:, h * n_all : (h + 1) * n_all]
        weights[:, h, 1 - zh] = weights_theirs[:, h]
    per_block = kv0.shape[1]
    chunk = quarter
    half = rows // 2
    mine = pl.ds(pl.multiple_of(yl * half, 16), half)
    other = pl.ds(pl.multiple_of((1 - yl) * half, 16), half)
    at = kv0.shape[0]
    lane_count = ours.shape[1]
    for i in range(query_rows.shape[1] // lane_count):
        lanes_here = slice(i * lane_count, (i + 1) * lane_count)
        query_rows[mine, lanes_here] = ours[at : at + half]
        query_rows[other, lanes_here] = theirs[at : at + half]
        at += half
    rope[mine, :] = rope_ours[...]
    rope[other, :] = theirs[at : at + half]
    query = query_rows[...]
    diagonal = lax.broadcasted_iota(jnp.int32, (rows, rows), 0) == lax.broadcasted_iota(
        jnp.int32, (rows, rows), 1
    )
    limit = jnp.sum(
        jnp.where(diagonal, lengths[pl.ds(place[4], 1), :], 0), axis=1, keepdims=True
    )
    limit = jnp.concatenate([limit] * heads, axis=0)
    all_rows = heads * rows
    lanes = lax.broadcasted_iota(jnp.int32, (all_rows, chunk), 1)
    rope_width = kv0.shape[0] - width
    q_lat = []
    for h in range(heads):
        w_uq = weights[:, h, :, 0:n_uq, :].reshape(-1, weights.shape[-1])
        w_uk = weights[:, h, :, n_uq : n_uq + n_uk, :].reshape(-1, weights.shape[-1])
        q_nope = dot(query, w_uq).astype(BF16)
        q_lat.append(dot_nt(q_nope, w_uk).astype(BF16))
    q_lat = jnp.concatenate(q_lat, axis=0)
    q_rope = jnp.concatenate(
        [rope[:, h * rope_width : (h + 1) * rope_width] for h in range(heads)], axis=0
    )
    top = jnp.full((all_rows, 1), -1e30, F32)
    for b, cache in enumerate(caches):
        s = dot(q_lat, cache[:width, :]) + dot(q_rope, cache[width:, :])
        s = s * temper
        for i in range(per_block // chunk):
            k = b * (per_block // chunk) + i
            piece = s[:, i * chunk : (i + 1) * chunk]
            piece = jnp.where(lanes + starts[k] < limit, piece, -1e30)
            top = jnp.maximum(top, jnp.max(piece, axis=1, keepdims=True))
            scores[:, k * chunk : (k + 1) * chunk] = piece
    total = jnp.zeros((all_rows, 1), F32)
    context = jnp.zeros((all_rows, width), F32)
    for b, cache in enumerate(caches):
        p = jnp.exp(scores[:, b * per_block : (b + 1) * per_block] - top)
        total = total + jnp.sum(p, axis=1, keepdims=True)
        context = context + dot_nt(p.astype(BF16), cache[:width, :])
    context = (context / total).astype(BF16)
    values = []
    for h in range(heads):
        w_uv = weights[:, h, :, n_uq + n_uk :, :].reshape(-1, weights.shape[-1])
        values.append(dot(context[h * rows : (h + 1) * rows], w_uv).astype(BF16))
    vdim = values[0].shape[1]
    wide = heads * vdim
    to = lax.broadcasted_iota(jnp.int32, (wide, wide), 1)
    source = lax.broadcasted_iota(jnp.int32, (wide, wide), 0)
    side = to // (wide // 2)
    head = to % (wide // 2) // (vdim // 2)
    item = to % (vdim // 2)
    wanted = head * vdim + item // 4 * 8 + jnp.where(side == 0, zh, 1 - zh) * 4 + item % 4
    move = jnp.where(source == wanted, 1.0, 0.0).astype(BF16)
    moved = dot(jnp.concatenate(values, axis=1), move).astype(BF16)
    keep_out[...] = moved[:, : wide // 2]
    give_out[...] = moved[:, wide // 2 :]


def feature_order(heads, plane, items):
    count = 4 * heads * plane * items
    to = np.arange(count).reshape(plane, 2, 2, heads, items).transpose(2, 1, 3, 0, 4).reshape(-1)
    return np.equal(to[:, None], np.arange(count)[None, :]).astype(np.float32)


def project_kernel(place, values, received, order, keep_out, give_out):
    core = place[3]
    lanes = received.shape[2]
    rows = [
        jnp.concatenate([values[i], values[i + 1]], axis=1) for i in range(0, values.shape[0], 2)
    ]
    rows = dot(jnp.concatenate(rows, axis=0), order[...]).astype(BF16)
    depth = rows.shape[1]
    each = depth // received.shape[0]
    columns = keep_out.shape[-1]
    count = 2 * columns // lanes
    first = received.shape[1] - count * each
    weights = jnp.concatenate(
        [
            received[:, at : at + each].reshape(depth, lanes)
            for at in range(first, received.shape[1], each)
        ],
        axis=1,
    )
    part = dot(rows, weights)
    even, odd = part[:, :columns], part[:, columns:]
    keep_out[...] = jnp.where(core == 0, even, odd).astype(BF16).reshape(keep_out.shape)
    give_out[...] = jnp.where(core == 0, odd, even).astype(BF16).reshape(give_out.shape)


def local(query_latent, query_rope, lengths, kv_cache, w_uq, w_uk, w_uv, w_out):
    yl, zh, zll, core = (lax.axis_index(a) for a in ("yl", "zh", "zll", "c"))
    plane = 16
    cache = kv_cache.T
    kv_width, tokens = cache.shape
    latent_width = w_uk.shape[1] * 32
    rope_width = kv_width - latent_width
    lanes = w_uq.shape[2]
    temper = 1.0 / math.sqrt(lanes + rope_width)
    n_uq, n_uk, n_uv = w_uq.shape[1], w_uk.shape[1], w_uv.shape[1]
    n_all = n_uq + n_uk + n_uv
    own_rows = query_latent.shape[0]
    heads_in = w_uq.shape[0]
    four, heads = heads_in // 2, heads_in // 4

    quarter = tokens // 4
    sequence = lax.axis_index("xh") * 4 + lax.axis_index("xl") * 2 + lax.axis_index("yh")
    place = jnp.stack([zh, yl, core * 2 + zll, core, sequence]).astype(jnp.int32)
    vmem = pl.BlockSpec(memory_space=pltpu.VMEM)
    smem = pl.BlockSpec(memory_space=pltpu.SMEM)
    weights = (w_uq, w_uk, w_uv)
    queries = (query_latent, query_rope)
    latent_chunks = query_latent.shape[1] // lanes
    n_sent = kv_width + four * n_all + (latent_chunks + 2) * own_rows
    packed = pl.pallas_call(
        pack_kernel,
        out_shape=jax.ShapeDtypeStruct((n_sent, lanes), BF16),
        in_specs=[smem] + [pl.BlockSpec(memory_space=pltpu.HBM)] * 6,
        out_specs=vmem,
        scratch_shapes=[pltpu.VMEM((four,) + w.shape[1:], BF16) for w in weights]
        + [pltpu.VMEM(x.shape, BF16) for x in queries]
        + [pltpu.SemaphoreType.DMA((6,))],
        compiler_params=pltpu.CompilerParams(vmem_limit_bytes=PACK_LIMIT),
        cost_estimate=pl.CostEstimate(flops=10**6, bytes_accessed=10**6, transcendentals=0),
        name="pack",
    )(place, cache, *weights, *queries)
    near = swap(cache, "yl")
    received = swap(packed, "zh")

    vpart, width = w_out.shape[1:]
    columns = width // 8
    w_rows = heads_in * vpart
    n_spread = heads * n_all + columns // lanes * w_rows
    spread = pl.pallas_call(
        spread_kernel,
        out_shape=jax.ShapeDtypeStruct((plane, n_spread, lanes), BF16),
        in_specs=[smem] + [vmem] * 4,
        out_specs=vmem,
        compiler_params=pltpu.CompilerParams(vmem_limit_bytes=VMEM_LIMIT),
        cost_estimate=pl.CostEstimate(flops=10**6, bytes_accessed=10**6, transcendentals=0),
        name="spread",
    )(place, *weights, w_out.reshape(w_rows, width))
    spread = exchange(spread, PLANE)

    n_pack = kv_width + (2 * latent_chunks + 2) * own_rows
    sent, packed, far_piece, rope_kept = pl.pallas_call(
        lambda *refs: unpack_kernel(*refs, sizes=(kv_width, n_all, plane // 2)),
        out_shape=(
            jax.ShapeDtypeStruct((plane // 2, four, n_all, lanes), BF16),
            jax.ShapeDtypeStruct((n_pack, lanes), BF16),
            jax.ShapeDtypeStruct((kv_width, quarter), BF16),
            jax.ShapeDtypeStruct((2 * own_rows, lanes), BF16),
        ),
        in_specs=[smem] + [vmem] * 3,
        out_specs=(vmem,) * 4,
        compiler_params=pltpu.CompilerParams(vmem_limit_bytes=VMEM_LIMIT),
        cost_estimate=pl.CostEstimate(
            flops=UNPACK_FLOPS, bytes_accessed=3 * 10**6, transcendentals=0
        ),
        name="unpack",
    )(place, received, *queries)
    rows = 4 * own_rows
    row_lengths = lengths.reshape(-1, rows)
    sent, packed, far_piece, near, row_lengths = lax.optimization_barrier(
        (sent, packed, far_piece, near, row_lengths)
    )
    sent, spread = lax.optimization_barrier((sent, spread))

    weights_far = exchange(sent.reshape(plane * heads, n_all, lanes), PLANE)
    weights_far = weights_far.reshape(plane, heads, n_all, lanes)

    packed_y = swap(packed, "yl")
    piece_z = swap(far_piece, "zll")
    piece_yz = lax.ppermute(far_piece, ("yl", "zll"), [(0, 3), (1, 2), (2, 1), (3, 0)])
    far = jnp.concatenate([far_piece, packed_y[:kv_width], piece_z, piece_yz], axis=1)
    far_other = swap(far, "c")

    keep, give = pl.pallas_call(
        lambda *refs: attend_kernel(
            *refs,
            sizes=(rows, heads, n_uq, n_uk, n_uv, latent_width),
            temper=temper,
        ),
        out_shape=(jax.ShapeDtypeStruct((rows, lanes), BF16),) * 2,
        in_specs=[smem] + [vmem] * 10,
        out_specs=(vmem,) * 2,
        scratch_shapes=[
            pltpu.VMEM((rows, query_latent.shape[1]), BF16),
            pltpu.VMEM((rows, lanes), BF16),
            pltpu.VMEM((heads * rows, 4 * tokens), F32),
            pltpu.VMEM((plane, heads, 2, n_all, lanes), BF16),
        ],
        compiler_params=pltpu.CompilerParams(vmem_limit_bytes=VMEM_LIMIT),
        cost_estimate=pl.CostEstimate(flops=10**9, bytes_accessed=5 * 10**6, transcendentals=0),
        name="attend",
    )(place, packed, packed_y, spread, weights_far, rope_kept, row_lengths, cache, near, far, far_other)

    values = ordered(keep, swap(give, "zh"), zh, 1)
    gathered = exchange(
        jnp.broadcast_to(values[None], (8,) + values.shape).reshape(-1, values.shape[1]), PART
    ).reshape((8,) + values.shape)
    order = jnp.asarray(feature_order(heads, plane, vpart), BF16)
    shape = (8, 2, own_rows, columns // 2)
    keep, give = pl.pallas_call(
        project_kernel,
        out_shape=(jax.ShapeDtypeStruct(shape, BF16),) * 2,
        in_specs=[smem] + [vmem] * 3,
        out_specs=(vmem,) * 2,
        compiler_params=pltpu.CompilerParams(vmem_limit_bytes=VMEM_LIMIT),
        cost_estimate=pl.CostEstimate(flops=2 * 10**8, bytes_accessed=2 * 10**6, transcendentals=0),
        name="project",
    )(place, gathered, spread, order)

    total = (keep.astype(F32) + swap(give, "c").astype(F32)).astype(BF16)
    total = jnp.transpose(exchange(total, PART), (1, 0, 2, 3))
    total = exchange(total.reshape((16,) + total.shape[2:]), COLUMN)
    return jnp.sum(total.astype(F32), axis=0).astype(BF16)


def solution(mesh):
    fine = Mesh(mesh.devices.reshape(SIZES), AXES)
    placed = (
        P(FSDP, None),
        P(FSDP, HEAD, None),
        P(),
        P(FSDP, None),
        P(HEAD, FSDP, None),
        P(HEAD, FSDP, None),
        P(HEAD, FSDP, None),
        P(HEAD, FSDP, None),
    )
    return jax.shard_map(
        local, mesh=fine, in_specs=placed, out_specs=P(FSDP, HEAD), check_vma=False
    )
```

```python
import math

import jax
import jax.numpy as jnp
from jax import lax
from jax.experimental import pallas as pl
from jax.experimental.pallas import tpu as pltpu
from jax.sharding import Mesh, PartitionSpec as P

AXES = ("xh", "xl", "yh", "yl", "zh", "zlh", "zll", "c")
SIZES = (2, 2, 2, 2, 2, 4, 2, 2)
FSDP = ("xh", "xl", "yh", "yl", "zh")
HEAD = ("zlh", "zll", "c")
PLANE = ("xh", "xl", "yh", "yl")
PART = ("xl", "yh", "yl")
COLUMN = ("zh", "zlh", "zll")
BF16 = jnp.bfloat16
F32 = jnp.float32
VMEM_LIMIT = 12 * 1024 * 1024
UNPACK_FLOPS = 2 * 10**10


def swap(block, axis):
    return lax.ppermute(block, axis, [(0, 1), (1, 0)])


def ordered(ours, theirs, position, dim):
    return jnp.where(
        position == 1,
        jnp.concatenate([theirs, ours], axis=dim),
        jnp.concatenate([ours, theirs], axis=dim),
    )


def exchange(blocks, axes):
    return lax.all_to_all(blocks, axes, 0, 0, tiled=True)


def dot(a, b):
    return jnp.dot(a, b, preferred_element_type=F32)


def dot_nt(a, b):
    return lax.dot_general(a, b, (((1,), (1,)), ((), ())), preferred_element_type=F32)


def head_pairs(rope):
    return [
        jnp.concatenate([rope[:, 2 * p, :], rope[:, 2 * p + 1, :]], axis=1)
        for p in range(rope.shape[1] // 2)
    ]


def pack_kernel(place, cache, w_uq, w_uk, w_uv, latent, rope, out):
    zh, quarter = place[0], place[2]
    lanes = out.shape[1]
    at = cache.shape[0]
    out[:at] = cache[:, pl.ds(pl.multiple_of(quarter * lanes, lanes), lanes)]
    four = w_uq.shape[0] // 2
    for h in range(four):
        for w in (w_uq, w_uk, w_uv):
            out[at : at + w.shape[1]] = w[(1 - zh) * four + h]
            at += w.shape[1]
    rows = latent.shape[0]
    for i in range(latent.shape[1] // lanes):
        out[at : at + rows] = latent[:, i * lanes : (i + 1) * lanes]
        at += rows
    pairs = head_pairs(rope)
    for p in range(len(pairs) // 2):
        out[at : at + rows] = jnp.where(zh == 0, pairs[p + len(pairs) // 2], pairs[p])
        at += rows


def spread_kernel(place, w_uq, w_uk, w_uv, w_out, out):
    zh = place[0]
    copies, lanes = out.shape[0], out.shape[2]
    four = w_uq.shape[0] // 2
    for h in range(four):
        at = h % (four // 2) * (w_uq.shape[1] + w_uk.shape[1] + w_uv.shape[1])
        for w in (w_uq, w_uk, w_uv):
            block = w[zh * four + h]
            for copy in range(h // (four // 2), copies, 2):
                out[copy, at : at + w.shape[1]] = block
            at += w.shape[1]
    rows, columns = w_out.shape[0], (out.shape[1] - at) // w_out.shape[0] * lanes
    parts = w_out.shape[1] // columns
    for copy in range(copies):
        begin = copy % parts * columns
        for i in range(columns // lanes):
            block = w_out[:, begin + i * lanes : begin + (i + 1) * lanes]
            out[copy, at + i * rows : at + (i + 1) * rows] = block


def unpack_kernel(
    place, received, latent, rope, sent, packed, piece, rope_out, *, sizes
):
    n_piece, n_all, copies = sizes
    zh, yl = place[0], place[1]
    own_rows = latent.shape[0]
    lanes = packed.shape[1]
    at = n_piece
    for h in range(sent.shape[1]):
        other = received[at : at + n_all]
        for copy in range(copies):
            sent[copy, h] = other
        at += n_all
    ours = pl.ds(pl.multiple_of(zh * own_rows, 16), own_rows)
    theirs = pl.ds(pl.multiple_of((1 - zh) * own_rows, 16), own_rows)
    to = 0
    for i in range(latent.shape[1] // lanes):
        packed[pl.ds(pl.multiple_of(to + zh * own_rows, 16), own_rows)] = latent[
            :, i * lanes : (i + 1) * lanes
        ]
        packed[pl.ds(pl.multiple_of(to + (1 - zh) * own_rows, 16), own_rows)] = received[
            at : at + own_rows
        ]
        to += 2 * own_rows
        at += own_rows
    pairs = head_pairs(rope)
    lower = [jnp.where(zh == 0, pairs[0], pairs[2]), received[at : at + own_rows]]
    upper = [jnp.where(zh == 0, pairs[1], pairs[3]), received[at + own_rows : at + 2 * own_rows]]
    stay = [jnp.where(yl == 0, x, y) for x, y in zip(lower, upper)]
    go = [jnp.where(yl == 0, y, x) for x, y in zip(lower, upper)]
    rope_out[ours] = stay[0]
    rope_out[theirs] = stay[1]
    packed[pl.ds(pl.multiple_of(to + zh * own_rows, 16), own_rows)] = go[0]
    packed[pl.ds(pl.multiple_of(to + (1 - zh) * own_rows, 16), own_rows)] = go[1]
    piece[...] = received[:n_piece]


def attend_kernel(
    place,
    ours,
    theirs,
    weights_ours,
    weights_theirs,
    rope_ours,
    lengths,
    kv0,
    kv1,
    kv2,
    kv3,
    keep_out,
    give_out,
    query_rows,
    rope,
    scores,
    weights,
    *,
    sizes,
    temper,
):
    rows, heads, n_uq, n_uk, n_uv, width = sizes
    caches = [kv0, kv1] + [kv.at[c] for kv in (kv2, kv3) for c in range(2)]
    spans, tokens = [], 0
    for cache in caches:
        spans.append((tokens, tokens + cache.shape[1]))
        tokens += cache.shape[1]
    zh, yl, core = place[0], place[1], place[3]
    zll = place[2] - core * 2
    quarter = kv0.shape[1] // 4
    starts = []
    for ylo in (yl, 1 - yl):
        for i in range(4):
            starts.append((ylo * 2 + zh) * kv0.shape[1] + i * quarter)
    for zo in (zll, 1 - zll):
        for co in (0, 1):
            for ylo in (yl, 1 - yl):
                starts.append((ylo * 2 + 1 - zh) * kv0.shape[1] + (co * 2 + zo) * quarter)
    n_all = n_uq + n_uk + n_uv
    for h in range(heads):
        weights[:, h, zh] = weights_ours[:, h * n_all : (h + 1) * n_all]
        weights[:, h, 1 - zh] = weights_theirs[:, h]
    chunk = quarter
    half = rows // 2
    mine = pl.ds(pl.multiple_of(yl * half, 16), half)
    other = pl.ds(pl.multiple_of((1 - yl) * half, 16), half)
    at = 0
    lane_count = ours.shape[1]
    for i in range(query_rows.shape[1] // lane_count):
        lanes_here = slice(i * lane_count, (i + 1) * lane_count)
        query_rows[mine, lanes_here] = ours[at : at + half]
        query_rows[other, lanes_here] = theirs[at : at + half]
        at += half
    rope[mine, :] = rope_ours[...]
    rope[other, :] = theirs[at : at + half]
    query = query_rows[...]
    diagonal = lax.broadcasted_iota(jnp.int32, (rows, rows), 0) == lax.broadcasted_iota(
        jnp.int32, (rows, rows), 1
    )
    limit = jnp.sum(
        jnp.where(diagonal, lengths[pl.ds(place[4], 1), :], 0), axis=1, keepdims=True
    )
    limit = jnp.concatenate([limit] * heads, axis=0)
    all_rows = heads * rows
    lanes = lax.broadcasted_iota(jnp.int32, (all_rows, chunk), 1)
    rope_width = kv0.shape[0] - width
    q_lat = []
    for h in range(heads):
        w_uq = weights[:, h, :, 0:n_uq, :].reshape(-1, weights.shape[-1])
        w_uk = weights[:, h, :, n_uq : n_uq + n_uk, :].reshape(-1, weights.shape[-1])
        q_nope = dot(query, w_uq).astype(BF16)
        q_lat.append(dot_nt(q_nope, w_uk).astype(BF16))
    q_lat = jnp.concatenate(q_lat, axis=0)
    q_rope = jnp.concatenate(
        [rope[:, h * rope_width : (h + 1) * rope_width] for h in range(heads)], axis=0
    )
    top = jnp.full((all_rows, 1), -1e30, F32)
    for (begin, end), cache in zip(spans, caches):
        s = dot(q_lat, cache[:width, :]) + dot(q_rope, cache[width:, :])
        s = s * temper
        for k in range(begin // chunk, end // chunk):
            piece = s[:, k * chunk - begin : (k + 1) * chunk - begin]
            piece = jnp.where(lanes + starts[k] < limit, piece, -1e30)
            top = jnp.maximum(top, jnp.max(piece, axis=1, keepdims=True))
            scores[:, k * chunk : (k + 1) * chunk] = piece
    total = jnp.zeros((all_rows, 1), F32)
    context = jnp.zeros((all_rows, width), F32)
    for (begin, end), cache in zip(spans, caches):
        p = jnp.exp(scores[:, begin:end] - top)
        total = total + jnp.sum(p, axis=1, keepdims=True)
        context = context + dot_nt(p.astype(BF16), cache[:width, :])
    context = (context / total).astype(BF16)
    values = []
    for h in range(heads):
        w_uv = weights[:, h, :, n_uq + n_uk :, :].reshape(-1, weights.shape[-1])
        values.append(dot(context[h * rows : (h + 1) * rows], w_uv).astype(BF16))
    vdim = values[0].shape[1]
    wide = heads * vdim
    to = lax.broadcasted_iota(jnp.int32, (wide, wide), 1)
    source = lax.broadcasted_iota(jnp.int32, (wide, wide), 0)
    side = to // (wide // 2)
    head = to % (wide // 2) // (vdim // 2)
    item = to % (vdim // 2)
    wanted = head * vdim + item // 4 * 8 + jnp.where(side == 0, zh, 1 - zh) * 4 + item % 4
    move = jnp.where(source == wanted, 1.0, 0.0).astype(BF16)
    moved = dot(jnp.concatenate(values, axis=1), move).astype(BF16)
    keep_out[...] = moved[:, : wide // 2]
    give_out[...] = moved[:, wide // 2 :]


def project_kernel(place, values, received, keep_out, give_out):
    core = place[3]
    lanes = received.shape[2]
    rows = [
        jnp.concatenate([values[i], values[i + 1]], axis=1) for i in range(0, values.shape[0], 2)
    ]
    rows = jnp.concatenate(rows, axis=0)
    depth = rows.shape[1]
    source = lax.broadcasted_iota(jnp.int32, (depth, depth), 0)
    to = lax.broadcasted_iota(jnp.int32, (depth, depth), 1)
    y, z, j = source // 256, source // 128 % 2, source // 64 % 2
    wanted = source // 4 % 16 * 32 + (z * 4 + y * 2 + j) * 4 + source % 4
    order = jnp.where(to == wanted, 1.0, 0.0).astype(BF16)
    rows = dot(rows, order).astype(BF16)
    each = depth // received.shape[0]
    columns = keep_out.shape[-1]
    count = 2 * columns // lanes
    first = received.shape[1] - count * each
    weights = jnp.concatenate(
        [
            received[:, at : at + each].reshape(depth, lanes)
            for at in range(first, received.shape[1], each)
        ],
        axis=1,
    )
    part = dot(rows, weights)
    even, odd = part[:, :columns], part[:, columns:]
    keep_out[...] = jnp.where(core == 0, even, odd).astype(BF16).reshape(keep_out.shape)
    give_out[...] = jnp.where(core == 0, odd, even).astype(BF16).reshape(give_out.shape)


def local(query_latent, query_rope, lengths, kv_cache, w_uq, w_uk, w_uv, w_out):
    yl, zh, zll, core = (lax.axis_index(a) for a in ("yl", "zh", "zll", "c"))
    plane = 16
    cache = kv_cache.T
    kv_width, tokens = cache.shape
    latent_width = w_uk.shape[1] * 32
    rope_width = kv_width - latent_width
    lanes = w_uq.shape[2]
    temper = 1.0 / math.sqrt(lanes + rope_width)
    n_uq, n_uk, n_uv = w_uq.shape[1], w_uk.shape[1], w_uv.shape[1]
    n_all = n_uq + n_uk + n_uv
    own_rows = query_latent.shape[0]
    heads_in = w_uq.shape[0]
    four, heads = heads_in // 2, heads_in // 4

    quarter = tokens // 4
    sequence = lax.axis_index("xh") * 4 + lax.axis_index("xl") * 2 + lax.axis_index("yh")
    place = jnp.stack([zh, yl, core * 2 + zll, core, sequence]).astype(jnp.int32)
    vmem = pl.BlockSpec(memory_space=pltpu.VMEM)
    smem = pl.BlockSpec(memory_space=pltpu.SMEM)
    weights = (w_uq, w_uk, w_uv)
    queries = (query_latent, query_rope)
    latent_chunks = query_latent.shape[1] // lanes
    n_sent = kv_width + four * n_all + (latent_chunks + 2) * own_rows
    packed = pl.pallas_call(
        pack_kernel,
        out_shape=jax.ShapeDtypeStruct((n_sent, lanes), BF16),
        in_specs=[smem] + [vmem] * 6,
        out_specs=vmem,
        compiler_params=pltpu.CompilerParams(vmem_limit_bytes=VMEM_LIMIT),
        cost_estimate=pl.CostEstimate(flops=10**6, bytes_accessed=10**6, transcendentals=0),
        name="pack",
    )(place, cache, *weights, *queries)
    near = swap(cache, "yl")
    received = swap(packed, "zh")

    vpart, width = w_out.shape[1:]
    columns = width // 8
    w_rows = heads_in * vpart
    n_spread = heads * n_all + columns // lanes * w_rows
    spread = pl.pallas_call(
        spread_kernel,
        out_shape=jax.ShapeDtypeStruct((plane, n_spread, lanes), BF16),
        in_specs=[smem] + [vmem] * 4,
        out_specs=vmem,
        compiler_params=pltpu.CompilerParams(vmem_limit_bytes=VMEM_LIMIT),
        cost_estimate=pl.CostEstimate(flops=10**6, bytes_accessed=10**6, transcendentals=0),
        name="spread",
    )(place, *weights, w_out.reshape(w_rows, width))
    spread = exchange(spread, PLANE)

    n_pack = (2 * latent_chunks + 2) * own_rows
    sent, packed, far_piece, rope_kept = pl.pallas_call(
        lambda *refs: unpack_kernel(*refs, sizes=(kv_width, n_all, plane // 2)),
        out_shape=(
            jax.ShapeDtypeStruct((plane // 2, four, n_all, lanes), BF16),
            jax.ShapeDtypeStruct((n_pack, lanes), BF16),
            jax.ShapeDtypeStruct((kv_width, quarter), BF16),
            jax.ShapeDtypeStruct((2 * own_rows, lanes), BF16),
        ),
        in_specs=[smem] + [vmem] * 3,
        out_specs=(vmem,) * 4,
        compiler_params=pltpu.CompilerParams(vmem_limit_bytes=VMEM_LIMIT),
        cost_estimate=pl.CostEstimate(
            flops=UNPACK_FLOPS, bytes_accessed=3 * 10**6, transcendentals=0
        ),
        name="unpack",
    )(place, received, *queries)
    rows = 4 * own_rows
    row_lengths = lengths.reshape(-1, rows)
    sent, packed, far_piece, near, row_lengths = lax.optimization_barrier(
        (sent, packed, far_piece, near, row_lengths)
    )
    sent, spread = lax.optimization_barrier((sent, spread))

    weights_far = exchange(sent.reshape(plane * heads, n_all, lanes), PLANE)
    weights_far = weights_far.reshape(plane, heads, n_all, lanes)

    packed_y = swap(packed, "yl")
    piece_z = swap(far_piece, "zll")
    piece_yz = lax.ppermute(far_piece, ("yl", "zll"), [(0, 3), (1, 2), (2, 1), (3, 0)])
    piece_y = swap(far_piece, "yl")
    far = lax.all_gather(jnp.concatenate([far_piece, piece_y], axis=1), "c", axis=0)
    far_z = lax.all_gather(jnp.concatenate([piece_z, piece_yz], axis=1), "c", axis=0)

    keep, give = pl.pallas_call(
        lambda *refs: attend_kernel(
            *refs,
            sizes=(rows, heads, n_uq, n_uk, n_uv, latent_width),
            temper=temper,
        ),
        out_shape=(jax.ShapeDtypeStruct((rows, lanes), BF16),) * 2,
        in_specs=[smem] + [vmem] * 10,
        out_specs=(vmem,) * 2,
        scratch_shapes=[
            pltpu.VMEM((rows, query_latent.shape[1]), BF16),
            pltpu.VMEM((rows, lanes), BF16),
            pltpu.VMEM((heads * rows, 4 * tokens), F32),
            pltpu.VMEM((plane, heads, 2, n_all, lanes), BF16),
        ],
        compiler_params=pltpu.CompilerParams(vmem_limit_bytes=VMEM_LIMIT),
        cost_estimate=pl.CostEstimate(flops=10**9, bytes_accessed=5 * 10**6, transcendentals=0),
        name="attend",
    )(place, packed, packed_y, spread, weights_far, rope_kept, row_lengths, cache, near, far, far_z)

    values = ordered(keep, swap(give, "zh"), zh, 1)
    gathered = exchange(
        jnp.broadcast_to(values[None], (8,) + values.shape).reshape(-1, values.shape[1]), PART
    ).reshape((8,) + values.shape)
    shape = (8, 2, own_rows, columns // 2)
    keep, give = pl.pallas_call(
        project_kernel,
        out_shape=(jax.ShapeDtypeStruct(shape, BF16),) * 2,
        in_specs=[smem] + [vmem] * 2,
        out_specs=(vmem,) * 2,
        compiler_params=pltpu.CompilerParams(vmem_limit_bytes=VMEM_LIMIT),
        cost_estimate=pl.CostEstimate(flops=2 * 10**8, bytes_accessed=2 * 10**6, transcendentals=0),
        name="project",
    )(place, gathered, spread)

    total = (keep.astype(F32) + swap(give, "c").astype(F32)).astype(BF16)
    total = jnp.transpose(exchange(total, PART), (1, 0, 2, 3))
    total = exchange(total.reshape((16,) + total.shape[2:]), COLUMN)
    return jnp.sum(total.astype(F32), axis=0).astype(BF16)


def solution(mesh):
    fine = Mesh(mesh.devices.reshape(SIZES), AXES)
    placed = (
        P(FSDP, None),
        P(FSDP, HEAD, None),
        P(),
        P(FSDP, None),
        P(HEAD, FSDP, None),
        P(HEAD, FSDP, None),
        P(HEAD, FSDP, None),
        P(HEAD, FSDP, None),
    )
    return jax.shard_map(
        local, mesh=fine, in_specs=placed, out_specs=P(FSDP, HEAD), check_vma=False
    )
```

```python
import math

import jax
import jax.numpy as jnp
from jax import lax
from jax.experimental import pallas as pl
from jax.experimental.pallas import tpu as pltpu
from jax.sharding import Mesh, PartitionSpec as P

AXES = ("xh", "xl", "yh", "yl", "zh", "zlh", "zll", "c")
SIZES = (2, 2, 2, 2, 2, 4, 2, 2)
FSDP = ("xh", "xl", "yh", "yl", "zh")
HEAD = ("zlh", "zll", "c")
PLANE = ("xh", "xl", "yh", "yl")
PART = ("xl", "yh", "yl")
COLUMN = ("zh", "zlh", "zll")
BF16 = jnp.bfloat16
F32 = jnp.float32
VMEM_LIMIT = 12 * 1024 * 1024
UNPACK_FLOPS = 2 * 10**10


def swap(block, axis):
    return lax.ppermute(block, axis, [(0, 1), (1, 0)])


def ordered(ours, theirs, position, dim):
    return jnp.where(
        position == 1,
        jnp.concatenate([theirs, ours], axis=dim),
        jnp.concatenate([ours, theirs], axis=dim),
    )


def exchange(blocks, axes):
    return lax.all_to_all(blocks, axes, 0, 0, tiled=True)


def dot(a, b):
    return jnp.dot(a, b, preferred_element_type=F32)


def dot_nt(a, b):
    return lax.dot_general(a, b, (((1,), (1,)), ((), ())), preferred_element_type=F32)


def head_pairs(rope):
    return [
        jnp.concatenate([rope[:, 2 * p, :], rope[:, 2 * p + 1, :]], axis=1)
        for p in range(rope.shape[1] // 2)
    ]


def pack_kernel(place, w_uq, w_uk, w_uv, latent, rope, out):
    zh = place[0]
    lanes = out.shape[1]
    at = 0
    four = w_uq.shape[0] // 2
    for h in range(four):
        for w in (w_uq, w_uk, w_uv):
            out[at : at + w.shape[1]] = w[(1 - zh) * four + h]
            at += w.shape[1]
    rows = latent.shape[0]
    for i in range(latent.shape[1] // lanes):
        out[at : at + rows] = latent[:, i * lanes : (i + 1) * lanes]
        at += rows
    pairs = head_pairs(rope)
    for p in range(len(pairs) // 2):
        out[at : at + rows] = jnp.where(zh == 0, pairs[p + len(pairs) // 2], pairs[p])
        at += rows


def spread_kernel(place, w_uq, w_uk, w_uv, w_out, out):
    zh = place[0]
    copies, lanes = out.shape[0], out.shape[2]
    four = w_uq.shape[0] // 2
    for h in range(four):
        at = h % (four // 2) * (w_uq.shape[1] + w_uk.shape[1] + w_uv.shape[1])
        for w in (w_uq, w_uk, w_uv):
            block = w[zh * four + h]
            for copy in range(h // (four // 2), copies, 2):
                out[copy, at : at + w.shape[1]] = block
            at += w.shape[1]
    rows, columns = w_out.shape[0], (out.shape[1] - at) // w_out.shape[0] * lanes
    parts = w_out.shape[1] // columns
    for copy in range(copies):
        begin = copy % parts * columns
        for i in range(columns // lanes):
            block = w_out[:, begin + i * lanes : begin + (i + 1) * lanes]
            out[copy, at + i * rows : at + (i + 1) * rows] = block


def unpack_kernel(
    place, received, latent, rope, sent, packed, rope_out, *, sizes
):
    n_all, copies = sizes
    zh, yl = place[0], place[1]
    own_rows = latent.shape[0]
    lanes = packed.shape[1]
    at = 0
    for h in range(sent.shape[1]):
        other = received[at : at + n_all]
        for copy in range(copies):
            sent[copy, h] = other
        at += n_all
    ours = pl.ds(pl.multiple_of(zh * own_rows, 16), own_rows)
    theirs = pl.ds(pl.multiple_of((1 - zh) * own_rows, 16), own_rows)
    to = 0
    for i in range(latent.shape[1] // lanes):
        packed[pl.ds(pl.multiple_of(to + zh * own_rows, 16), own_rows)] = latent[
            :, i * lanes : (i + 1) * lanes
        ]
        packed[pl.ds(pl.multiple_of(to + (1 - zh) * own_rows, 16), own_rows)] = received[
            at : at + own_rows
        ]
        to += 2 * own_rows
        at += own_rows
    pairs = head_pairs(rope)
    lower = [jnp.where(zh == 0, pairs[0], pairs[2]), received[at : at + own_rows]]
    upper = [jnp.where(zh == 0, pairs[1], pairs[3]), received[at + own_rows : at + 2 * own_rows]]
    stay = [jnp.where(yl == 0, x, y) for x, y in zip(lower, upper)]
    go = [jnp.where(yl == 0, y, x) for x, y in zip(lower, upper)]
    rope_out[ours] = stay[0]
    rope_out[theirs] = stay[1]
    packed[pl.ds(pl.multiple_of(to + zh * own_rows, 16), own_rows)] = go[0]
    packed[pl.ds(pl.multiple_of(to + (1 - zh) * own_rows, 16), own_rows)] = go[1]


def attend_kernel(
    place,
    ours,
    theirs,
    weights_ours,
    weights_theirs,
    rope_ours,
    lengths,
    kv0,
    kv1,
    kv2,
    kv3,
    keep_out,
    give_out,
    query_rows,
    rope,
    scores,
    weights,
    *,
    sizes,
    temper,
):
    rows, heads, n_uq, n_uk, n_uv, width = sizes
    caches = [kv0, kv1] + [kv.at[c] for kv in (kv2, kv3) for c in range(2)]
    spans, tokens = [], 0
    for cache in caches:
        spans.append((tokens, tokens + cache.shape[1]))
        tokens += cache.shape[1]
    zh, yl, core = place[0], place[1], place[3]
    zll = place[2] - core * 2
    quarter = kv0.shape[1] // 4
    starts = []
    for ylo in (yl, 1 - yl):
        for i in range(4):
            starts.append((ylo * 2 + zh) * kv0.shape[1] + i * quarter)
    for zo in (zll, 1 - zll):
        for co in (0, 1):
            for ylo in (yl, 1 - yl):
                starts.append((ylo * 2 + 1 - zh) * kv0.shape[1] + (co * 2 + zo) * quarter)
    n_all = n_uq + n_uk + n_uv
    for h in range(heads):
        weights[:, h, zh] = weights_ours[:, h * n_all : (h + 1) * n_all]
        weights[:, h, 1 - zh] = weights_theirs[:, h]
    chunk = quarter
    half = rows // 2
    mine = pl.ds(pl.multiple_of(yl * half, 16), half)
    other = pl.ds(pl.multiple_of((1 - yl) * half, 16), half)
    at = 0
    lane_count = ours.shape[1]
    for i in range(query_rows.shape[1] // lane_count):
        lanes_here = slice(i * lane_count, (i + 1) * lane_count)
        query_rows[mine, lanes_here] = ours[at : at + half]
        query_rows[other, lanes_here] = theirs[at : at + half]
        at += half
    rope[mine, :] = rope_ours[...]
    rope[other, :] = theirs[at : at + half]
    query = query_rows[...]
    diagonal = lax.broadcasted_iota(jnp.int32, (rows, rows), 0) == lax.broadcasted_iota(
        jnp.int32, (rows, rows), 1
    )
    limit = jnp.sum(
        jnp.where(diagonal, lengths[pl.ds(place[4], 1), :], 0), axis=1, keepdims=True
    )
    limit = jnp.concatenate([limit] * heads, axis=0)
    all_rows = heads * rows
    lanes = lax.broadcasted_iota(jnp.int32, (all_rows, chunk), 1)
    rope_width = kv0.shape[0] - width
    q_lat = []
    for h in range(heads):
        w_uq = weights[:, h, :, 0:n_uq, :].reshape(-1, weights.shape[-1])
        w_uk = weights[:, h, :, n_uq : n_uq + n_uk, :].reshape(-1, weights.shape[-1])
        q_nope = dot(query, w_uq).astype(BF16)
        q_lat.append(dot_nt(q_nope, w_uk).astype(BF16))
    q_lat = jnp.concatenate(q_lat, axis=0)
    q_rope = jnp.concatenate(
        [rope[:, h * rope_width : (h + 1) * rope_width] for h in range(heads)], axis=0
    )
    top = jnp.full((all_rows, 1), -1e30, F32)
    for (begin, end), cache in zip(spans, caches):
        s = dot(q_lat, cache[:width, :]) + dot(q_rope, cache[width:, :])
        s = s * temper
        for k in range(begin // chunk, end // chunk):
            piece = s[:, k * chunk - begin : (k + 1) * chunk - begin]
            piece = jnp.where(lanes + starts[k] < limit, piece, -1e30)
            top = jnp.maximum(top, jnp.max(piece, axis=1, keepdims=True))
            scores[:, k * chunk : (k + 1) * chunk] = piece
    total = jnp.zeros((all_rows, 1), F32)
    context = jnp.zeros((all_rows, width), F32)
    for (begin, end), cache in zip(spans, caches):
        p = jnp.exp(scores[:, begin:end] - top)
        total = total + jnp.sum(p, axis=1, keepdims=True)
        context = context + dot_nt(p.astype(BF16), cache[:width, :])
    context = (context / total).astype(BF16)
    values = []
    for h in range(heads):
        w_uv = weights[:, h, :, n_uq + n_uk :, :].reshape(-1, weights.shape[-1])
        values.append(dot(context[h * rows : (h + 1) * rows], w_uv).astype(BF16))
    vdim = values[0].shape[1]
    wide = heads * vdim
    to = lax.broadcasted_iota(jnp.int32, (wide, wide), 1)
    source = lax.broadcasted_iota(jnp.int32, (wide, wide), 0)
    side = to // (wide // 2)
    head = to % (wide // 2) // (vdim // 2)
    item = to % (vdim // 2)
    wanted = head * vdim + item // 4 * 8 + jnp.where(side == 0, zh, 1 - zh) * 4 + item % 4
    move = jnp.where(source == wanted, 1.0, 0.0).astype(BF16)
    moved = dot(jnp.concatenate(values, axis=1), move).astype(BF16)
    keep_out[...] = moved[:, : wide // 2]
    give_out[...] = moved[:, wide // 2 :]


def project_kernel(place, values, received, keep_out, give_out):
    core = place[3]
    lanes = received.shape[2]
    rows = [
        jnp.concatenate([values[i], values[i + 1]], axis=1) for i in range(0, values.shape[0], 2)
    ]
    rows = jnp.concatenate(rows, axis=0)
    depth = rows.shape[1]
    source = lax.broadcasted_iota(jnp.int32, (depth, depth), 0)
    to = lax.broadcasted_iota(jnp.int32, (depth, depth), 1)
    y, z, j = source // 256, source // 128 % 2, source // 64 % 2
    wanted = source // 4 % 16 * 32 + (z * 4 + y * 2 + j) * 4 + source % 4
    order = jnp.where(to == wanted, 1.0, 0.0).astype(BF16)
    rows = dot(rows, order).astype(BF16)
    each = depth // received.shape[0]
    columns = keep_out.shape[-1]
    count = 2 * columns // lanes
    first = received.shape[1] - count * each
    weights = jnp.concatenate(
        [
            received[:, at : at + each].reshape(depth, lanes)
            for at in range(first, received.shape[1], each)
        ],
        axis=1,
    )
    part = dot(rows, weights)
    even, odd = part[:, :columns], part[:, columns:]
    keep_out[...] = jnp.where(core == 0, even, odd).astype(BF16).reshape(keep_out.shape)
    give_out[...] = jnp.where(core == 0, odd, even).astype(BF16).reshape(give_out.shape)


def local(query_latent, query_rope, lengths, kv_cache, w_uq, w_uk, w_uv, w_out):
    yl, zh, zll, core = (lax.axis_index(a) for a in ("yl", "zh", "zll", "c"))
    plane = 16
    cache = kv_cache.T
    kv_width, tokens = cache.shape
    latent_width = w_uk.shape[1] * 32
    rope_width = kv_width - latent_width
    lanes = w_uq.shape[2]
    temper = 1.0 / math.sqrt(lanes + rope_width)
    n_uq, n_uk, n_uv = w_uq.shape[1], w_uk.shape[1], w_uv.shape[1]
    n_all = n_uq + n_uk + n_uv
    own_rows = query_latent.shape[0]
    heads_in = w_uq.shape[0]
    four, heads = heads_in // 2, heads_in // 4

    quarter = tokens // 4
    sequence = lax.axis_index("xh") * 4 + lax.axis_index("xl") * 2 + lax.axis_index("yh")
    place = jnp.stack([zh, yl, core * 2 + zll, core, sequence]).astype(jnp.int32)
    vmem = pl.BlockSpec(memory_space=pltpu.VMEM)
    smem = pl.BlockSpec(memory_space=pltpu.SMEM)
    weights = (w_uq, w_uk, w_uv)
    queries = (query_latent, query_rope)
    latent_chunks = query_latent.shape[1] // lanes
    n_sent = four * n_all + (latent_chunks + 2) * own_rows
    packed = pl.pallas_call(
        pack_kernel,
        out_shape=jax.ShapeDtypeStruct((n_sent, lanes), BF16),
        in_specs=[smem] + [vmem] * 5,
        out_specs=vmem,
        compiler_params=pltpu.CompilerParams(vmem_limit_bytes=VMEM_LIMIT),
        cost_estimate=pl.CostEstimate(flops=10**6, bytes_accessed=10**6, transcendentals=0),
        name="pack",
    )(place, *weights, *queries)
    piece = lax.dynamic_slice_in_dim(cache, (core * 2 + zll) * quarter, quarter, 1)
    far_piece = swap(piece, "zh")
    near = swap(cache, "yl")
    received = swap(packed, "zh")

    vpart, width = w_out.shape[1:]
    columns = width // 8
    w_rows = heads_in * vpart
    n_spread = heads * n_all + columns // lanes * w_rows
    spread = pl.pallas_call(
        spread_kernel,
        out_shape=jax.ShapeDtypeStruct((plane, n_spread, lanes), BF16),
        in_specs=[smem] + [vmem] * 4,
        out_specs=vmem,
        compiler_params=pltpu.CompilerParams(vmem_limit_bytes=VMEM_LIMIT),
        cost_estimate=pl.CostEstimate(flops=10**6, bytes_accessed=10**6, transcendentals=0),
        name="spread",
    )(place, *weights, w_out.reshape(w_rows, width))
    spread = exchange(spread, PLANE)

    n_pack = (2 * latent_chunks + 2) * own_rows
    sent, packed, rope_kept = pl.pallas_call(
        lambda *refs: unpack_kernel(*refs, sizes=(n_all, plane // 2)),
        out_shape=(
            jax.ShapeDtypeStruct((plane // 2, four, n_all, lanes), BF16),
            jax.ShapeDtypeStruct((n_pack, lanes), BF16),
            jax.ShapeDtypeStruct((2 * own_rows, lanes), BF16),
        ),
        in_specs=[smem] + [vmem] * 3,
        out_specs=(vmem,) * 3,
        compiler_params=pltpu.CompilerParams(vmem_limit_bytes=VMEM_LIMIT),
        cost_estimate=pl.CostEstimate(
            flops=UNPACK_FLOPS, bytes_accessed=3 * 10**6, transcendentals=0
        ),
        name="unpack",
    )(place, received, *queries)
    rows = 4 * own_rows
    row_lengths = lengths.reshape(-1, rows)

    piece_y = swap(far_piece, "yl")
    piece_z = swap(far_piece, "zll")
    piece_yz = lax.ppermute(far_piece, ("yl", "zll"), [(0, 3), (1, 2), (2, 1), (3, 0)])
    far = lax.all_gather(jnp.concatenate([far_piece, piece_y], axis=1), "c", axis=0)
    far_z = lax.all_gather(jnp.concatenate([piece_z, piece_yz], axis=1), "c", axis=0)
    sent, spread, far, far_z, near, row_lengths = lax.optimization_barrier(
        (sent, spread, far, far_z, near, row_lengths)
    )

    weights_far = exchange(sent.reshape(plane * heads, n_all, lanes), PLANE)
    weights_far = weights_far.reshape(plane, heads, n_all, lanes)

    packed_y = swap(packed, "yl")

    keep, give = pl.pallas_call(
        lambda *refs: attend_kernel(
            *refs,
            sizes=(rows, heads, n_uq, n_uk, n_uv, latent_width),
            temper=temper,
        ),
        out_shape=(jax.ShapeDtypeStruct((rows, lanes), BF16),) * 2,
        in_specs=[smem] + [vmem] * 10,
        out_specs=(vmem,) * 2,
        scratch_shapes=[
            pltpu.VMEM((rows, query_latent.shape[1]), BF16),
            pltpu.VMEM((rows, lanes), BF16),
            pltpu.VMEM((heads * rows, 4 * tokens), F32),
            pltpu.VMEM((plane, heads, 2, n_all, lanes), BF16),
        ],
        compiler_params=pltpu.CompilerParams(vmem_limit_bytes=VMEM_LIMIT),
        cost_estimate=pl.CostEstimate(flops=10**9, bytes_accessed=5 * 10**6, transcendentals=0),
        name="attend",
    )(place, packed, packed_y, spread, weights_far, rope_kept, row_lengths, cache, near, far, far_z)

    values = ordered(keep, swap(give, "zh"), zh, 1)
    gathered = exchange(
        jnp.broadcast_to(values[None], (8,) + values.shape).reshape(-1, values.shape[1]), PART
    ).reshape((8,) + values.shape)
    shape = (8, 2, own_rows, columns // 2)
    keep, give = pl.pallas_call(
        project_kernel,
        out_shape=(jax.ShapeDtypeStruct(shape, BF16),) * 2,
        in_specs=[smem] + [vmem] * 2,
        out_specs=(vmem,) * 2,
        compiler_params=pltpu.CompilerParams(vmem_limit_bytes=VMEM_LIMIT),
        cost_estimate=pl.CostEstimate(flops=2 * 10**8, bytes_accessed=2 * 10**6, transcendentals=0),
        name="project",
    )(place, gathered, spread)

    total = (keep.astype(F32) + swap(give, "c").astype(F32)).astype(BF16)
    total = jnp.transpose(exchange(total, PART), (1, 0, 2, 3))
    total = exchange(total.reshape((16,) + total.shape[2:]), COLUMN)
    return jnp.sum(total.astype(F32), axis=0).astype(BF16)


def solution(mesh):
    fine = Mesh(mesh.devices.reshape(SIZES), AXES)
    placed = (
        P(FSDP, None),
        P(FSDP, HEAD, None),
        P(),
        P(FSDP, None),
        P(HEAD, FSDP, None),
        P(HEAD, FSDP, None),
        P(HEAD, FSDP, None),
        P(HEAD, FSDP, None),
    )
    return jax.shard_map(
        local, mesh=fine, in_specs=placed, out_specs=P(FSDP, HEAD), check_vma=False
    )
```

```python
import math

import jax
import jax.numpy as jnp
from jax import lax
from jax.experimental import pallas as pl
from jax.experimental.pallas import tpu as pltpu
from jax.sharding import Mesh, PartitionSpec as P

AXES = ("xh", "xl", "yh", "yl", "zh", "zlh", "zll", "c")
SIZES = (2, 2, 2, 2, 2, 4, 2, 2)
FSDP = ("xh", "xl", "yh", "yl", "zh")
HEAD = ("zlh", "zll", "c")
PLANE = ("xh", "xl", "yh", "yl")
PART = ("xl", "yh", "yl")
COLUMN = ("zh", "zlh", "zll")
BF16 = jnp.bfloat16
F32 = jnp.float32
VMEM_LIMIT = 12 * 1024 * 1024
UNPACK_FLOPS = 145 * 10**8


def swap(block, axis):
    return lax.ppermute(block, axis, [(0, 1), (1, 0)])


def ordered(ours, theirs, position, dim):
    return jnp.where(
        position == 1,
        jnp.concatenate([theirs, ours], axis=dim),
        jnp.concatenate([ours, theirs], axis=dim),
    )


def exchange(blocks, axes):
    return lax.all_to_all(blocks, axes, 0, 0, tiled=True)


def dot(a, b):
    return jnp.dot(a, b, preferred_element_type=F32)


def dot_nt(a, b):
    return lax.dot_general(a, b, (((1,), (1,)), ((), ())), preferred_element_type=F32)


def head_pairs(rope):
    return [
        jnp.concatenate([rope[:, 2 * p, :], rope[:, 2 * p + 1, :]], axis=1)
        for p in range(rope.shape[1] // 2)
    ]


def pack_kernel(place, w_uq, w_uk, w_uv, latent, rope, out):
    zh = place[0]
    lanes = out.shape[1]
    at = 0
    four = w_uq.shape[0] // 2
    for h in range(four):
        for w in (w_uq, w_uk, w_uv):
            out[at : at + w.shape[1]] = w[(1 - zh) * four + h]
            at += w.shape[1]
    rows = latent.shape[0]
    for i in range(latent.shape[1] // lanes):
        out[at : at + rows] = latent[:, i * lanes : (i + 1) * lanes]
        at += rows
    pairs = head_pairs(rope)
    for p in range(len(pairs) // 2):
        out[at : at + rows] = jnp.where(zh == 0, pairs[p + len(pairs) // 2], pairs[p])
        at += rows


def spread_kernel(place, w_uq, w_uk, w_uv, w_out, out):
    zh = place[0]
    copies, lanes = out.shape[0], out.shape[2]
    four = w_uq.shape[0] // 2
    for h in range(four):
        at = h % (four // 2) * (w_uq.shape[1] + w_uk.shape[1] + w_uv.shape[1])
        for w in (w_uq, w_uk, w_uv):
            block = w[zh * four + h]
            for copy in range(h // (four // 2), copies, 2):
                out[copy, at : at + w.shape[1]] = block
            at += w.shape[1]
    rows, columns = w_out.shape[0], (out.shape[1] - at) // w_out.shape[0] * lanes
    parts = w_out.shape[1] // columns
    for copy in range(copies):
        begin = copy % parts * columns
        for i in range(columns // lanes):
            block = w_out[:, begin + i * lanes : begin + (i + 1) * lanes]
            out[copy, at + i * rows : at + (i + 1) * rows] = block


def unpack_kernel(
    place, received, latent, rope, sent, packed, rope_out, *, sizes
):
    n_all, copies = sizes
    zh, yl = place[0], place[1]
    own_rows = latent.shape[0]
    lanes = packed.shape[1]
    at = 0
    for h in range(sent.shape[1]):
        other = received[at : at + n_all]
        for copy in range(copies):
            sent[copy, h] = other
        at += n_all
    ours = pl.ds(pl.multiple_of(zh * own_rows, 16), own_rows)
    theirs = pl.ds(pl.multiple_of((1 - zh) * own_rows, 16), own_rows)
    to = 0
    for i in range(latent.shape[1] // lanes):
        packed[pl.ds(pl.multiple_of(to + zh * own_rows, 16), own_rows)] = latent[
            :, i * lanes : (i + 1) * lanes
        ]
        packed[pl.ds(pl.multiple_of(to + (1 - zh) * own_rows, 16), own_rows)] = received[
            at : at + own_rows
        ]
        to += 2 * own_rows
        at += own_rows
    pairs = head_pairs(rope)
    lower = [jnp.where(zh == 0, pairs[0], pairs[2]), received[at : at + own_rows]]
    upper = [jnp.where(zh == 0, pairs[1], pairs[3]), received[at + own_rows : at + 2 * own_rows]]
    stay = [jnp.where(yl == 0, x, y) for x, y in zip(lower, upper)]
    go = [jnp.where(yl == 0, y, x) for x, y in zip(lower, upper)]
    rope_out[ours] = stay[0]
    rope_out[theirs] = stay[1]
    packed[pl.ds(pl.multiple_of(to + zh * own_rows, 16), own_rows)] = go[0]
    packed[pl.ds(pl.multiple_of(to + (1 - zh) * own_rows, 16), own_rows)] = go[1]


def attend_kernel(
    place,
    ours,
    theirs,
    weights_ours,
    weights_theirs,
    rope_ours,
    lengths,
    kv0,
    kv1,
    kv2,
    kv3,
    keep_out,
    give_out,
    query_rows,
    rope,
    scores,
    weights,
    *,
    sizes,
    temper,
):
    rows, heads, n_uq, n_uk, n_uv, width = sizes
    caches = [kv0] + [kv.at[c] for kv in (kv1, kv2, kv3) for c in range(2)]
    spans, tokens = [], 0
    for cache in caches:
        spans.append((tokens, tokens + cache.shape[1]))
        tokens += cache.shape[1]
    zh, yl, core = place[0], place[1], place[3]
    zll = place[2] - core * 2
    quarter = kv0.shape[1] // 4
    starts = []
    for ylo in (yl, 1 - yl):
        for i in range(4):
            starts.append((ylo * 2 + zh) * kv0.shape[1] + i * quarter)
    for zo in (zll, 1 - zll):
        for co in (0, 1):
            for ylo in (yl, 1 - yl):
                starts.append((ylo * 2 + 1 - zh) * kv0.shape[1] + (co * 2 + zo) * quarter)
    n_all = n_uq + n_uk + n_uv
    for h in range(heads):
        weights[:, h, zh] = weights_ours[:, h * n_all : (h + 1) * n_all]
        weights[:, h, 1 - zh] = weights_theirs[:, h]
    chunk = quarter
    half = rows // 2
    mine = pl.ds(pl.multiple_of(yl * half, 16), half)
    other = pl.ds(pl.multiple_of((1 - yl) * half, 16), half)
    at = 0
    lane_count = ours.shape[1]
    for i in range(query_rows.shape[1] // lane_count):
        lanes_here = slice(i * lane_count, (i + 1) * lane_count)
        query_rows[mine, lanes_here] = ours[at : at + half]
        query_rows[other, lanes_here] = theirs[at : at + half]
        at += half
    rope[mine, :] = rope_ours[...]
    rope[other, :] = theirs[at : at + half]
    query = query_rows[...]
    diagonal = lax.broadcasted_iota(jnp.int32, (rows, rows), 0) == lax.broadcasted_iota(
        jnp.int32, (rows, rows), 1
    )
    limit = jnp.sum(
        jnp.where(diagonal, lengths[pl.ds(place[4], 1), :], 0), axis=1, keepdims=True
    )
    limit = jnp.concatenate([limit] * heads, axis=0)
    all_rows = heads * rows
    lanes = lax.broadcasted_iota(jnp.int32, (all_rows, chunk), 1)
    rope_width = kv0.shape[0] - width
    q_lat = []
    for h in range(heads):
        w_uq = weights[:, h, :, 0:n_uq, :].reshape(-1, weights.shape[-1])
        w_uk = weights[:, h, :, n_uq : n_uq + n_uk, :].reshape(-1, weights.shape[-1])
        q_nope = dot(query, w_uq).astype(BF16)
        q_lat.append(dot_nt(q_nope, w_uk).astype(BF16))
    q_lat = jnp.concatenate(q_lat, axis=0)
    q_rope = jnp.concatenate(
        [rope[:, h * rope_width : (h + 1) * rope_width] for h in range(heads)], axis=0
    )
    top = jnp.full((all_rows, 1), -1e30, F32)
    for (begin, end), cache in zip(spans, caches):
        s = dot(q_lat, cache[:width, :]) + dot(q_rope, cache[width:, :])
        s = s * temper
        for k in range(begin // chunk, end // chunk):
            piece = s[:, k * chunk - begin : (k + 1) * chunk - begin]
            piece = jnp.where(lanes + starts[k] < limit, piece, -1e30)
            top = jnp.maximum(top, jnp.max(piece, axis=1, keepdims=True))
            scores[:, k * chunk : (k + 1) * chunk] = piece
    total = jnp.zeros((all_rows, 1), F32)
    context = jnp.zeros((all_rows, width), F32)
    for (begin, end), cache in zip(spans, caches):
        p = jnp.exp(scores[:, begin:end] - top)
        total = total + jnp.sum(p, axis=1, keepdims=True)
        context = context + dot_nt(p.astype(BF16), cache[:width, :])
    context = (context / total).astype(BF16)
    values = []
    for h in range(heads):
        w_uv = weights[:, h, :, n_uq + n_uk :, :].reshape(-1, weights.shape[-1])
        values.append(dot(context[h * rows : (h + 1) * rows], w_uv).astype(BF16))
    vdim = values[0].shape[1]
    wide = heads * vdim
    to = lax.broadcasted_iota(jnp.int32, (wide, wide), 1)
    source = lax.broadcasted_iota(jnp.int32, (wide, wide), 0)
    side = to // (wide // 2)
    head = to % (wide // 2) // (vdim // 2)
    item = to % (vdim // 2)
    wanted = head * vdim + item // 4 * 8 + jnp.where(side == 0, zh, 1 - zh) * 4 + item % 4
    move = jnp.where(source == wanted, 1.0, 0.0).astype(BF16)
    moved = dot(jnp.concatenate(values, axis=1), move).astype(BF16)
    keep_out[...] = moved[:, : wide // 2]
    give_out[...] = moved[:, wide // 2 :]


def project_kernel(place, values, received, keep_out, give_out):
    core = place[3]
    lanes = received.shape[2]
    rows = [
        jnp.concatenate([values[i], values[i + 1]], axis=1) for i in range(0, values.shape[0], 2)
    ]
    rows = jnp.concatenate(rows, axis=0)
    depth = rows.shape[1]
    source = lax.broadcasted_iota(jnp.int32, (depth, depth), 0)
    to = lax.broadcasted_iota(jnp.int32, (depth, depth), 1)
    y, z, j = source // 256, source // 128 % 2, source // 64 % 2
    wanted = source // 4 % 16 * 32 + (z * 4 + y * 2 + j) * 4 + source % 4
    order = jnp.where(to == wanted, 1.0, 0.0).astype(BF16)
    rows = dot(rows, order).astype(BF16)
    each = depth // received.shape[0]
    columns = keep_out.shape[-1]
    count = 2 * columns // lanes
    first = received.shape[1] - count * each
    weights = jnp.concatenate(
        [
            received[:, at : at + each].reshape(depth, lanes)
            for at in range(first, received.shape[1], each)
        ],
        axis=1,
    )
    part = dot(rows, weights)
    even, odd = part[:, :columns], part[:, columns:]
    keep_out[...] = jnp.where(core == 0, even, odd).astype(BF16).reshape(keep_out.shape)
    give_out[...] = jnp.where(core == 0, odd, even).astype(BF16).reshape(give_out.shape)


def local(query_latent, query_rope, lengths, kv_cache, w_uq, w_uk, w_uv, w_out):
    yl, zh, zll, core = (lax.axis_index(a) for a in ("yl", "zh", "zll", "c"))
    plane = 16
    cache = kv_cache.T
    kv_width, tokens = cache.shape
    latent_width = w_uk.shape[1] * 32
    rope_width = kv_width - latent_width
    lanes = w_uq.shape[2]
    temper = 1.0 / math.sqrt(lanes + rope_width)
    n_uq, n_uk, n_uv = w_uq.shape[1], w_uk.shape[1], w_uv.shape[1]
    n_all = n_uq + n_uk + n_uv
    own_rows = query_latent.shape[0]
    heads_in = w_uq.shape[0]
    four, heads = heads_in // 2, heads_in // 4

    quarter = tokens // 4
    sequence = lax.axis_index("xh") * 4 + lax.axis_index("xl") * 2 + lax.axis_index("yh")
    place = jnp.stack([zh, yl, core * 2 + zll, core, sequence]).astype(jnp.int32)
    vmem = pl.BlockSpec(memory_space=pltpu.VMEM)
    smem = pl.BlockSpec(memory_space=pltpu.SMEM)
    weights = (w_uq, w_uk, w_uv)
    queries = (query_latent, query_rope)
    latent_chunks = query_latent.shape[1] // lanes
    n_sent = four * n_all + (latent_chunks + 2) * own_rows
    packed = pl.pallas_call(
        pack_kernel,
        out_shape=jax.ShapeDtypeStruct((n_sent, lanes), BF16),
        in_specs=[smem] + [vmem] * 5,
        out_specs=vmem,
        compiler_params=pltpu.CompilerParams(vmem_limit_bytes=VMEM_LIMIT),
        cost_estimate=pl.CostEstimate(flops=10**6, bytes_accessed=10**6, transcendentals=0),
        name="pack",
    )(place, *weights, *queries)
    piece = lax.dynamic_slice_in_dim(cache, (core * 2 + zll) * quarter, quarter, 1)
    far_piece = swap(piece, "zh")
    near = swap(lax.dynamic_slice_in_dim(cache, core * (tokens // 2), tokens // 2, 1), "yl")
    near, w_out = lax.optimization_barrier((near, w_out))
    received = swap(packed, "zh")

    vpart, width = w_out.shape[1:]
    columns = width // 8
    w_rows = heads_in * vpart
    n_spread = heads * n_all + columns // lanes * w_rows
    spread = pl.pallas_call(
        spread_kernel,
        out_shape=jax.ShapeDtypeStruct((plane, n_spread, lanes), BF16),
        in_specs=[smem] + [vmem] * 4,
        out_specs=vmem,
        compiler_params=pltpu.CompilerParams(vmem_limit_bytes=VMEM_LIMIT),
        cost_estimate=pl.CostEstimate(flops=10**6, bytes_accessed=10**6, transcendentals=0),
        name="spread",
    )(place, *weights, w_out.reshape(w_rows, width))
    spread = exchange(spread, PLANE)

    n_pack = (2 * latent_chunks + 2) * own_rows
    sent, packed, rope_kept = pl.pallas_call(
        lambda *refs: unpack_kernel(*refs, sizes=(n_all, plane // 2)),
        out_shape=(
            jax.ShapeDtypeStruct((plane // 2, four, n_all, lanes), BF16),
            jax.ShapeDtypeStruct((n_pack, lanes), BF16),
            jax.ShapeDtypeStruct((2 * own_rows, lanes), BF16),
        ),
        in_specs=[smem] + [vmem] * 3,
        out_specs=(vmem,) * 3,
        compiler_params=pltpu.CompilerParams(vmem_limit_bytes=VMEM_LIMIT),
        cost_estimate=pl.CostEstimate(
            flops=UNPACK_FLOPS, bytes_accessed=3 * 10**6, transcendentals=0
        ),
        name="unpack",
    )(place, received, *queries)
    rows = 4 * own_rows
    row_lengths = lengths.reshape(-1, rows)

    piece_y = swap(far_piece, "yl")
    piece_z = swap(far_piece, "zll")
    piece_yz = lax.ppermute(far_piece, ("yl", "zll"), [(0, 3), (1, 2), (2, 1), (3, 0)])
    sent, spread, piece_y, piece_z, piece_yz, row_lengths = lax.optimization_barrier(
        (sent, spread, piece_y, piece_z, piece_yz, row_lengths)
    )

    weights_far = exchange(sent.reshape(plane * heads, n_all, lanes), PLANE)
    weights_far = weights_far.reshape(plane, heads, n_all, lanes)

    near = lax.all_gather(near, "c", axis=0)
    far = lax.all_gather(jnp.concatenate([far_piece, piece_y], axis=1), "c", axis=0)
    far_z = lax.all_gather(jnp.concatenate([piece_z, piece_yz], axis=1), "c", axis=0)

    packed_y = swap(packed, "yl")

    keep, give = pl.pallas_call(
        lambda *refs: attend_kernel(
            *refs,
            sizes=(rows, heads, n_uq, n_uk, n_uv, latent_width),
            temper=temper,
        ),
        out_shape=(jax.ShapeDtypeStruct((rows, lanes), BF16),) * 2,
        in_specs=[smem] + [vmem] * 10,
        out_specs=(vmem,) * 2,
        scratch_shapes=[
            pltpu.VMEM((rows, query_latent.shape[1]), BF16),
            pltpu.VMEM((rows, lanes), BF16),
            pltpu.VMEM((heads * rows, 4 * tokens), F32),
            pltpu.VMEM((plane, heads, 2, n_all, lanes), BF16),
        ],
        compiler_params=pltpu.CompilerParams(vmem_limit_bytes=VMEM_LIMIT),
        cost_estimate=pl.CostEstimate(flops=10**9, bytes_accessed=5 * 10**6, transcendentals=0),
        name="attend",
    )(place, packed, packed_y, spread, weights_far, rope_kept, row_lengths, cache, near, far, far_z)

    values = ordered(keep, swap(give, "zh"), zh, 1)
    gathered = exchange(
        jnp.broadcast_to(values[None], (8,) + values.shape).reshape(-1, values.shape[1]), PART
    ).reshape((8,) + values.shape)
    shape = (8, 2, own_rows, columns // 2)
    keep, give = pl.pallas_call(
        project_kernel,
        out_shape=(jax.ShapeDtypeStruct(shape, BF16),) * 2,
        in_specs=[smem] + [vmem] * 2,
        out_specs=(vmem,) * 2,
        compiler_params=pltpu.CompilerParams(vmem_limit_bytes=VMEM_LIMIT),
        cost_estimate=pl.CostEstimate(flops=2 * 10**8, bytes_accessed=2 * 10**6, transcendentals=0),
        name="project",
    )(place, gathered, spread)

    total = (keep.astype(F32) + swap(give, "c").astype(F32)).astype(BF16)
    total = jnp.transpose(exchange(total, PART), (1, 0, 2, 3))
    total = exchange(total.reshape((16,) + total.shape[2:]), COLUMN)
    return jnp.sum(total.astype(F32), axis=0).astype(BF16)


def solution(mesh):
    fine = Mesh(mesh.devices.reshape(SIZES), AXES)
    placed = (
        P(FSDP, None),
        P(FSDP, HEAD, None),
        P(),
        P(FSDP, None),
        P(HEAD, FSDP, None),
        P(HEAD, FSDP, None),
        P(HEAD, FSDP, None),
        P(HEAD, FSDP, None),
    )
    return jax.shard_map(
        local, mesh=fine, in_specs=placed, out_specs=P(FSDP, HEAD), check_vma=False
    )
```

```python
import math

import jax
import jax.numpy as jnp
from jax import lax
from jax.experimental import pallas as pl
from jax.experimental.pallas import tpu as pltpu
from jax.sharding import Mesh, PartitionSpec as P

AXES = ("xh", "xl", "yh", "yl", "zh", "zlh", "zll", "c")
SIZES = (2, 2, 2, 2, 2, 4, 2, 2)
FSDP = ("xh", "xl", "yh", "yl", "zh")
HEAD = ("zlh", "zll", "c")
PLANE = ("xh", "xl", "yh", "yl")
PART = ("xl", "yh", "yl")
COLUMN = ("zh", "zlh", "zll")
BF16 = jnp.bfloat16
F32 = jnp.float32
VMEM_LIMIT = 12 * 1024 * 1024
UNPACK_FLOPS = 139 * 10**8
HOLD_FLOPS = 4 * 10**9


def swap(block, axis):
    return lax.ppermute(block, axis, [(0, 1), (1, 0)])


def ordered(ours, theirs, position, dim):
    return jnp.where(
        position == 1,
        jnp.concatenate([theirs, ours], axis=dim),
        jnp.concatenate([ours, theirs], axis=dim),
    )


def exchange(blocks, axes):
    return lax.all_to_all(blocks, axes, 0, 0, tiled=True)


def dot(a, b):
    return jnp.dot(a, b, preferred_element_type=F32)


def dot_nt(a, b):
    return lax.dot_general(a, b, (((1,), (1,)), ((), ())), preferred_element_type=F32)


def head_pairs(rope):
    return [
        jnp.concatenate([rope[:, 2 * p, :], rope[:, 2 * p + 1, :]], axis=1)
        for p in range(rope.shape[1] // 2)
    ]


def pack_kernel(place, w_uq, w_uk, w_uv, latent, rope, out):
    zh = place[0]
    lanes = out.shape[1]
    at = 0
    four = w_uq.shape[0] // 2
    for h in range(four):
        for w in (w_uq, w_uk, w_uv):
            out[at : at + w.shape[1]] = w[(1 - zh) * four + h]
            at += w.shape[1]
    rows = latent.shape[0]
    for i in range(latent.shape[1] // lanes):
        out[at : at + rows] = latent[:, i * lanes : (i + 1) * lanes]
        at += rows
    pairs = head_pairs(rope)
    for p in range(len(pairs) // 2):
        out[at : at + rows] = jnp.where(zh == 0, pairs[p + len(pairs) // 2], pairs[p])
        at += rows


def spread_kernel(place, w_uq, w_uk, w_uv, w_out, out):
    zh = place[0]
    copies, lanes = out.shape[0], out.shape[2]
    four = w_uq.shape[0] // 2
    for h in range(four):
        at = h % (four // 2) * (w_uq.shape[1] + w_uk.shape[1] + w_uv.shape[1])
        for w in (w_uq, w_uk, w_uv):
            block = w[zh * four + h]
            for copy in range(h // (four // 2), copies, 2):
                out[copy, at : at + w.shape[1]] = block
            at += w.shape[1]
    rows, columns = w_out.shape[0], (out.shape[1] - at) // w_out.shape[0] * lanes
    parts = w_out.shape[1] // columns
    for copy in range(copies):
        begin = copy % parts * columns
        for i in range(columns // lanes):
            block = w_out[:, begin + i * lanes : begin + (i + 1) * lanes]
            out[copy, at + i * rows : at + (i + 1) * rows] = block


def unpack_kernel(
    place, received, latent, rope, sent, packed, rope_out, *, sizes
):
    n_all, copies = sizes
    zh, yl = place[0], place[1]
    own_rows = latent.shape[0]
    lanes = packed.shape[1]
    at = 0
    for h in range(sent.shape[1]):
        other = received[at : at + n_all]
        for copy in range(copies):
            sent[copy, h] = other
        at += n_all
    ours = pl.ds(pl.multiple_of(zh * own_rows, 16), own_rows)
    theirs = pl.ds(pl.multiple_of((1 - zh) * own_rows, 16), own_rows)
    to = 0
    for i in range(latent.shape[1] // lanes):
        packed[pl.ds(pl.multiple_of(to + zh * own_rows, 16), own_rows)] = latent[
            :, i * lanes : (i + 1) * lanes
        ]
        packed[pl.ds(pl.multiple_of(to + (1 - zh) * own_rows, 16), own_rows)] = received[
            at : at + own_rows
        ]
        to += 2 * own_rows
        at += own_rows
    pairs = head_pairs(rope)
    lower = [jnp.where(zh == 0, pairs[0], pairs[2]), received[at : at + own_rows]]
    upper = [jnp.where(zh == 0, pairs[1], pairs[3]), received[at + own_rows : at + 2 * own_rows]]
    stay = [jnp.where(yl == 0, x, y) for x, y in zip(lower, upper)]
    go = [jnp.where(yl == 0, y, x) for x, y in zip(lower, upper)]
    rope_out[ours] = stay[0]
    rope_out[theirs] = stay[1]
    packed[pl.ds(pl.multiple_of(to + zh * own_rows, 16), own_rows)] = go[0]
    packed[pl.ds(pl.multiple_of(to + (1 - zh) * own_rows, 16), own_rows)] = go[1]


def hold_kernel(piece, out):
    out[...] = piece[...]


def attend_kernel(
    place,
    ours,
    theirs,
    weights_ours,
    weights_theirs,
    rope_ours,
    lengths,
    kv0,
    kv1,
    kv2,
    kv3,
    keep_out,
    give_out,
    query_rows,
    rope,
    scores,
    weights,
    *,
    sizes,
    temper,
):
    rows, heads, n_uq, n_uk, n_uv, width = sizes
    caches = [kv0] + [kv.at[c] for kv in (kv1, kv2, kv3) for c in range(2)]
    spans, tokens = [], 0
    for cache in caches:
        spans.append((tokens, tokens + cache.shape[1]))
        tokens += cache.shape[1]
    zh, yl, core = place[0], place[1], place[3]
    zll = place[2] - core * 2
    quarter = kv0.shape[1] // 4
    starts = []
    for ylo in (yl, 1 - yl):
        for i in range(4):
            starts.append((ylo * 2 + zh) * kv0.shape[1] + i * quarter)
    for zo in (zll, 1 - zll):
        for co in (0, 1):
            for ylo in (yl, 1 - yl):
                starts.append((ylo * 2 + 1 - zh) * kv0.shape[1] + (co * 2 + zo) * quarter)
    n_all = n_uq + n_uk + n_uv
    for h in range(heads):
        weights[:, h, zh] = weights_ours[:, h * n_all : (h + 1) * n_all]
        weights[:, h, 1 - zh] = weights_theirs[:, h]
    chunk = quarter
    half = rows // 2
    mine = pl.ds(pl.multiple_of(yl * half, 16), half)
    other = pl.ds(pl.multiple_of((1 - yl) * half, 16), half)
    at = 0
    lane_count = ours.shape[1]
    for i in range(query_rows.shape[1] // lane_count):
        lanes_here = slice(i * lane_count, (i + 1) * lane_count)
        query_rows[mine, lanes_here] = ours[at : at + half]
        query_rows[other, lanes_here] = theirs[at : at + half]
        at += half
    rope[mine, :] = rope_ours[...]
    rope[other, :] = theirs[at : at + half]
    query = query_rows[...]
    diagonal = lax.broadcasted_iota(jnp.int32, (rows, rows), 0) == lax.broadcasted_iota(
        jnp.int32, (rows, rows), 1
    )
    limit = jnp.sum(
        jnp.where(diagonal, lengths[pl.ds(place[4], 1), :], 0), axis=1, keepdims=True
    )
    limit = jnp.concatenate([limit] * heads, axis=0)
    all_rows = heads * rows
    lanes = lax.broadcasted_iota(jnp.int32, (all_rows, chunk), 1)
    rope_width = kv0.shape[0] - width
    q_lat = []
    for h in range(heads):
        w_uq = weights[:, h, :, 0:n_uq, :].reshape(-1, weights.shape[-1])
        w_uk = weights[:, h, :, n_uq : n_uq + n_uk, :].reshape(-1, weights.shape[-1])
        q_nope = dot(query, w_uq).astype(BF16)
        q_lat.append(dot_nt(q_nope, w_uk).astype(BF16))
    q_lat = jnp.concatenate(q_lat, axis=0)
    q_rope = jnp.concatenate(
        [rope[:, h * rope_width : (h + 1) * rope_width] for h in range(heads)], axis=0
    )
    top = jnp.full((all_rows, 1), -1e30, F32)
    for (begin, end), cache in zip(spans, caches):
        s = dot(q_lat, cache[:width, :]) + dot(q_rope, cache[width:, :])
        s = s * temper
        for k in range(begin // chunk, end // chunk):
            piece = s[:, k * chunk - begin : (k + 1) * chunk - begin]
            piece = jnp.where(lanes + starts[k] < limit, piece, -1e30)
            top = jnp.maximum(top, jnp.max(piece, axis=1, keepdims=True))
            scores[:, k * chunk : (k + 1) * chunk] = piece
    total = jnp.zeros((all_rows, 1), F32)
    context = jnp.zeros((all_rows, width), F32)
    for (begin, end), cache in zip(spans, caches):
        p = jnp.exp(scores[:, begin:end] - top)
        total = total + jnp.sum(p, axis=1, keepdims=True)
        context = context + dot_nt(p.astype(BF16), cache[:width, :])
    context = (context / total).astype(BF16)
    values = []
    for h in range(heads):
        w_uv = weights[:, h, :, n_uq + n_uk :, :].reshape(-1, weights.shape[-1])
        values.append(dot(context[h * rows : (h + 1) * rows], w_uv).astype(BF16))
    vdim = values[0].shape[1]
    wide = heads * vdim
    to = lax.broadcasted_iota(jnp.int32, (wide, wide), 1)
    source = lax.broadcasted_iota(jnp.int32, (wide, wide), 0)
    side = to // (wide // 2)
    head = to % (wide // 2) // (vdim // 2)
    item = to % (vdim // 2)
    wanted = head * vdim + item // 4 * 8 + jnp.where(side == 0, zh, 1 - zh) * 4 + item % 4
    move = jnp.where(source == wanted, 1.0, 0.0).astype(BF16)
    moved = dot(jnp.concatenate(values, axis=1), move).astype(BF16)
    keep_out[...] = moved[:, : wide // 2]
    give_out[...] = moved[:, wide // 2 :]


def project_kernel(place, values, received, keep_out, give_out):
    core = place[3]
    lanes = received.shape[2]
    rows = [
        jnp.concatenate([values[i], values[i + 1]], axis=1) for i in range(0, values.shape[0], 2)
    ]
    rows = jnp.concatenate(rows, axis=0)
    depth = rows.shape[1]
    source = lax.broadcasted_iota(jnp.int32, (depth, depth), 0)
    to = lax.broadcasted_iota(jnp.int32, (depth, depth), 1)
    y, z, j = source // 256, source // 128 % 2, source // 64 % 2
    wanted = source // 4 % 16 * 32 + (z * 4 + y * 2 + j) * 4 + source % 4
    order = jnp.where(to == wanted, 1.0, 0.0).astype(BF16)
    rows = dot(rows, order).astype(BF16)
    each = depth // received.shape[0]
    columns = keep_out.shape[-1]
    count = 2 * columns // lanes
    first = received.shape[1] - count * each
    weights = jnp.concatenate(
        [
            received[:, at : at + each].reshape(depth, lanes)
            for at in range(first, received.shape[1], each)
        ],
        axis=1,
    )
    part = dot(rows, weights)
    even, odd = part[:, :columns], part[:, columns:]
    keep_out[...] = jnp.where(core == 0, even, odd).astype(BF16).reshape(keep_out.shape)
    give_out[...] = jnp.where(core == 0, odd, even).astype(BF16).reshape(give_out.shape)


def local(query_latent, query_rope, lengths, kv_cache, w_uq, w_uk, w_uv, w_out):
    yl, zh, zll, core = (lax.axis_index(a) for a in ("yl", "zh", "zll", "c"))
    plane = 16
    cache = kv_cache.T
    kv_width, tokens = cache.shape
    latent_width = w_uk.shape[1] * 32
    rope_width = kv_width - latent_width
    lanes = w_uq.shape[2]
    temper = 1.0 / math.sqrt(lanes + rope_width)
    n_uq, n_uk, n_uv = w_uq.shape[1], w_uk.shape[1], w_uv.shape[1]
    n_all = n_uq + n_uk + n_uv
    own_rows = query_latent.shape[0]
    heads_in = w_uq.shape[0]
    four, heads = heads_in // 2, heads_in // 4

    quarter = tokens // 4
    sequence = lax.axis_index("xh") * 4 + lax.axis_index("xl") * 2 + lax.axis_index("yh")
    place = jnp.stack([zh, yl, core * 2 + zll, core, sequence]).astype(jnp.int32)
    vmem = pl.BlockSpec(memory_space=pltpu.VMEM)
    smem = pl.BlockSpec(memory_space=pltpu.SMEM)
    weights = (w_uq, w_uk, w_uv)
    queries = (query_latent, query_rope)
    latent_chunks = query_latent.shape[1] // lanes
    n_sent = four * n_all + (latent_chunks + 2) * own_rows
    piece = lax.dynamic_slice_in_dim(cache, (core * 2 + zll) * quarter, quarter, 1)
    far_piece = swap(piece, "zh")
    near = swap(lax.dynamic_slice_in_dim(cache, core * (tokens // 2), tokens // 2, 1), "yl")
    near, w_out = lax.optimization_barrier((near, w_out))

    vpart, width = w_out.shape[1:]
    columns = width // 8
    w_rows = heads_in * vpart
    n_spread = heads * n_all + columns // lanes * w_rows
    spread = pl.pallas_call(
        spread_kernel,
        out_shape=jax.ShapeDtypeStruct((plane, n_spread, lanes), BF16),
        in_specs=[smem] + [vmem] * 4,
        out_specs=vmem,
        compiler_params=pltpu.CompilerParams(vmem_limit_bytes=VMEM_LIMIT),
        cost_estimate=pl.CostEstimate(flops=10**6, bytes_accessed=10**6, transcendentals=0),
        name="spread",
    )(place, *weights, w_out.reshape(w_rows, width))
    queries_after, spread = lax.optimization_barrier((query_latent, spread))
    spread = exchange(spread, PLANE)
    packed = pl.pallas_call(
        pack_kernel,
        out_shape=jax.ShapeDtypeStruct((n_sent, lanes), BF16),
        in_specs=[smem] + [vmem] * 5,
        out_specs=vmem,
        compiler_params=pltpu.CompilerParams(vmem_limit_bytes=VMEM_LIMIT),
        cost_estimate=pl.CostEstimate(flops=10**6, bytes_accessed=10**6, transcendentals=0),
        name="pack",
    )(place, *weights, queries_after, query_rope)
    received = swap(packed, "zh")

    n_pack = (2 * latent_chunks + 2) * own_rows
    sent, packed, rope_kept = pl.pallas_call(
        lambda *refs: unpack_kernel(*refs, sizes=(n_all, plane // 2)),
        out_shape=(
            jax.ShapeDtypeStruct((plane // 2, four, n_all, lanes), BF16),
            jax.ShapeDtypeStruct((n_pack, lanes), BF16),
            jax.ShapeDtypeStruct((2 * own_rows, lanes), BF16),
        ),
        in_specs=[smem] + [vmem] * 3,
        out_specs=(vmem,) * 3,
        compiler_params=pltpu.CompilerParams(vmem_limit_bytes=VMEM_LIMIT),
        cost_estimate=pl.CostEstimate(
            flops=UNPACK_FLOPS, bytes_accessed=3 * 10**6, transcendentals=0
        ),
        name="unpack",
    )(place, received, *queries)
    rows = 4 * own_rows
    row_lengths = lengths.reshape(-1, rows)

    far_piece = pl.pallas_call(
        hold_kernel,
        out_shape=jax.ShapeDtypeStruct(far_piece.shape, BF16),
        in_specs=[vmem],
        out_specs=vmem,
        compiler_params=pltpu.CompilerParams(vmem_limit_bytes=VMEM_LIMIT),
        cost_estimate=pl.CostEstimate(flops=HOLD_FLOPS, bytes_accessed=10**6, transcendentals=0),
        name="hold",
    )(far_piece)
    piece_y = swap(far_piece, "yl")
    piece_z = swap(far_piece, "zll")
    piece_yz = lax.ppermute(far_piece, ("yl", "zll"), [(0, 3), (1, 2), (2, 1), (3, 0)])
    sent, spread, piece_y, piece_z, piece_yz, row_lengths = lax.optimization_barrier(
        (sent, spread, piece_y, piece_z, piece_yz, row_lengths)
    )

    weights_far = exchange(sent.reshape(plane * heads, n_all, lanes), PLANE)
    weights_far = weights_far.reshape(plane, heads, n_all, lanes)

    near = lax.all_gather(near, "c", axis=0)
    far = lax.all_gather(jnp.concatenate([far_piece, piece_y], axis=1), "c", axis=0)
    far_z = lax.all_gather(jnp.concatenate([piece_z, piece_yz], axis=1), "c", axis=0)

    packed_y = swap(packed, "yl")

    keep, give = pl.pallas_call(
        lambda *refs: attend_kernel(
            *refs,
            sizes=(rows, heads, n_uq, n_uk, n_uv, latent_width),
            temper=temper,
        ),
        out_shape=(jax.ShapeDtypeStruct((rows, lanes), BF16),) * 2,
        in_specs=[smem] + [vmem] * 10,
        out_specs=(vmem,) * 2,
        scratch_shapes=[
            pltpu.VMEM((rows, query_latent.shape[1]), BF16),
            pltpu.VMEM((rows, lanes), BF16),
            pltpu.VMEM((heads * rows, 4 * tokens), F32),
            pltpu.VMEM((plane, heads, 2, n_all, lanes), BF16),
        ],
        compiler_params=pltpu.CompilerParams(vmem_limit_bytes=VMEM_LIMIT),
        cost_estimate=pl.CostEstimate(flops=10**9, bytes_accessed=5 * 10**6, transcendentals=0),
        name="attend",
    )(place, packed, packed_y, spread, weights_far, rope_kept, row_lengths, cache, near, far, far_z)

    values = ordered(keep, swap(give, "zh"), zh, 1)
    gathered = exchange(
        jnp.broadcast_to(values[None], (8,) + values.shape).reshape(-1, values.shape[1]), PART
    ).reshape((8,) + values.shape)
    shape = (8, 2, own_rows, columns // 2)
    keep, give = pl.pallas_call(
        project_kernel,
        out_shape=(jax.ShapeDtypeStruct(shape, BF16),) * 2,
        in_specs=[smem] + [vmem] * 2,
        out_specs=(vmem,) * 2,
        compiler_params=pltpu.CompilerParams(vmem_limit_bytes=VMEM_LIMIT),
        cost_estimate=pl.CostEstimate(flops=2 * 10**8, bytes_accessed=2 * 10**6, transcendentals=0),
        name="project",
    )(place, gathered, spread)

    total = (keep.astype(F32) + swap(give, "c").astype(F32)).astype(BF16)
    total = jnp.transpose(exchange(total, PART), (1, 0, 2, 3))
    total = exchange(total.reshape((16,) + total.shape[2:]), COLUMN)
    return jnp.sum(total.astype(F32), axis=0).astype(BF16)


def solution(mesh):
    fine = Mesh(mesh.devices.reshape(SIZES), AXES)
    placed = (
        P(FSDP, None),
        P(FSDP, HEAD, None),
        P(),
        P(FSDP, None),
        P(HEAD, FSDP, None),
        P(HEAD, FSDP, None),
        P(HEAD, FSDP, None),
        P(HEAD, FSDP, None),
    )
    return jax.shard_map(
        local, mesh=fine, in_specs=placed, out_specs=P(FSDP, HEAD), check_vma=False
    )
```

```python
import math

import jax
import jax.numpy as jnp
from jax import lax
from jax.experimental import pallas as pl
from jax.experimental.pallas import tpu as pltpu
from jax.sharding import Mesh, PartitionSpec as P

AXES = ("xh", "xl", "yh", "yl", "zh", "zlh", "zll", "c")
SIZES = (2, 2, 2, 2, 2, 4, 2, 2)
FSDP = ("xh", "xl", "yh", "yl", "zh")
HEAD = ("zlh", "zll", "c")
PLANE = ("xh", "xl", "yh", "yl")
PART = ("xl", "yh", "yl")
COLUMN = ("zh", "zlh", "zll")
BF16 = jnp.bfloat16
F32 = jnp.float32
VMEM_LIMIT = 12 * 1024 * 1024
UNPACK_FLOPS = 139 * 10**8
HOLD_FLOPS = 4 * 10**9


def swap(block, axis):
    return lax.ppermute(block, axis, [(0, 1), (1, 0)])


def ordered(ours, theirs, position, dim):
    return jnp.where(
        position == 1,
        jnp.concatenate([theirs, ours], axis=dim),
        jnp.concatenate([ours, theirs], axis=dim),
    )


def exchange(blocks, axes):
    return lax.all_to_all(blocks, axes, 0, 0, tiled=True)


def dot(a, b):
    return jnp.dot(a, b, preferred_element_type=F32)


def dot_nt(a, b):
    return lax.dot_general(a, b, (((1,), (1,)), ((), ())), preferred_element_type=F32)


def head_pairs(rope):
    return [
        jnp.concatenate([rope[:, 2 * p, :], rope[:, 2 * p + 1, :]], axis=1)
        for p in range(rope.shape[1] // 2)
    ]


def pack_kernel(place, w_uq, w_uk, w_uv, latent, rope, out):
    zh = place[0]
    lanes = out.shape[1]
    at = 0
    four = w_uq.shape[0] // 2
    for h in range(four):
        for w in (w_uq, w_uk, w_uv):
            out[at : at + w.shape[1]] = w[(1 - zh) * four + h]
            at += w.shape[1]
    rows = latent.shape[0]
    for i in range(latent.shape[1] // lanes):
        out[at : at + rows] = latent[:, i * lanes : (i + 1) * lanes]
        at += rows
    pairs = head_pairs(rope)
    for p in range(len(pairs) // 2):
        out[at : at + rows] = jnp.where(zh == 0, pairs[p + len(pairs) // 2], pairs[p])
        at += rows


def spread_kernel(place, w_uq, w_uk, w_uv, w_out, out):
    zh = place[0]
    copies, lanes = out.shape[0], out.shape[2]
    four = w_uq.shape[0] // 2
    for h in range(four):
        at = h % (four // 2) * (w_uq.shape[1] + w_uk.shape[1] + w_uv.shape[1])
        for w in (w_uq, w_uk, w_uv):
            block = w[zh * four + h]
            for copy in range(h // (four // 2), copies, 2):
                out[copy, at : at + w.shape[1]] = block
            at += w.shape[1]
    rows, columns = w_out.shape[0], (out.shape[1] - at) // w_out.shape[0] * lanes
    parts = w_out.shape[1] // columns
    for copy in range(copies):
        begin = copy % parts * columns
        for i in range(columns // lanes):
            block = w_out[:, begin + i * lanes : begin + (i + 1) * lanes]
            out[copy, at + i * rows : at + (i + 1) * rows] = block


def unpack_kernel(
    place, received, latent, rope, sent, packed, rope_out, *, sizes
):
    n_all, copies = sizes
    zh, yl = place[0], place[1]
    own_rows = latent.shape[0]
    lanes = packed.shape[1]
    at = 0
    for h in range(sent.shape[1]):
        other = received[at : at + n_all]
        for copy in range(copies):
            sent[copy, h] = other
        at += n_all
    ours = pl.ds(pl.multiple_of(zh * own_rows, 16), own_rows)
    theirs = pl.ds(pl.multiple_of((1 - zh) * own_rows, 16), own_rows)
    to = 0
    for i in range(latent.shape[1] // lanes):
        packed[pl.ds(pl.multiple_of(to + zh * own_rows, 16), own_rows)] = latent[
            :, i * lanes : (i + 1) * lanes
        ]
        packed[pl.ds(pl.multiple_of(to + (1 - zh) * own_rows, 16), own_rows)] = received[
            at : at + own_rows
        ]
        to += 2 * own_rows
        at += own_rows
    pairs = head_pairs(rope)
    lower = [jnp.where(zh == 0, pairs[0], pairs[2]), received[at : at + own_rows]]
    upper = [jnp.where(zh == 0, pairs[1], pairs[3]), received[at + own_rows : at + 2 * own_rows]]
    stay = [jnp.where(yl == 0, x, y) for x, y in zip(lower, upper)]
    go = [jnp.where(yl == 0, y, x) for x, y in zip(lower, upper)]
    rope_out[ours] = stay[0]
    rope_out[theirs] = stay[1]
    packed[pl.ds(pl.multiple_of(to + zh * own_rows, 16), own_rows)] = go[0]
    packed[pl.ds(pl.multiple_of(to + (1 - zh) * own_rows, 16), own_rows)] = go[1]


def hold_kernel(piece, out):
    out[...] = piece[...]


def attend_kernel(
    place,
    ours,
    theirs,
    weights_ours,
    weights_theirs,
    rope_ours,
    lengths,
    kv0,
    kv1,
    kv2,
    kv3,
    keep_out,
    give_out,
    query_rows,
    rope,
    scores,
    weights,
    *,
    sizes,
    temper,
):
    rows, heads, n_uq, n_uk, n_uv, width = sizes
    caches = [kv0] + [kv.at[c] for kv in (kv1, kv2, kv3) for c in range(2)]
    spans, tokens = [], 0
    for cache in caches:
        spans.append((tokens, tokens + cache.shape[1]))
        tokens += cache.shape[1]
    zh, yl, core = place[0], place[1], place[3]
    zll = place[2] - core * 2
    quarter = kv0.shape[1] // 4
    starts = []
    for ylo in (yl, 1 - yl):
        for i in range(4):
            starts.append((ylo * 2 + zh) * kv0.shape[1] + i * quarter)
    for zo in (zll, 1 - zll):
        for co in (0, 1):
            for ylo in (yl, 1 - yl):
                starts.append((ylo * 2 + 1 - zh) * kv0.shape[1] + (co * 2 + zo) * quarter)
    n_all = n_uq + n_uk + n_uv
    for h in range(heads):
        weights[:, h, zh] = weights_ours[:, h * n_all : (h + 1) * n_all]
        weights[:, h, 1 - zh] = weights_theirs[:, h]
    chunk = quarter
    half = rows // 2
    mine = pl.ds(pl.multiple_of(yl * half, 16), half)
    other = pl.ds(pl.multiple_of((1 - yl) * half, 16), half)
    at = 0
    lane_count = ours.shape[1]
    for i in range(query_rows.shape[1] // lane_count):
        lanes_here = slice(i * lane_count, (i + 1) * lane_count)
        query_rows[mine, lanes_here] = ours[at : at + half]
        query_rows[other, lanes_here] = theirs[at : at + half]
        at += half
    rope[mine, :] = rope_ours[...]
    rope[other, :] = theirs[at : at + half]
    query = query_rows[...]
    diagonal = lax.broadcasted_iota(jnp.int32, (rows, rows), 0) == lax.broadcasted_iota(
        jnp.int32, (rows, rows), 1
    )
    limit = jnp.sum(
        jnp.where(diagonal, lengths[pl.ds(place[4], 1), :], 0), axis=1, keepdims=True
    )
    limit = jnp.concatenate([limit] * heads, axis=0)
    all_rows = heads * rows
    lanes = lax.broadcasted_iota(jnp.int32, (all_rows, chunk), 1)
    rope_width = kv0.shape[0] - width
    q_lat = []
    for h in range(heads):
        w_uq = weights[:, h, :, 0:n_uq, :].reshape(-1, weights.shape[-1])
        w_uk = weights[:, h, :, n_uq : n_uq + n_uk, :].reshape(-1, weights.shape[-1])
        q_nope = dot(query, w_uq).astype(BF16)
        q_lat.append(dot_nt(q_nope, w_uk).astype(BF16))
    q_lat = jnp.concatenate(q_lat, axis=0)
    q_rope = jnp.concatenate(
        [rope[:, h * rope_width : (h + 1) * rope_width] for h in range(heads)], axis=0
    )
    top = jnp.full((all_rows, 1), -1e30, F32)
    for (begin, end), cache in zip(spans, caches):
        s = dot(q_lat, cache[:width, :]) + dot(q_rope, cache[width:, :])
        s = s * temper
        for k in range(begin // chunk, end // chunk):
            piece = s[:, k * chunk - begin : (k + 1) * chunk - begin]
            piece = jnp.where(lanes + starts[k] < limit, piece, -1e30)
            top = jnp.maximum(top, jnp.max(piece, axis=1, keepdims=True))
            scores[:, k * chunk : (k + 1) * chunk] = piece
    total = jnp.zeros((all_rows, 1), F32)
    context = jnp.zeros((all_rows, width), F32)
    for (begin, end), cache in zip(spans, caches):
        p = jnp.exp(scores[:, begin:end] - top)
        total = total + jnp.sum(p, axis=1, keepdims=True)
        context = context + dot_nt(p.astype(BF16), cache[:width, :])
    context = (context / total).astype(BF16)
    values = []
    for h in range(heads):
        w_uv = weights[:, h, :, n_uq + n_uk :, :].reshape(-1, weights.shape[-1])
        values.append(dot(context[h * rows : (h + 1) * rows], w_uv).astype(BF16))
    vdim = values[0].shape[1]
    wide = heads * vdim
    to = lax.broadcasted_iota(jnp.int32, (wide, wide), 1)
    source = lax.broadcasted_iota(jnp.int32, (wide, wide), 0)
    side = to // (wide // 2)
    head = to % (wide // 2) // (vdim // 2)
    item = to % (vdim // 2)
    wanted = head * vdim + item // 4 * 8 + jnp.where(side == 0, zh, 1 - zh) * 4 + item % 4
    move = jnp.where(source == wanted, 1.0, 0.0).astype(BF16)
    moved = dot(jnp.concatenate(values, axis=1), move).astype(BF16)
    keep_out[...] = moved[:, : wide // 2]
    give_out[...] = moved[:, wide // 2 :]


def project_kernel(place, values, received, keep_out, give_out):
    core = place[3]
    lanes = received.shape[2]
    rows = [
        jnp.concatenate([values[i], values[i + 1]], axis=1) for i in range(0, values.shape[0], 2)
    ]
    rows = jnp.concatenate(rows, axis=0)
    depth = rows.shape[1]
    source = lax.broadcasted_iota(jnp.int32, (depth, depth), 0)
    to = lax.broadcasted_iota(jnp.int32, (depth, depth), 1)
    y, z, j = source // 256, source // 128 % 2, source // 64 % 2
    wanted = source // 4 % 16 * 32 + (z * 4 + y * 2 + j) * 4 + source % 4
    order = jnp.where(to == wanted, 1.0, 0.0).astype(BF16)
    rows = dot(rows, order).astype(BF16)
    each = depth // received.shape[0]
    columns = keep_out.shape[-1]
    count = 2 * columns // lanes
    first = received.shape[1] - count * each
    weights = jnp.concatenate(
        [
            received[:, at : at + each].reshape(depth, lanes)
            for at in range(first, received.shape[1], each)
        ],
        axis=1,
    )
    part = dot(rows, weights)
    even, odd = part[:, :columns], part[:, columns:]
    keep_out[...] = jnp.where(core == 0, even, odd).astype(BF16).reshape(keep_out.shape)
    give_out[...] = jnp.where(core == 0, odd, even).astype(BF16).reshape(give_out.shape)


def local(query_latent, query_rope, lengths, kv_cache, w_uq, w_uk, w_uv, w_out):
    yl, zh, zll, core = (lax.axis_index(a) for a in ("yl", "zh", "zll", "c"))
    plane = 16
    cache = kv_cache.T
    kv_width, tokens = cache.shape
    latent_width = w_uk.shape[1] * 32
    rope_width = kv_width - latent_width
    lanes = w_uq.shape[2]
    temper = 1.0 / math.sqrt(lanes + rope_width)
    n_uq, n_uk, n_uv = w_uq.shape[1], w_uk.shape[1], w_uv.shape[1]
    n_all = n_uq + n_uk + n_uv
    own_rows = query_latent.shape[0]
    heads_in = w_uq.shape[0]
    four, heads = heads_in // 2, heads_in // 4

    quarter = tokens // 4
    sequence = lax.axis_index("xh") * 4 + lax.axis_index("xl") * 2 + lax.axis_index("yh")
    place = jnp.stack([zh, yl, core * 2 + zll, core, sequence]).astype(jnp.int32)
    vmem = pl.BlockSpec(memory_space=pltpu.VMEM)
    smem = pl.BlockSpec(memory_space=pltpu.SMEM)
    weights = (w_uq, w_uk, w_uv)
    queries = (query_latent, query_rope)
    latent_chunks = query_latent.shape[1] // lanes
    n_sent = four * n_all + (latent_chunks + 2) * own_rows
    piece = lax.dynamic_slice_in_dim(cache, (core * 2 + zll) * quarter, quarter, 1)
    far_piece = swap(piece, "zh")
    near = swap(lax.dynamic_slice_in_dim(cache, core * (tokens // 2), tokens // 2, 1), "yl")
    near, w_out = lax.optimization_barrier((near, w_out))

    vpart, width = w_out.shape[1:]
    columns = width // 8
    w_rows = heads_in * vpart
    n_spread = heads * n_all + columns // lanes * w_rows
    spread = pl.pallas_call(
        spread_kernel,
        out_shape=jax.ShapeDtypeStruct((plane, n_spread, lanes), BF16),
        in_specs=[smem] + [vmem] * 4,
        out_specs=vmem,
        compiler_params=pltpu.CompilerParams(vmem_limit_bytes=VMEM_LIMIT),
        cost_estimate=pl.CostEstimate(flops=10**6, bytes_accessed=10**6, transcendentals=0),
        name="spread",
    )(place, *weights, w_out.reshape(w_rows, width))
    queries_after, spread = lax.optimization_barrier((query_latent, spread))
    spread = exchange(spread, PLANE)
    packed = pl.pallas_call(
        pack_kernel,
        out_shape=jax.ShapeDtypeStruct((n_sent, lanes), BF16),
        in_specs=[smem] + [vmem] * 5,
        out_specs=vmem,
        compiler_params=pltpu.CompilerParams(vmem_limit_bytes=VMEM_LIMIT),
        cost_estimate=pl.CostEstimate(flops=10**6, bytes_accessed=10**6, transcendentals=0),
        name="pack",
    )(place, *weights, queries_after, query_rope)
    received = swap(packed, "zh")

    n_pack = (2 * latent_chunks + 2) * own_rows
    sent, packed, rope_kept = pl.pallas_call(
        lambda *refs: unpack_kernel(*refs, sizes=(n_all, plane // 2)),
        out_shape=(
            jax.ShapeDtypeStruct((plane // 2, four, n_all, lanes), BF16),
            jax.ShapeDtypeStruct((n_pack, lanes), BF16),
            jax.ShapeDtypeStruct((2 * own_rows, lanes), BF16),
        ),
        in_specs=[smem] + [vmem] * 3,
        out_specs=(vmem,) * 3,
        compiler_params=pltpu.CompilerParams(vmem_limit_bytes=VMEM_LIMIT),
        cost_estimate=pl.CostEstimate(
            flops=UNPACK_FLOPS, bytes_accessed=3 * 10**6, transcendentals=0
        ),
        name="unpack",
    )(place, received, *queries)
    rows = 4 * own_rows
    row_lengths = lengths.reshape(-1, rows)

    far_piece = pl.pallas_call(
        hold_kernel,
        out_shape=jax.ShapeDtypeStruct(far_piece.shape, BF16),
        in_specs=[vmem],
        out_specs=vmem,
        compiler_params=pltpu.CompilerParams(vmem_limit_bytes=VMEM_LIMIT),
        cost_estimate=pl.CostEstimate(flops=HOLD_FLOPS, bytes_accessed=10**6, transcendentals=0),
        name="hold",
    )(far_piece)
    piece_y = swap(far_piece, "yl")
    piece_z = swap(far_piece, "zll")
    piece_yz = lax.ppermute(far_piece, ("yl", "zll"), [(0, 3), (1, 2), (2, 1), (3, 0)])
    packed_y = swap(packed, "yl")
    sent, spread, piece_y, piece_z, piece_yz, row_lengths, packed_y = lax.optimization_barrier(
        (sent, spread, piece_y, piece_z, piece_yz, row_lengths, packed_y)
    )

    weights_far = exchange(sent.reshape(plane * heads, n_all, lanes), PLANE)
    weights_far = weights_far.reshape(plane, heads, n_all, lanes)

    near = lax.all_gather(near, "c", axis=0)
    far = lax.all_gather(jnp.concatenate([far_piece, piece_y], axis=1), "c", axis=0)
    far_z = lax.all_gather(jnp.concatenate([piece_z, piece_yz], axis=1), "c", axis=0)

    keep, give = pl.pallas_call(
        lambda *refs: attend_kernel(
            *refs,
            sizes=(rows, heads, n_uq, n_uk, n_uv, latent_width),
            temper=temper,
        ),
        out_shape=(jax.ShapeDtypeStruct((rows, lanes), BF16),) * 2,
        in_specs=[smem] + [vmem] * 10,
        out_specs=(vmem,) * 2,
        scratch_shapes=[
            pltpu.VMEM((rows, query_latent.shape[1]), BF16),
            pltpu.VMEM((rows, lanes), BF16),
            pltpu.VMEM((heads * rows, 4 * tokens), F32),
            pltpu.VMEM((plane, heads, 2, n_all, lanes), BF16),
        ],
        compiler_params=pltpu.CompilerParams(vmem_limit_bytes=VMEM_LIMIT),
        cost_estimate=pl.CostEstimate(flops=10**9, bytes_accessed=5 * 10**6, transcendentals=0),
        name="attend",
    )(place, packed, packed_y, spread, weights_far, rope_kept, row_lengths, cache, near, far, far_z)

    values = ordered(keep, swap(give, "zh"), zh, 1)
    gathered = exchange(
        jnp.broadcast_to(values[None], (8,) + values.shape).reshape(-1, values.shape[1]), PART
    ).reshape((8,) + values.shape)
    shape = (8, 2, own_rows, columns // 2)
    keep, give = pl.pallas_call(
        project_kernel,
        out_shape=(jax.ShapeDtypeStruct(shape, BF16),) * 2,
        in_specs=[smem] + [vmem] * 2,
        out_specs=(vmem,) * 2,
        compiler_params=pltpu.CompilerParams(vmem_limit_bytes=VMEM_LIMIT),
        cost_estimate=pl.CostEstimate(flops=2 * 10**8, bytes_accessed=2 * 10**6, transcendentals=0),
        name="project",
    )(place, gathered, spread)

    total = (keep.astype(F32) + swap(give, "c").astype(F32)).astype(BF16)
    total = jnp.transpose(exchange(total, PART), (1, 0, 2, 3))
    total = exchange(total.reshape((16,) + total.shape[2:]), COLUMN)
    return jnp.sum(total.astype(F32), axis=0).astype(BF16)


def solution(mesh):
    fine = Mesh(mesh.devices.reshape(SIZES), AXES)
    placed = (
        P(FSDP, None),
        P(FSDP, HEAD, None),
        P(),
        P(FSDP, None),
        P(HEAD, FSDP, None),
        P(HEAD, FSDP, None),
        P(HEAD, FSDP, None),
        P(HEAD, FSDP, None),
    )
    return jax.shard_map(
        local, mesh=fine, in_specs=placed, out_specs=P(FSDP, HEAD), check_vma=False
    )
```
